32 devices in a mesh: img: 2 (over core), rows: 16 (over z, y, x).
Axes of the slice: x: 2, y: 2, z: 4, core: 2. Of those that a mesh axis runs over, the one named last changes fastest.
Arguments:
- tokens: bfloat16 [672, 42, 768], P(('img', 'rows')), may hold values from -6 to 6
- extent: int32 [16, 2], replicated, may hold values from 16 to 32, as said below
- pre_gain: bfloat16 [768], P(('img', 'rows')), may hold values from 0.099609375 to 1.8984375
- pre_bias: bfloat16 [768], P(('img', 'rows')), may hold values from -1.75 to 1.75
- triple_weight: bfloat16 [768, 2304], P(('img', 'rows')), may hold values from -0.21875 to 0.21875
- triple_bias: bfloat16 [1536], P(('img', 'rows')), may hold values from -3 to 3
- height_table: bfloat16 [27, 64], replicated, may hold values from -0.5 to 0.5
- width_table: bfloat16 [27, 64], replicated, may hold values from -0.5 to 0.5
- output_weight: bfloat16 [768, 768], P(('img', 'rows')), may hold values from -0.875 to 0.875
- output_bias: bfloat16 [768], P(('img', 'rows')), may hold values from -1.75 to 1.75
- post_gain: bfloat16 [768], P(('img', 'rows')), may hold values from 0.099609375 to 1.8984375
- post_bias: bfloat16 [768], P(('img', 'rows')), may hold values from -1.75 to 1.75
- expand_weight: bfloat16 [768, 3072], P(('img', 'rows')), may hold values from -0.21875 to 0.21875
- expand_bias: bfloat16 [3072], P(('img', 'rows')), may hold values from -3 to 3
- reduce_weight: bfloat16 [3072, 768], P(('img', 'rows')), may hold values from -0.109375 to 0.109375
- reduce_bias: bfloat16 [768], P(('img', 'rows')), may hold values from -1.75 to 1.75
- cotangent: bfloat16 [672, 42, 768], P(('img', 'rows')), may hold values from -6 to 6
Outputs:
- block_output: bfloat16 [672, 42, 768], P(('img', 'rows'))
- input_grad: bfloat16 [672, 42, 768], P(('img', 'rows'))
- pre_gain_grad: float32 [768], P(('img', 'rows'))
- pre_bias_grad: float32 [768], P(('img', 'rows'))
- triple_weight_grad: float32 [768, 2304], P(('img', 'rows'))
- triple_bias_grad: float32 [1536], P(('img', 'rows'))
- height_table_grad: float32 [27, 64], replicated
- width_table_grad: float32 [27, 64], replicated
- output_weight_grad: float32 [768, 768], P(('img', 'rows'))
- output_bias_grad: float32 [768], P(('img', 'rows'))
- post_gain_grad: float32 [768], P(('img', 'rows'))
- post_bias_grad: float32 [768], P(('img', 'rows'))
- expand_weight_grad: float32 [768, 3072], P(('img', 'rows'))
- expand_bias_grad: float32 [3072], P(('img', 'rows'))
- reduce_weight_grad: float32 [3072, 768], P(('img', 'rows'))
- reduce_bias_grad: float32 [768], P(('img', 'rows'))
The draws below stay inside these ranges and needn't reach their ends.
Inputs may be any that keep to these rules, and one draw needn't show every extreme that they name: extent[i] is image i's real height and width; the larger of the two is 32, and some image has a side of 16.
All inputs are finite; a program needn't handle non-finite values.
Results may differ from the reference program's by a relative error of at most 0.012.
Values may be sent and summed in bfloat16 or wider, within the bound.
No kernel may reach another device: no remote copies, remote signals or barrier semaphores. Data moves between devices by JAX's collectives and lax.ppermute only.
A program may use at most 448 MiB of HBM per device.

```python
import jax
import jax.numpy as jnp
from jax import lax

D = 768
HEADS = 12
HEAD_DIM = 64
FF = 3072
WIN = 14
REAL = 32
GRID = 42
TABLE = 27
IMAGES = 16


def draw_extent(key, part):
    key = jax.random.fold_in(key, 7)
    first, second, third = jax.random.split(key, 3)
    short_side = jax.random.randint(first, (IMAGES,), REAL // 2, REAL + 1).astype(jnp.int32)
    chosen = jax.random.randint(third, (), 0, IMAGES)
    short_side = jnp.where(jnp.arange(IMAGES) == chosen, REAL // 2, short_side).astype(jnp.int32)
    which = jax.random.randint(second, (IMAGES,), 0, 2)
    long_side = jnp.full((IMAGES,), REAL, jnp.int32)
    height = jnp.where(which == 0, long_side, short_side)
    across = jnp.where(which == 0, short_side, long_side)
    return jnp.stack([height, across], axis=1).astype(jnp.int32)


def level_of(rng, dims, cuts, least, top_value):
    level = 1.0
    for dim, blocks in cuts:
        heights = jax.random.uniform(jax.random.fold_in(jax.random.fold_in(rng, 6), dim), (blocks,), jnp.float32, least / len(cuts), top_value / len(cuts))
        level = level * jnp.repeat(jnp.exp(heights), dims[dim] // blocks).reshape((-1,) + (1,) * (len(dims) - 1 - dim))
    return level


def gaussian(stream_key, dims, width, limit, cuts=(), held_as=jnp.bfloat16):
    entries = width * jax.random.normal(stream_key, dims, jnp.float32)
    if cuts:
        entries = entries * level_of(stream_key, dims, cuts, -0.22, 0.18)
    return jnp.clip(entries, -limit, limit).astype(held_as)


def setup_inputs(seed: int = 0) -> dict:
    streams_of = jax.random.split(jax.random.key(seed), 18)
    return {
        "tokens": gaussian(streams_of[0], (IMAGES * GRID, GRID, D), 1.0, 6.0, ((0, 32),)),
        "extent": draw_extent(jax.random.fold_in(streams_of[17], 71), 0),
        "pre_gain": jnp.clip(1.0 + 0.18 * jax.random.normal(streams_of[2], (D,), jnp.float32), 0.099609375, 1.8984375).astype(jnp.bfloat16),
        "pre_bias": gaussian(streams_of[3], (D,), 0.3, 1.75, ((0, 32),)),
        "triple_weight": gaussian(streams_of[4], (D, 3 * D), D ** -0.5, 0.21875, ((0, 32),)),
        "triple_bias": gaussian(streams_of[5], (2 * D,), 0.5, 3.0, ((0, 32),)),
        "height_table": gaussian(streams_of[6], (TABLE, HEAD_DIM), 0.08, 0.5),
        "width_table": gaussian(streams_of[7], (TABLE, HEAD_DIM), 0.08, 0.5),
        "output_weight": gaussian(streams_of[8], (D, D), (D // 16) ** -0.5, 0.875, ((0, 32),)),
        "output_bias": gaussian(streams_of[9], (D,), 0.3, 1.75, ((0, 32),)),
        "post_gain": jnp.clip(1.0 + 0.18 * jax.random.normal(streams_of[10], (D,), jnp.float32), 0.099609375, 1.8984375).astype(jnp.bfloat16),
        "post_bias": gaussian(streams_of[11], (D,), 0.3, 1.75, ((0, 32),)),
        "expand_weight": gaussian(streams_of[12], (D, FF), D ** -0.5, 0.21875, ((0, 32),)),
        "expand_bias": gaussian(streams_of[13], (FF,), 0.5, 3.0, ((0, 32),)),
        "reduce_weight": gaussian(streams_of[14], (FF, D), FF ** -0.5, 0.109375, ((0, 32),)),
        "reduce_bias": gaussian(streams_of[15], (D,), 0.3, 1.75, ((0, 32),)),
        "cotangent": gaussian(streams_of[16], (IMAGES * GRID, GRID, D), 1.0, 6.0, ((0, 32),)),
    }


@jax.custom_vjp
def low(v):
    return lax.optimization_barrier(v.astype(jnp.bfloat16)).astype(jnp.float32)

@jax.custom_vjp
def low_back(v):
    return v

def low_keep(v):
    return (low(v), None)

def low_pass(kept, grad):
    return (grad,)

def back_keep(v):
    return (v, None)

def back_low(kept, grad):
    return (low(grad),)
low.defvjp(low_keep, low_pass)
low_back.defvjp(back_keep, back_low)

def layer_norm(value, gain, bias):
    center = lax.optimization_barrier(jnp.mean(value, axis=-1, keepdims=True))
    centred = value - center
    variance = lax.optimization_barrier(jnp.mean(centred * centred, axis=-1, keepdims=True))
    return centred * lax.rsqrt(variance + 1e-06) * gain + bias

def matmul(left, right):
    return jnp.dot(left, right, precision=lax.Precision.HIGHEST, preferred_element_type=jnp.float32)

def relative(table):
    offsets = jnp.arange(WIN, dtype=jnp.int32)[:, None] - jnp.arange(WIN, dtype=jnp.int32)[None, :] + WIN - 1
    return table[offsets]

def window_attend(queries, keys, values, height_rel, width_rel):
    count = GRID // WIN
    finest = lax.Precision.HIGHEST
    query_six = queries.reshape(count, WIN, count, WIN, HEADS, HEAD_DIM)
    key_six = keys.reshape(count, WIN, count, WIN, HEADS, HEAD_DIM)
    value_six = values.reshape(count, WIN, count, WIN, HEADS, HEAD_DIM)
    scores = jnp.einsum('arbchd,asbkhd->abhrcsk', query_six, key_six, precision=finest) * HEAD_DIM ** (-0.5)
    along_rows = jnp.einsum('arbchd,rsd->abhrcs', query_six, height_rel, precision=finest)
    along_cols = jnp.einsum('arbchd,ckd->abhrck', query_six, width_rel, precision=finest)
    scores = scores + along_rows[..., None] + along_cols[..., None, :]
    shape = scores.shape
    scores = low_back(scores.reshape(shape[:5] + (WIN * WIN,)))
    probs = low(jax.nn.softmax(scores, axis=-1)).reshape(shape)
    mixed = jnp.einsum('abhrcsk,asbkhd->arbchd', probs, value_six, precision=finest)
    return mixed.reshape(GRID, GRID, D)

def reference(tokens, extent, pre_gain, pre_bias, triple_weight, triple_bias, height_table, width_table, output_weight, output_bias, post_gain, post_bias, expand_weight, expand_bias, reduce_weight, reduce_bias, cotangent):
    positions = jnp.arange(GRID, dtype=jnp.int32)
    inside = (positions[None, :, None] < extent[:, 0:1, None]) & (positions[None, None, :] < extent[:, 1:2, None])
    mask = inside.astype(jnp.float32).reshape(IMAGES * GRID, GRID, 1)

    def forward(inputs, pre_gain, pre_bias, triple_weight, triple_bias, height_table, width_table, output_weight, output_bias, post_gain, post_bias, expand_weight, expand_bias, reduce_weight, reduce_bias):
        entry = low(mask * layer_norm(inputs, pre_gain, pre_bias))
        joint = matmul(entry, triple_weight)
        queries = low_back(low(joint[..., :D] + triple_bias[:D]))
        keys = low_back(low(joint[..., D:2 * D]))
        values = low_back(low(joint[..., 2 * D:] + triple_bias[D:]))
        height_rel = relative(height_table)
        width_rel = relative(width_table)

        def attend_one(block):
            return window_attend(block[0], block[1], block[2], height_rel, width_rel)

        def per_image(array):
            return array.reshape(IMAGES, GRID, GRID, D)
        mixed = lax.map(jax.checkpoint(attend_one), (per_image(queries), per_image(keys), per_image(values)))
        mixed = low_back(low(mixed.reshape(IMAGES * GRID, GRID, D)))
        branch = low_back(matmul(mixed, output_weight) + output_bias)
        middle = inputs + mask * branch
        entry_two = low(layer_norm(middle, post_gain, post_bias))
        hidden = low_back(matmul(entry_two, expand_weight) + expand_bias)
        active = low(jax.nn.gelu(hidden, approximate=False))
        result = low_back(matmul(active, reduce_weight) + reduce_bias)
        return mask * (middle + result)
    floats = [item.astype(jnp.float32) for item in (tokens, pre_gain, pre_bias, triple_weight, triple_bias, height_table, width_table, output_weight, output_bias, post_gain, post_bias, expand_weight, expand_bias, reduce_weight, reduce_bias)]
    outputs, pullback = jax.vjp(forward, *floats)
    grads = pullback(cotangent.astype(jnp.float32))
    return (outputs.astype(jnp.bfloat16), grads[0].astype(jnp.bfloat16), grads[1], grads[2], grads[3], grads[4], grads[5], grads[6], grads[7], grads[8], grads[9], grads[10], grads[11], grads[12], grads[13], grads[14])
```

```python
from functools import partial

import jax
import jax.numpy as jnp
import numpy as np
from jax import lax
from jax.experimental import pallas as pl
from jax.experimental.pallas import tpu as pltpu
from jax.sharding import PartitionSpec as P

HEADS = 12
HEAD_DIM = 64
WIN = 14
REAL = 32
KEYS = 208
BF = jnp.bfloat16
F32 = jnp.float32
VMEM_LIMIT = 60 * 2**20

SEGMENTS = []
_offset = 0
for _row, _rows in ((0, WIN), (WIN, REAL - 2 * WIN)):
    for _col, _cols in ((0, WIN), (WIN, WIN), (2 * WIN, REAL - 2 * WIN)):
        _padded = -(-_rows * _cols // 16) * 16
        SEGMENTS.append((_row, _rows, _col, _cols, _padded, _offset))
        _offset += _padded
TOKENS = _offset
BAND = REAL - WIN


def window_constants():
    band_row = np.full((TOKENS,), 0, np.int32)
    column = np.full((TOKENS,), 0, np.int32)
    valid = np.zeros((TOKENS,), np.int32)
    along = np.zeros((TOKENS,), np.int32)
    across = np.zeros((TOKENS,), np.int32)
    onehots = np.zeros((len(SEGMENTS), KEYS, 128), np.float32)
    for number, (row, rows, col, cols, padded, offset) in enumerate(SEGMENTS):
        spots = [(a, b) for a in range(rows) for b in range(cols)]
        for place, (a, b) in enumerate(spots):
            band_row[offset + place] = row + a
            column[offset + place] = col + b
            valid[offset + place] = 1
            along[offset + place] = a
            across[offset + place] = b
        rest = [(s, t) for s in range(WIN) for t in range(WIN) if s >= rows or t >= cols]
        slots = spots + [None] * (padded - len(spots)) + rest
        slots = slots + [None] * (KEYS - len(slots))
        for place, spot in enumerate(slots):
            for head in range(2):
                if spot is None:
                    onehots[number, place, 32 * head + 15] = -1e30
                else:
                    for part in range(2):
                        onehots[number, place, 32 * head + 16 * part + spot[0]] = 1
                        onehots[number, place, 64 + 32 * head + 16 * part + spot[1]] = 1
    return band_row, column, valid, along, across, onehots


BAND_ROW, COLUMN, VALID, ALONG, ACROSS, ONEHOTS = window_constants()


def shift_amounts():
    amounts = np.zeros((TOKENS, 128), np.int32)
    amounts[:, :64] = (WIN - 1 - ALONG)[:, None]
    amounts[:, 64:] = (WIN - 1 - ACROSS)[:, None]
    return amounts


SHIFTS = shift_amounts()


def dot_t(left, right):
    return lax.dot_general(left, right, (((1,), (1,)), ((), ())), preferred_element_type=F32)


def dot_f(left, right):
    return lax.dot_general(left, right, (((0,), (0,)), ((), ())), preferred_element_type=F32)


def dot_n(left, right):
    return lax.dot_general(left, right, (((1,), (0,)), ((), ())), preferred_element_type=F32)


def lanes_of(shape):
    return lax.broadcasted_iota(jnp.int32, shape, len(shape) - 1)


def relative_features(queries, table, shifts):
    terms = dot_n(queries, table)
    for bit in range(4):
        rolled = pltpu.roll(terms, 128 - (1 << bit), 1)
        terms = jnp.where((shifts & (1 << bit)) != 0, rolled, terms)
    high = terms.astype(BF).astype(F32)
    low = pltpu.roll(terms - high, 16, 1)
    lane = lanes_of(terms.shape) & 31
    mixed = jnp.where(lane < WIN, high, jnp.where((lane >= 16) & (lane < 16 + WIN), low, 0.0))
    return jnp.where(lane == 15, 1.0, mixed).astype(BF)


def stacked_queries(queries, features, start, count):
    lane = lanes_of((count, 128))
    first = lane < 64
    even = (lane & 32) == 0
    part = queries[start : start + count] * jnp.asarray(0.125, BF)
    extra = features[start : start + count]
    zero = jnp.zeros_like(part)
    top = jnp.concatenate([jnp.where(first, part, zero), jnp.where(even, extra, zero)], 1)
    low = jnp.concatenate([jnp.where(first, zero, part), jnp.where(even, zero, extra)], 1)
    return jnp.concatenate([top, low], 0)


def window_keys(array, start, count, fill):
    if count == KEYS:
        return array[start : start + count]
    rest = jnp.broadcast_to(fill, (KEYS - count, 128)).astype(BF)
    return jnp.concatenate([array[start : start + count], rest], 0)


def tiles_of(total):
    return [(begin, min(128, total - begin)) for begin in range(0, total, 128)]


def attend_kernel(q_ref, k_ref, v_ref, fill_ref, table_ref, shifts_ref, onehots_ref, mixed_ref, lse_ref):
    queries = q_ref[...]
    features = relative_features(queries, table_ref[...], shifts_ref[...])
    keys, values = k_ref[...], v_ref[...]
    fill = fill_ref[...]
    base = 0
    for number, (_, _, _, _, count, start) in enumerate(SEGMENTS):
        left = stacked_queries(queries, features, start, count)
        right = jnp.concatenate(
            [window_keys(keys, start, count, jnp.zeros((1, 128), BF)), onehots_ref[number]], 1
        )
        held = window_keys(values, start, count, fill)
        outs = []
        for begin, size in tiles_of(2 * count):
            scores = dot_t(right, left[begin : begin + size])
            top = jnp.max(scores, axis=0, keepdims=True)
            weights = jnp.exp(scores - top)
            total = jnp.sum(weights, axis=0, keepdims=True)
            lse_ref[0, 0:1, base + begin : base + begin + size] = top + jnp.log(total)
            out = dot_f(held, weights.astype(BF)) * (1.0 / total)
            outs.append(out.T)
        both = jnp.concatenate(outs, 0)
        lane = lanes_of((count, 128))
        mixed = jnp.where(lane < 64, both[:count], both[count:])
        mixed_ref[start : start + count, :] = mixed.astype(BF)
        base += -(-2 * count // 128) * 128


LSE = sum(-(-2 * segment[4] // 128) * 128 for segment in SEGMENTS)


def attend_back_kernel(
    q_ref, k_ref, v_ref, g_ref, lse_ref, fill_ref, table_ref, shifts_ref, onehots_ref,
    dq_ref, dk_ref, dv_ref, dtable_ref, dbias_ref, probs_ref, dscores_ref, slots_ref,
):
    queries = q_ref[...]
    shifts = shifts_ref[...]
    table = table_ref[...]
    features = relative_features(queries, table, shifts)
    keys, values, grads = k_ref[...], v_ref[...], g_ref[...]
    fill = fill_ref[...]
    base = 0
    bias_sum = jnp.zeros((1, 128), F32)
    for number, (_, _, _, _, count, start) in enumerate(SEGMENTS):
        left = stacked_queries(queries, features, start, count)
        right = jnp.concatenate(
            [window_keys(keys, start, count, jnp.zeros((1, 128), BF)), onehots_ref[number]], 1
        )
        held = window_keys(values, start, count, fill)
        lane = lanes_of((count, 128))
        first = lane < 64
        part = grads[start : start + count]
        zero = jnp.zeros_like(part)
        pulls = jnp.concatenate([jnp.where(first, part, zero), jnp.where(first, zero, part)], 0)
        for begin, size in tiles_of(2 * count):
            scores = dot_t(right, left[begin : begin + size])
            probs = jnp.exp(scores - lse_ref[0, 0:1, base + begin : base + begin + size])
            dprobs = dot_t(held, pulls[begin : begin + size])
            product = probs * dprobs
            delta = jnp.sum(product, axis=0, keepdims=True)
            probs_ref[:, begin : begin + size] = probs.astype(BF)
            dscores_ref[:, begin : begin + size] = (product - probs * delta).astype(BF)
        dscores = dscores_ref[:, : 2 * count]
        dvalues = dot_n(probs_ref[:, : 2 * count], pulls)
        dkeys = dot_n(dscores, left[:, :128])
        dv_ref[start : start + count, :] = dvalues[:count].astype(BF)
        dk_ref[start : start + count, :] = dkeys[:count].astype(BF)
        bias_sum = bias_sum + jnp.sum(dvalues, axis=0, keepdims=True)
        both = dot_f(dscores, right)
        dq = jnp.where(first, both[:count, :128], both[count:, :128]) * 0.125
        even = (lane & 32) == 0
        extra = jnp.where(even, both[:count, 128:], both[count:, 128:])
        slots = jnp.where((lane & 31) < WIN, extra, 0.0)
        amounts = shifts[start : start + count]
        for bit in range(4):
            rolled = pltpu.roll(slots, 1 << bit, 1)
            slots = jnp.where((amounts & (1 << bit)) != 0, rolled, slots)
        high = slots.astype(BF)
        low = (slots - high.astype(F32)).astype(BF)
        slots_ref[start : start + count, :128] = high
        slots_ref[start : start + count, 128:] = low
        dq = dq + dot_t(jnp.concatenate([high, low], 1), jnp.concatenate([table, table], 1))
        dq_ref[start : start + count, :] = dq.astype(BF)
        base += -(-2 * count // 128) * 128
    found = dot_f(slots_ref[...], queries)
    dtable_ref[0] = found[:128] + found[128:]
    dbias_ref[...] = bias_sum


def whole(shape):
    return pl.BlockSpec(shape, lambda step: (0,) * len(shape))


def column(offset, rows=TOKENS):
    return pl.BlockSpec((rows, 128), lambda step: (0, offset + step))


def reversed_table(height_table, width_table):
    slots = height_table.shape[0]
    pad = ((0, 0), (0, 32 - slots))
    height = jnp.pad(height_table[::-1].T, pad)
    width = jnp.pad(width_table[::-1].T, pad)
    none = jnp.zeros_like(height)
    top = jnp.concatenate([height, none, width, none], 1)
    low = jnp.concatenate([none, height, none, width], 1)
    return jnp.concatenate([top, low], 0)


def attend(joint, fill, table):
    pairs = HEADS // 2
    return pl.pallas_call(
        attend_kernel,
        grid=(pairs,),
        in_specs=[
            column(0), column(pairs), column(2 * pairs), column(0, 1),
            whole((128, 128)), whole((TOKENS, 128)), whole((len(SEGMENTS), KEYS, 128)),
        ],
        out_specs=[column(0), pl.BlockSpec((1, 8, LSE), lambda step: (step, 0, 0))],
        out_shape=[
            jax.ShapeDtypeStruct((TOKENS, pairs * 128), BF),
            jax.ShapeDtypeStruct((pairs, 8, LSE), F32),
        ],
        compiler_params=pltpu.CompilerParams(vmem_limit_bytes=VMEM_LIMIT),
        name="attend",
    )(joint, joint, joint, fill, table, jnp.asarray(SHIFTS), jnp.asarray(ONEHOTS, BF))


def attend_back(joint, grad_mixed, lse, fill, table):
    pairs = HEADS // 2
    wide = jax.ShapeDtypeStruct((TOKENS, pairs * 128), BF)
    return pl.pallas_call(
        attend_back_kernel,
        grid=(pairs,),
        in_specs=[
            column(0), column(pairs), column(2 * pairs), column(0),
            pl.BlockSpec((1, 8, LSE), lambda step: (step, 0, 0)), column(0, 1),
            whole((128, 128)), whole((TOKENS, 128)), whole((len(SEGMENTS), KEYS, 128)),
        ],
        out_specs=[
            column(0), column(0), column(0),
            pl.BlockSpec((1, 128, 128), lambda step: (step, 0, 0)), column(0, 1),
        ],
        out_shape=[
            wide, wide, wide,
            jax.ShapeDtypeStruct((pairs, 128, 128), F32),
            jax.ShapeDtypeStruct((1, pairs * 128), F32),
        ],
        scratch_shapes=[
            pltpu.VMEM((KEYS, 512), BF), pltpu.VMEM((KEYS, 512), BF), pltpu.VMEM((TOKENS, 256), BF),
        ],
        compiler_params=pltpu.CompilerParams(vmem_limit_bytes=VMEM_LIMIT),
        name="attend_back",
    )(joint, joint, joint, grad_mixed, lse, fill, table, jnp.asarray(SHIFTS), jnp.asarray(ONEHOTS, BF))


def table_grads(found, slots):
    total = jnp.sum(found, axis=0)
    height = total[0:32, :64] + total[32:64, 64:]
    width = total[64:96, :64] + total[96:128, 64:]
    return height[:slots][::-1], width[:slots][::-1]


def pack_kernel(parity_ref, own_ref, far_ref, out_ref, stage_ref):
    parity = parity_ref[0]
    moved = far_ref.shape[0]
    stage_ref[...] = jnp.zeros_like(stage_ref)
    for row in range(BAND):
        if row < moved:
            line = jnp.where(parity == 0, own_ref[row, :REAL], far_ref[row]).astype(F32)
        else:
            line = own_ref[row - moved * parity, :REAL].astype(F32)
        for first, rows, col, cols, _, offset in SEGMENTS:
            if first <= row < first + rows:
                place = offset + (row - first) * cols
                stage_ref[place : place + cols, :] = line[col : col + cols]
    out_ref[...] = stage_ref[...].astype(out_ref.dtype)


def pack(parity, own, far):
    width = own.shape[2]
    return pl.pallas_call(
        pack_kernel,
        in_specs=[
            pl.BlockSpec(memory_space=pltpu.SMEM),
            pl.BlockSpec(memory_space=pltpu.VMEM),
            pl.BlockSpec(memory_space=pltpu.VMEM),
        ],
        out_specs=pl.BlockSpec(memory_space=pltpu.VMEM),
        out_shape=jax.ShapeDtypeStruct((TOKENS, width), BF),
        scratch_shapes=[pltpu.VMEM((TOKENS, width), F32)],
        compiler_params=pltpu.CompilerParams(vmem_limit_bytes=VMEM_LIMIT),
        name="pack",
    )(parity.reshape(1), own, far)


def unpack_kernel(parity_ref, win_ref, far_ref, out_ref, wide_ref, stage_ref):
    parity = parity_ref[0]
    moved = far_ref.shape[0]
    wide_ref[...] = win_ref[...].astype(F32)
    for row in range(BAND):
        for first, rows, col, cols, _, offset in SEGMENTS:
            if first <= row < first + rows:
                place = offset + (row - first) * cols
                stage_ref[row, col : col + cols, :] = wide_ref[place : place + cols, :]
    out_ref[...] = jnp.zeros_like(out_ref)
    for row in range(out_ref.shape[0]):
        near = stage_ref[row] if row < WIN else far_ref[row - WIN].astype(F32)
        other = stage_ref[row + moved] if row + moved < BAND else jnp.zeros_like(near)
        out_ref[row, :REAL, :] = jnp.where(parity == 0, near, other).astype(out_ref.dtype)


def unpack(parity, win, far, shape):
    width = win.shape[1]
    return pl.pallas_call(
        unpack_kernel,
        in_specs=[
            pl.BlockSpec(memory_space=pltpu.SMEM),
            pl.BlockSpec(memory_space=pltpu.VMEM),
            pl.BlockSpec(memory_space=pltpu.VMEM),
        ],
        out_specs=pl.BlockSpec(memory_space=pltpu.VMEM),
        out_shape=jax.ShapeDtypeStruct(shape, BF),
        scratch_shapes=[pltpu.VMEM((TOKENS, width), F32), pltpu.VMEM((BAND, REAL, width), F32)],
        compiler_params=pltpu.CompilerParams(vmem_limit_bytes=VMEM_LIMIT),
        name="unpack",
    )(parity.reshape(1), win, far)


def send_rows_kernel(win_ref, out_ref, wide_ref, stage_ref):
    wide_ref[...] = win_ref[...].astype(F32)
    for row in range(out_ref.shape[0]):
        for first, rows, col, cols, _, offset in SEGMENTS:
            if first <= row < first + rows:
                place = offset + (row - first) * cols
                stage_ref[row, col : col + cols, :] = wide_ref[place : place + cols, :]
    out_ref[...] = stage_ref[...].astype(out_ref.dtype)


def send_rows(win, moved):
    width = win.shape[1]
    return pl.pallas_call(
        send_rows_kernel,
        in_specs=[pl.BlockSpec(memory_space=pltpu.VMEM)],
        out_specs=pl.BlockSpec(memory_space=pltpu.VMEM),
        out_shape=jax.ShapeDtypeStruct((moved, REAL, width), BF),
        scratch_shapes=[pltpu.VMEM((TOKENS, width), F32), pltpu.VMEM((moved, REAL, width), F32)],
        compiler_params=pltpu.CompilerParams(vmem_limit_bytes=VMEM_LIMIT),
        name="send_rows",
    )(win)


def rows_place():
    me = lax.axis_index("rows")
    return me % 2, me // 2 % 2, me // 4


def swap_rows(block, bit):
    count = lax.axis_size("rows")
    return lax.ppermute(block, "rows", [(place, place ^ (1 << bit)) for place in range(count)])


def swap_img(block):
    return lax.ppermute(block, "img", [(0, 1), (1, 0)])


def shift_depth(block, step):
    count = lax.axis_size("rows")
    return lax.ppermute(
        block, "rows", [(place, (place + 4 * step) % count) for place in range(count)]
    )


def in_order(bit, mine, other, axis):
    return jnp.where(
        bit == 0, jnp.stack([mine, other], axis), jnp.stack([other, mine], axis)
    )


def gather_depth(block):
    depth = lax.axis_size("rows") // 4
    place = rows_place()[2]
    parts = [block] + [shift_depth(block, step) for step in range(1, depth)]
    turned = [parts[-step % depth] for step in range(depth)]
    twice = jnp.stack(turned + turned)
    return lax.dynamic_slice_in_dim(twice, depth - place, depth, 0)


def halves(block):
    cut = block.shape[-1] // 256 * 128
    return block[..., :cut], block[..., cut:]


def gather_blocks(block):
    x, y, _ = rows_place()
    first, second = halves(gather_depth(block))
    first = in_order(x, first, swap_rows(first, 0), 1)
    second = in_order(y, second, swap_rows(second, 1), 1)
    first = in_order(y, first, swap_rows(first, 1), 1)
    second = in_order(x, second, swap_rows(second, 0), 2)
    full = jnp.concatenate([first, second], -1).reshape(-1, block.shape[-1])
    other = swap_img(full)
    both = in_order(lax.axis_index("img"), full, other, 0)
    return both.reshape(-1, block.shape[-1])


def pick(array, place, axis):
    return lax.dynamic_index_in_dim(array, place, axis, keepdims=False)


def fold(block, place, axis, send):
    given = pick(block, 1 - place, axis).astype(BF)
    kept = pick(block, place, axis).astype(F32)
    return (kept + send(given).astype(F32)).astype(BF)


def scatter_blocks(total):
    x, y, z = rows_place()
    count = lax.axis_size("rows")
    depth = count // 4
    columns = total.shape[-1]
    block = fold(total.reshape(2, -1, columns), lax.axis_index("img"), 0, swap_img)
    block = block.reshape(depth, 2, 2, -1, columns)
    first, second = halves(block)
    first = fold(first, x, 2, lambda part: swap_rows(part, 0))
    second = fold(second, y, 1, lambda part: swap_rows(part, 1))
    first = fold(first, y, 1, lambda part: swap_rows(part, 1))
    second = fold(second, x, 1, lambda part: swap_rows(part, 0))
    block = jnp.concatenate([first, second], -1)
    result = pick(block, z, 0).astype(F32)
    for step in range(1, depth):
        given = pick(block, (z + step) % depth, 0)
        result = result + shift_depth(given, step).astype(F32)
    return result


def sum_all(value):
    value = value + swap_img(value)
    value = value + swap_rows(value, 0)
    value = value + swap_rows(value, 1)
    return jnp.sum(gather_depth(value), axis=0)


def layer_norm(value, gain, bias):
    center = jnp.mean(value, axis=-1, keepdims=True)
    centred = value - center
    variance = jnp.mean(centred * centred, axis=-1, keepdims=True)
    return centred * lax.rsqrt(variance + 1e-06) * gain + bias


def to_odd(block):
    count = lax.axis_size("rows")
    return lax.ppermute(block, "rows", [(place, place + 1) for place in range(0, count, 2)])


def to_even(block):
    count = lax.axis_size("rows")
    return lax.ppermute(block, "rows", [(place + 1, place) for place in range(0, count, 2)])


def local(
    tokens,
    extent,
    pre_gain,
    pre_bias,
    triple_weight,
    triple_bias,
    height_table,
    width_table,
    output_weight,
    output_bias,
    post_gain,
    post_bias,
    expand_weight,
    expand_bias,
    reduce_weight,
    reduce_bias,
    cotangent,
):
    rows_dev, _, width = tokens.shape
    moved = rows_dev - WIN
    block = pre_gain.shape[0]
    parity = lax.axis_index("rows") % 2
    image = lax.axis_index("img") * (lax.axis_size("rows") // 2) + lax.axis_index("rows") // 2
    sides = lax.dynamic_slice(extent, (image, 0), (1, 2))

    vectors = [
        vector.reshape(block, -1)
        for vector in (
            pre_gain, pre_bias, triple_bias, output_bias, post_gain, post_bias, expand_bias, reduce_bias,
        )
    ]
    counts = [vector.shape[1] for vector in vectors]
    vectors = jnp.pad(jnp.concatenate(vectors, 1), ((0, 0), (0, 128 - sum(counts))))
    first_all = gather_blocks(jnp.concatenate([triple_weight, vectors], 1))
    triple_all, vectors_all = first_all[:, : 3 * width], first_all[:, 3 * width :]
    second_all = gather_blocks(jnp.concatenate([output_weight, expand_weight], 1))
    output_all, expand_all = second_all[:, :width], second_all[:, width:]
    reduce_all = gather_blocks(reduce_weight)

    spread = []
    begin = 0
    for count in counts:
        spread.append(vectors_all[:, begin : begin + count].reshape(-1).astype(F32))
        begin += count
    (
        pre_gain_all, pre_bias_all, triple_bias_all, output_bias_all, post_gain_all, post_bias_all,
        expand_bias_all, reduce_bias_all,
    ) = spread

    far_tokens = to_odd(tokens[WIN:, :REAL])
    far_pulls = to_odd(cotangent[WIN:, :REAL])
    flat = pack(parity, tokens, far_tokens).astype(F32)
    pulls = pack(parity, cotangent, far_pulls).astype(F32)
    band_row, column_of = jnp.asarray(BAND_ROW), jnp.asarray(COLUMN)
    real_row = jnp.where(parity == 0, band_row, band_row + WIN)
    inside = (real_row < sides[0, 0]) & (column_of < sides[0, 1]) & (jnp.asarray(VALID) == 1)
    inside = inside & ((parity == 1) | (band_row < WIN))
    mask = inside.astype(F32)[:, None]

    normed, pre_back = jax.vjp(layer_norm, flat, pre_gain_all, pre_bias_all)
    entry = (mask * normed).astype(BF)
    added = jnp.concatenate([triple_bias_all[:width], jnp.zeros((width,), F32), triple_bias_all[width:]])
    joint = (dot_n(entry, triple_all) + added).astype(BF)
    table = reversed_table(height_table, width_table)
    fill = triple_bias_all[None, width:].astype(BF)
    mixed, lse = attend(joint, fill, table)
    branch = dot_n(mixed, output_all) + output_bias_all
    middle = flat + mask * branch
    normed_two, post_back = jax.vjp(layer_norm, middle, post_gain_all, post_bias_all)
    entry_two = normed_two.astype(BF)
    hidden = dot_n(entry_two, expand_all) + expand_bias_all
    active, gelu_back = jax.vjp(partial(jax.nn.gelu, approximate=False), hidden)
    active_round = active.astype(BF)
    result = dot_n(active_round, reduce_all) + reduce_bias_all
    out_win = (mask * (middle + result)).astype(BF)
    block_output = unpack(parity, out_win, to_even(send_rows(out_win, moved)), tokens.shape)

    incoming = mask * pulls
    incoming_round = incoming.astype(BF)
    reduce_weight_grad = dot_f(active_round, incoming_round)
    reduce_bias_grad = jnp.sum(incoming, axis=0)
    (grad_hidden,) = gelu_back(dot_t(incoming_round, reduce_all))
    grad_hidden = grad_hidden.astype(BF)
    expand_weight_grad = dot_f(entry_two, grad_hidden)
    expand_bias_grad = jnp.sum(grad_hidden, axis=0, dtype=F32)
    grad_middle, post_gain_grad, post_bias_grad = post_back(dot_t(grad_hidden, expand_all))
    grad_middle = incoming + grad_middle
    reduce_shard = scatter_blocks(reduce_weight_grad)
    grad_branch = (mask * grad_middle).astype(BF)
    output_weight_grad = dot_f(mixed, grad_branch)
    output_bias_grad = jnp.sum(grad_branch, axis=0, dtype=F32)
    second_shard = scatter_blocks(jnp.concatenate([output_weight_grad, expand_weight_grad], 1))
    grad_mixed = dot_t(grad_branch, output_all).astype(BF)
    grad_queries, grad_keys, grad_values, found, values_bias_grad = attend_back(
        joint, grad_mixed, lse, fill, table
    )
    tables = sum_all(jnp.stack(table_grads(found, height_table.shape[0])))
    grad_joint = jnp.concatenate([grad_queries, grad_keys, grad_values], axis=1)
    triple_weight_grad = dot_f(entry, grad_joint)
    triple_bias_grad = jnp.concatenate(
        [jnp.sum(grad_queries, axis=0, dtype=F32), values_bias_grad[0]]
    )
    grad_entry = dot_t(grad_joint, triple_all)
    grad_flat, pre_gain_grad, pre_bias_grad = pre_back(mask * grad_entry)
    grad_win = (grad_middle + grad_flat).astype(BF)
    input_grad = unpack(parity, grad_win, to_even(send_rows(grad_win, moved)), tokens.shape)
    vector_grads = jnp.concatenate(
        [
            vector.reshape(width, -1)
            for vector in (
                pre_gain_grad, pre_bias_grad, triple_bias_grad, output_bias_grad, post_gain_grad,
                post_bias_grad, expand_bias_grad, reduce_bias_grad,
            )
        ],
        1,
    )
    vector_grads = jnp.pad(vector_grads, ((0, 0), (0, 128 - sum(counts))))
    first_shard = scatter_blocks(jnp.concatenate([triple_weight_grad, vector_grads], 1))
    shards = []
    begin = 3 * width
    for count in counts:
        shards.append(first_shard[:, begin : begin + count].reshape(-1))
        begin += count
    return (
        block_output,
        input_grad,
        shards[0],
        shards[1],
        first_shard[:, : 3 * width],
        shards[2],
        tables[0],
        tables[1],
        second_shard[:, :width],
        shards[3],
        shards[4],
        shards[5],
        second_shard[:, width:],
        shards[6],
        reduce_shard,
        shards[7],
    )


def solution(mesh):
    split = P(("img", "rows"))
    flat = P(("img", "rows"), None)
    grids = P(("img", "rows"), None, None)
    in_specs = (
        grids, P(), split, split, flat, split, P(), P(), flat, split, split, split, flat, split,
        flat, split, grids,
    )
    out_specs = (
        grids, grids, split, split, flat, split, P(), P(), flat, split, split, split, flat, split,
        flat, split,
    )
    return jax.shard_map(local, mesh=mesh, in_specs=in_specs, out_specs=out_specs, check_vma=False)
```

```python
from functools import partial

import jax
import jax.numpy as jnp
import numpy as np
from jax import lax
from jax.experimental import pallas as pl
from jax.experimental.pallas import tpu as pltpu
from jax.sharding import PartitionSpec as P

HEADS = 12
HEAD_DIM = 64
WIN = 14
REAL = 32
KEYS = 208
BF = jnp.bfloat16
F32 = jnp.float32
VMEM_LIMIT = 60 * 2**20


def cost(microseconds):
    return pl.CostEstimate(flops=int(microseconds * 1000000000), bytes_accessed=1, transcendentals=0)


ANY = pl.BlockSpec(memory_space=pl.ANY)

SEGMENTS = []
_offset = 0
for _row, _rows in ((0, WIN), (WIN, REAL - 2 * WIN)):
    for _col, _cols in ((0, WIN), (WIN, WIN), (2 * WIN, REAL - 2 * WIN)):
        _padded = -(-_rows * _cols // 16) * 16
        SEGMENTS.append((_row, _rows, _col, _cols, _padded, _offset))
        _offset += _padded
TOKENS = _offset
BAND = REAL - WIN


def ordered(kernel, count, earlier):
    def body(*refs):
        kernel(*refs[:count], *refs[count + len(earlier) :])

    return body


def window_constants():
    band_row = np.full((TOKENS,), 0, np.int32)
    column = np.full((TOKENS,), 0, np.int32)
    valid = np.zeros((TOKENS,), np.int32)
    along = np.zeros((TOKENS,), np.int32)
    across = np.zeros((TOKENS,), np.int32)
    onehots = np.zeros((len(SEGMENTS), KEYS, 128), np.float32)
    for number, (row, rows, col, cols, padded, offset) in enumerate(SEGMENTS):
        spots = [(a, b) for a in range(rows) for b in range(cols)]
        for place, (a, b) in enumerate(spots):
            band_row[offset + place] = row + a
            column[offset + place] = col + b
            valid[offset + place] = 1
            along[offset + place] = a
            across[offset + place] = b
        rest = [(s, t) for s in range(WIN) for t in range(WIN) if s >= rows or t >= cols]
        slots = spots + [None] * (padded - len(spots)) + rest
        slots = slots + [None] * (KEYS - len(slots))
        for place, spot in enumerate(slots):
            for head in range(2):
                if spot is None:
                    onehots[number, place, 32 * head + 15] = -1e30
                else:
                    for part in range(2):
                        onehots[number, place, 32 * head + 16 * part + spot[0]] = 1
                        onehots[number, place, 64 + 32 * head + 16 * part + spot[1]] = 1
    return band_row, column, valid, along, across, onehots


BAND_ROW, COLUMN, VALID, ALONG, ACROSS, ONEHOTS = window_constants()


def shift_amounts():
    amounts = np.zeros((TOKENS, 128), np.int32)
    amounts[:, :64] = (WIN - 1 - ALONG)[:, None]
    amounts[:, 64:] = (WIN - 1 - ACROSS)[:, None]
    return amounts


SHIFTS = shift_amounts()


def dot_t(left, right):
    return lax.dot_general(left, right, (((1,), (1,)), ((), ())), preferred_element_type=F32)


def dot_f(left, right):
    return lax.dot_general(left, right, (((0,), (0,)), ((), ())), preferred_element_type=F32)


def dot_n(left, right):
    return lax.dot_general(left, right, (((1,), (0,)), ((), ())), preferred_element_type=F32)


def lanes_of(shape):
    return lax.broadcasted_iota(jnp.int32, shape, len(shape) - 1)


def relative_features(queries, table, shifts):
    terms = dot_n(queries, table)
    for bit in range(4):
        rolled = pltpu.roll(terms, 128 - (1 << bit), 1)
        terms = jnp.where((shifts & (1 << bit)) != 0, rolled, terms)
    high = terms.astype(BF).astype(F32)
    low = pltpu.roll(terms - high, 16, 1)
    lane = lanes_of(terms.shape) & 31
    mixed = jnp.where(lane < WIN, high, jnp.where((lane >= 16) & (lane < 16 + WIN), low, 0.0))
    return jnp.where(lane == 15, 1.0, mixed).astype(BF)


def stacked_queries(queries, features, start, count):
    lane = lanes_of((count, 128))
    first = lane < 64
    even = (lane & 32) == 0
    part = queries[start : start + count] * jnp.asarray(0.125, BF)
    extra = features[start : start + count]
    zero = jnp.zeros_like(part)
    top = jnp.concatenate([jnp.where(first, part, zero), jnp.where(even, extra, zero)], 1)
    low = jnp.concatenate([jnp.where(first, zero, part), jnp.where(even, zero, extra)], 1)
    return jnp.concatenate([top, low], 0)


def window_keys(array, start, count, fill):
    if count == KEYS:
        return array[start : start + count]
    rest = jnp.broadcast_to(fill, (KEYS - count, 128)).astype(BF)
    return jnp.concatenate([array[start : start + count], rest], 0)


def tiles_of(total):
    return [(begin, min(128, total - begin)) for begin in range(0, total, 128)]


def lane_spots():
    spots = []
    base = 0
    for _, _, _, _, count, _ in SEGMENTS:
        spots.append((base, 2 * count))
        base += -(-2 * count // 128) * 128
    return spots


def window_sides(number, queries, features, keys, onehots_ref):
    _, _, _, _, count, start = SEGMENTS[number]
    left = stacked_queries(queries, features, start, count)
    none = jnp.zeros((1, 128), BF)
    right = jnp.concatenate([window_keys(keys, start, count, none), onehots_ref[number]], 1)
    return left, right


def attend_kernel(
    q_ref, k_ref, v_ref, fill_ref, table_ref, shifts_ref, onehots_ref,
    mixed_ref, lse_ref, features_ref, scores_ref, weights_ref,
):
    queries = q_ref[...]
    features = relative_features(queries, table_ref[...], shifts_ref[...])
    features_ref[...] = features
    keys, values = k_ref[...], v_ref[...]
    fill = fill_ref[...]
    spots = lane_spots()
    for number, (base, size) in enumerate(spots):
        left, right = window_sides(number, queries, features, keys, onehots_ref)
        scores_ref[:, base : base + size] = dot_t(right, left)
    totals = []
    for base, size in spots:
        scores = scores_ref[:, base : base + size]
        top = jnp.max(scores, axis=0, keepdims=True)
        weights = jnp.exp(scores - top)
        total = jnp.sum(weights, axis=0, keepdims=True)
        lse_ref[0, 0:1, base : base + size] = top + jnp.log(total)
        weights_ref[:, base : base + size] = weights.astype(BF)
        totals.append(1.0 / total)
    for (_, _, _, _, count, start), (base, size), scale in zip(SEGMENTS, spots, totals):
        held = window_keys(values, start, count, fill).T
        both = (dot_n(held, weights_ref[:, base : base + size]) * scale).T
        lane = lanes_of((count, 128))
        mixed = jnp.where(lane < 64, both[:count], both[count:])
        mixed_ref[start : start + count, :] = mixed.astype(BF)


LSE = sum(-(-2 * segment[4] // 128) * 128 for segment in SEGMENTS)


def attend_back_kernel(
    q_ref, k_ref, v_ref, g_ref, lse_ref, features_ref, fill_ref, table_ref, shifts_ref, onehots_ref,
    dqkv_ref, dtable_ref, dbias_ref,
    scores_ref, dprobs_ref, probs_ref, dscores_ref, back_ref, slots_ref,
):
    queries = q_ref[...]
    shifts = shifts_ref[...]
    table = table_ref[...]
    features = features_ref[...]
    keys, values, grads = k_ref[...], v_ref[...], g_ref[...]
    fill = fill_ref[...]
    spots = lane_spots()

    def stacked_pulls(start, count):
        first = lanes_of((count, 128)) < 64
        part = grads[start : start + count]
        zero = jnp.zeros_like(part)
        return jnp.concatenate([jnp.where(first, part, zero), jnp.where(first, zero, part)], 0)

    for number, (base, size) in enumerate(spots):
        _, _, _, _, count, start = SEGMENTS[number]
        left, right = window_sides(number, queries, features, keys, onehots_ref)
        scores_ref[:, base : base + size] = dot_t(right, left)
        held = window_keys(values, start, count, fill)
        dprobs_ref[:, base : base + size] = dot_t(held, stacked_pulls(start, count))
    for base, size in spots:
        lanes = slice(base, base + size)
        probs = jnp.exp(scores_ref[:, lanes] - lse_ref[0, 0:1, lanes])
        product = probs * dprobs_ref[:, lanes]
        delta = jnp.sum(product, axis=0, keepdims=True)
        probs_ref[:, lanes] = probs.astype(BF)
        dscores_ref[:, lanes] = (product - probs * delta).astype(BF)
    bias_sum = jnp.zeros((1, 128), F32)
    for number, (base, size) in enumerate(spots):
        _, _, _, _, count, start = SEGMENTS[number]
        left, right = window_sides(number, queries, features, keys, onehots_ref)
        dscores = dscores_ref[:, base : base + size]
        dvalues = dot_n(probs_ref[:, base : base + size], stacked_pulls(start, count))
        dkeys = dot_n(dscores, left[:, :128])
        dqkv_ref[start : start + count, 256:] = dvalues[:count].astype(BF)
        dqkv_ref[start : start + count, 128:256] = dkeys[:count].astype(BF)
        bias_sum = bias_sum + jnp.sum(dvalues, axis=0, keepdims=True)
        both = dot_f(dscores, right)
        lane = lanes_of((count, 128))
        back_ref[start : start + count, :128] = jnp.where(lane < 64, both[:count, :128], both[count:, :128])
        back_ref[start : start + count, 128:] = jnp.where(
            (lane & 32) == 0, both[:count, 128:], both[count:, 128:]
        )
    lane = lanes_of((TOKENS, 128)) & 31
    slots = jnp.where(lane < WIN, back_ref[:, 128:], 0.0)
    for bit in range(4):
        rolled = pltpu.roll(slots, 1 << bit, 1)
        slots = jnp.where((shifts & (1 << bit)) != 0, rolled, slots)
    high = slots.astype(BF)
    low = (slots - high.astype(F32)).astype(BF)
    slots_ref[:, :128] = high
    slots_ref[:, 128:] = low
    dq = back_ref[:, :128] * 0.125 + dot_t(slots_ref[...], jnp.concatenate([table, table], 1))
    dq = dq.astype(BF)
    dqkv_ref[:, :128] = dq
    found = dot_f(slots_ref[...], queries)
    dtable_ref[0] = found[:128] + found[128:]
    query_sum = jnp.sum(dq.astype(F32), axis=0, keepdims=True)
    dbias_ref[...] = jnp.concatenate([query_sum, bias_sum], 0)


def whole(shape):
    return pl.BlockSpec(shape, lambda step: (0,) * len(shape))


def column(offset, rows=TOKENS):
    return pl.BlockSpec((rows, 128), lambda step: (0, offset + step))


def reversed_table(height_table, width_table):
    slots = height_table.shape[0]
    pad = ((0, 0), (0, 32 - slots))
    height = jnp.pad(height_table[::-1].T, pad)
    width = jnp.pad(width_table[::-1].T, pad)
    none = jnp.zeros_like(height)
    top = jnp.concatenate([height, none, width, none], 1)
    low = jnp.concatenate([none, height, none, width], 1)
    return jnp.concatenate([top, low], 0)


def attend(joint, fill, table, begin, count, given, *earlier):
    pairs = HEADS // 2
    shapes = [
        jax.ShapeDtypeStruct((TOKENS, pairs * 128), BF),
        jax.ShapeDtypeStruct((pairs, 8, LSE), F32),
        jax.ShapeDtypeStruct((TOKENS, pairs * 128), BF),
    ]
    return pl.pallas_call(
        ordered(attend_kernel, 7, tuple(given) + earlier),
        grid=(count,),
        in_specs=[
            column(begin), column(pairs + begin), column(2 * pairs + begin), column(begin, 1),
            whole((128, 128)), whole((TOKENS, 128)), whole((len(SEGMENTS), KEYS, 128)),
        ] + [ANY] * (len(given) + len(earlier)),
        out_specs=[
            column(begin), pl.BlockSpec((1, 8, LSE), lambda step: (begin + step, 0, 0)), column(begin),
        ],
        out_shape=shapes,
        input_output_aliases={7 + place: place for place in range(len(given))},
        scratch_shapes=[pltpu.VMEM((KEYS, LSE), F32), pltpu.VMEM((KEYS, LSE), BF)],
        compiler_params=pltpu.CompilerParams(vmem_limit_bytes=VMEM_LIMIT),
        cost_estimate=cost(5.5),
        name="attend",
    )(joint, joint, joint, fill, table, jnp.asarray(SHIFTS), jnp.asarray(ONEHOTS, BF), *given, *earlier)


def attend_back(joint, grad_mixed, lse, features, fill, table, begin, count, *earlier):
    pairs = HEADS // 2

    def kernel(*refs):
        attend_back_kernel(*refs[:10], *refs[10 + len(earlier) :])

    return pl.pallas_call(
        kernel,
        grid=(count,),
        in_specs=[
            column(begin), column(pairs + begin), column(2 * pairs + begin), column(begin),
            pl.BlockSpec((1, 8, LSE), lambda step: (begin + step, 0, 0)), column(begin), column(begin, 1),
            whole((128, 128)), whole((TOKENS, 128)), whole((len(SEGMENTS), KEYS, 128)),
        ] + [pl.BlockSpec(memory_space=pl.ANY)] * len(earlier),
        out_specs=[
            pl.BlockSpec((TOKENS, 384), lambda step: (0, step)),
            pl.BlockSpec((1, 128, 128), lambda step: (step, 0, 0)), column(0, 2),
        ],
        out_shape=[
            jax.ShapeDtypeStruct((TOKENS, count * 384), BF),
            jax.ShapeDtypeStruct((count, 128, 128), F32),
            jax.ShapeDtypeStruct((2, count * 128), F32),
        ],
        scratch_shapes=[
            pltpu.VMEM((KEYS, LSE), F32), pltpu.VMEM((KEYS, LSE), F32),
            pltpu.VMEM((KEYS, LSE), BF), pltpu.VMEM((KEYS, LSE), BF),
            pltpu.VMEM((TOKENS, 256), F32), pltpu.VMEM((TOKENS, 256), BF),
        ],
        compiler_params=pltpu.CompilerParams(vmem_limit_bytes=VMEM_LIMIT),
        cost_estimate=cost(14.5),
        name="attend_back",
    )(
        joint, joint, joint, grad_mixed, lse, features, fill, table, jnp.asarray(SHIFTS), jnp.asarray(ONEHOTS, BF),
        *earlier,
    )


def tie(value, *earlier):
    def kernel(*refs):
        pass

    return pl.pallas_call(
        kernel,
        in_specs=[pl.BlockSpec(memory_space=pl.ANY)] * (1 + len(earlier)),
        out_specs=pl.BlockSpec(memory_space=pl.ANY),
        out_shape=jax.ShapeDtypeStruct(value.shape, value.dtype),
        input_output_aliases={0: 0},
        name="tie",
    )(value, *earlier)


def table_grads(found, slots):
    total = jnp.sum(found, axis=0)
    height = total[0:32, :64] + total[32:64, 64:]
    width = total[64:96, :64] + total[96:128, 64:]
    return height[:slots][::-1], width[:slots][::-1]


def pack_kernel(masked, moved, parity_ref, own_ref, far_ref, mask_ref, out_ref, stage_ref):
    parity = parity_ref[0]
    stage_ref[...] = jnp.zeros_like(stage_ref)
    for row in range(BAND):
        if row < moved:
            line = jnp.where(parity == 0, own_ref[row, :REAL], far_ref[row]).astype(F32)
        else:
            line = own_ref[row - moved * parity, :REAL].astype(F32)
        for first, rows, col, cols, _, offset in SEGMENTS:
            if first <= row < first + rows:
                place = offset + (row - first) * cols
                stage_ref[place : place + cols, :] = line[col : col + cols]
    if masked:
        out_ref[...] = (stage_ref[...] * mask_ref[...]).astype(out_ref.dtype)
    else:
        out_ref[...] = stage_ref[...].astype(out_ref.dtype)


def pack(parity, own, far, mask, masked, *earlier):
    width = own.shape[2]
    vmem = pl.BlockSpec(memory_space=pltpu.VMEM)
    return pl.pallas_call(
        ordered(partial(pack_kernel, masked, far.shape[0]), 4, earlier),
        in_specs=[pl.BlockSpec(memory_space=pltpu.SMEM), vmem, vmem, vmem] + [ANY] * len(earlier),
        out_specs=vmem,
        out_shape=jax.ShapeDtypeStruct((TOKENS, width), BF),
        scratch_shapes=[pltpu.VMEM((TOKENS, width), F32)],
        compiler_params=pltpu.CompilerParams(vmem_limit_bytes=VMEM_LIMIT),
        cost_estimate=cost(3),
        name="pack",
    )(parity.reshape(1), own, far, mask, *earlier)


def unpack_kernel(moved, parity_ref, win_ref, far_ref, out_ref, wide_ref, stage_ref):
    parity = parity_ref[0]
    wide_ref[...] = win_ref[...].astype(F32)
    for row in range(BAND):
        for first, rows, col, cols, _, offset in SEGMENTS:
            if first <= row < first + rows:
                place = offset + (row - first) * cols
                stage_ref[row, col : col + cols, :] = wide_ref[place : place + cols, :]
    out_ref[...] = jnp.zeros_like(out_ref)
    for row in range(out_ref.shape[0]):
        near = stage_ref[row] if row < WIN else far_ref[row - WIN].astype(F32)
        other = stage_ref[row + moved] if row + moved < BAND else jnp.zeros_like(near)
        out_ref[row, :REAL, :] = jnp.where(parity == 0, near, other).astype(out_ref.dtype)


def unpack(parity, win, far, shape, *earlier):
    width = win.shape[1]
    return pl.pallas_call(
        ordered(partial(unpack_kernel, far.shape[0]), 3, earlier),
        in_specs=[
            pl.BlockSpec(memory_space=pltpu.SMEM),
            pl.BlockSpec(memory_space=pltpu.VMEM),
            pl.BlockSpec(memory_space=pltpu.VMEM),
        ] + [ANY] * len(earlier),
        out_specs=pl.BlockSpec(memory_space=pltpu.VMEM),
        out_shape=jax.ShapeDtypeStruct(shape, BF),
        scratch_shapes=[pltpu.VMEM((TOKENS, width), F32), pltpu.VMEM((BAND, REAL, width), F32)],
        compiler_params=pltpu.CompilerParams(vmem_limit_bytes=VMEM_LIMIT),
        cost_estimate=cost(3),
        name="unpack",
    )(parity.reshape(1), win, far, *earlier)


def send_rows_kernel(win_ref, out_ref, wide_ref, stage_ref):
    wide_ref[...] = win_ref[...].astype(F32)
    for row in range(out_ref.shape[0]):
        for first, rows, col, cols, _, offset in SEGMENTS:
            if first <= row < first + rows:
                place = offset + (row - first) * cols
                stage_ref[row, col : col + cols, :] = wide_ref[place : place + cols, :]
    out_ref[...] = stage_ref[...].astype(out_ref.dtype)


def send_rows(win, moved, *earlier):
    width = win.shape[1]
    vmem = pl.BlockSpec(memory_space=pltpu.VMEM)
    return pl.pallas_call(
        ordered(send_rows_kernel, 1, earlier),
        in_specs=[vmem] + [ANY] * len(earlier),
        out_specs=vmem,
        out_shape=jax.ShapeDtypeStruct((moved, REAL, width), BF),
        scratch_shapes=[pltpu.VMEM((TOKENS, width), F32), pltpu.VMEM((moved, REAL, width), F32)],
        compiler_params=pltpu.CompilerParams(vmem_limit_bytes=VMEM_LIMIT),
        cost_estimate=cost(2.6),
        name="send_rows",
    )(win, *earlier)


def gelu_parts(hidden):
    bell = jnp.exp(hidden * hidden * -0.5)
    size = jnp.abs(hidden)
    turn = pl.reciprocal(1.0 + 0.3275911 * 0.7071067811865476 * size)
    poly = turn * (
        0.5 * 0.254829592
        + turn
        * (
            0.5 * -0.284496736
            + turn * (0.5 * 1.421413741 + turn * (0.5 * -1.453152027 + turn * (0.5 * 1.061405429)))
        )
    )
    tail = poly * bell
    below = jnp.where(hidden >= 0, 1.0 - tail, tail)
    return hidden * below, below + hidden * (0.3989422804014327 * bell)


def mlp_kernel(
    img_ref, entry_ref, pull_ref, expand_ref, expand_far_ref, bias_ref, reduce_ref, reduce_far_ref,
    result_ref, back_ref, dreduce_ref, dexpand_far_ref, dexpand_ref, dbias_ref, turned_ref,
):
    step = pl.program_id(0)
    first_half = step < pl.num_programs(0) // 2
    low = img_ref[0] == 0

    @pl.when(step == 0)
    def _():
        result_ref[...] = jnp.zeros_like(result_ref)
        back_ref[...] = jnp.zeros_like(back_ref)
        turned_ref[...] = entry_ref[...].T

    near, far = expand_ref[...], expand_far_ref[...]
    expand = jnp.concatenate([jnp.where(low, near, far), jnp.where(low, far, near)], 0)
    reduce = jnp.where(first_half, reduce_far_ref[...], reduce_ref[...])
    pull = pull_ref[...]
    hidden = dot_n(entry_ref[...], expand) + bias_ref[...]
    active, slope = gelu_parts(hidden)
    active = active.astype(BF)
    grad = (dot_t(pull, reduce) * slope).astype(BF)
    result_ref[...] += dot_n(active, reduce)
    back_ref[...] += dot_t(grad, expand)
    dexpand = dot_n(turned_ref[...], grad)
    half = dexpand_ref.shape[0]
    dexpand_far_ref[...] = jnp.where(low, dexpand[half:], dexpand[:half]).astype(BF)
    dexpand_ref[...] = jnp.where(low, dexpand[:half], dexpand[half:]).astype(BF)
    dbias_ref[...] = jnp.sum(grad.astype(F32), axis=0, keepdims=True)
    dreduce_ref[...] = dot_f(active, pull).astype(BF)


def mlp(img, entry_two, incoming, expand, expand_far, bias, reduce, reduce_far, *earlier, chunk=768):
    width = entry_two.shape[1]
    hidden = bias.shape[1]
    tokens = entry_two.shape[0]
    steps = hidden // chunk
    half = steps // 2

    def place(step, img):
        return (step + (1 - img[0]) * half) % steps

    def fixed(rows, columns):
        return pl.BlockSpec((rows, columns), lambda step, img: (0, 0))

    def across(rows):
        return pl.BlockSpec((rows, chunk), lambda step, img: (0, place(step, img)))

    return pl.pallas_call(
        ordered(mlp_kernel, 8, earlier),
        grid_spec=pltpu.PrefetchScalarGridSpec(
            num_scalar_prefetch=1,
            grid=(steps,),
            in_specs=[
                fixed(tokens, width), fixed(tokens, width), across(width // 2), across(width // 2), across(1),
                pl.BlockSpec((chunk, width), lambda step, img: (jnp.maximum(step - half, 0), 0)),
                pl.BlockSpec((chunk, width), lambda step, img: (jnp.minimum(step, half - 1), 0)),
            ] + [ANY] * len(earlier),
            out_specs=[
                fixed(tokens, width), fixed(tokens, width),
                pl.BlockSpec((chunk, width), lambda step, img: (place(step, img), 0)),
                across(width // 2), across(width // 2), across(1),
            ],
            scratch_shapes=[pltpu.VMEM((width, tokens), BF)],
        ),
        out_shape=[
            jax.ShapeDtypeStruct((tokens, width), F32),
            jax.ShapeDtypeStruct((tokens, width), F32),
            jax.ShapeDtypeStruct((hidden, width), BF),
            jax.ShapeDtypeStruct((width // 2, hidden), BF),
            jax.ShapeDtypeStruct((width // 2, hidden), BF),
            jax.ShapeDtypeStruct((1, hidden), F32),
        ],
        compiler_params=pltpu.CompilerParams(vmem_limit_bytes=VMEM_LIMIT),
        cost_estimate=cost(29),
        name="mlp",
    )(img.reshape(1), entry_two, incoming, expand, expand_far, bias, reduce, reduce_far, *earlier)


def project_kernel(img_ref, x_ref, mask_ref, rows_ref, near_ref, far_ref, bias_ref, entry_ref, joint_ref):
    @pl.when(pl.program_id(0) == 0)
    def _():
        value = x_ref[...].astype(F32)
        centred = value - jnp.mean(value, axis=1, keepdims=True)
        variance = jnp.mean(centred * centred, axis=1, keepdims=True)
        normed = centred * lax.rsqrt(variance + 1e-06) * rows_ref[0:1] + rows_ref[1:2]
        entry_ref[...] = (mask_ref[...] * normed).astype(BF)

    low = img_ref[0] == 0
    near, far = near_ref[...], far_ref[...]
    weight = jnp.concatenate([jnp.where(low, near, far), jnp.where(low, far, near)], 0)
    joint_ref[...] = (dot_n(entry_ref[...], weight) + bias_ref[...]).astype(BF)


def project(img, x, mask, rows, near, far, bias, *earlier, chunk=768):
    tokens, width = x.shape
    total = bias.shape[1]

    def across(rows):
        return pl.BlockSpec((rows, chunk), lambda step: (0, step))

    return pl.pallas_call(
        ordered(project_kernel, 7, earlier),
        grid=(total // chunk,),
        in_specs=[
            pl.BlockSpec(memory_space=pltpu.SMEM), whole((tokens, width)), whole((tokens, 1)),
            whole((8, width)), across(width // 2), across(width // 2), across(1),
        ] + [ANY] * len(earlier),
        out_specs=[whole((tokens, width)), across(tokens)],
        out_shape=[
            jax.ShapeDtypeStruct((tokens, width), BF), jax.ShapeDtypeStruct((tokens, total), BF),
        ],
        compiler_params=pltpu.CompilerParams(vmem_limit_bytes=VMEM_LIMIT),
        cost_estimate=cost(7),
        name="project",
    )(img.reshape(1), x, mask, rows, near, far, bias, *earlier)


def project_back_kernel(
    img_ref, x_ref, mask_ref, rows_ref, middle_ref, pull_ref,
    nq_ref, nk_ref, nv_ref, fq_ref, fk_ref, fv_ref, *refs,
):
    grad_ref, sums_ref, near_ref, far_ref = refs[-4:]
    step = pl.program_id(0)

    @pl.when(step == 0)
    def _():
        near_ref[...] = jnp.zeros_like(near_ref)
        far_ref[...] = jnp.zeros_like(far_ref)

    pull = pull_ref[...]
    near_ref[...] += dot_t(pull, jnp.concatenate([nq_ref[...], nk_ref[...], nv_ref[...]], 1))
    far_ref[...] += dot_t(pull, jnp.concatenate([fq_ref[...], fk_ref[...], fv_ref[...]], 1))

    @pl.when(step == pl.num_programs(0) - 1)
    def _():
        low = img_ref[0] == 0
        near, far = near_ref[...], far_ref[...]
        grad = jnp.concatenate([jnp.where(low, near, far), jnp.where(low, far, near)], 1) * mask_ref[...]
        value = x_ref[...].astype(F32)
        centred = value - jnp.mean(value, axis=1, keepdims=True)
        variance = jnp.mean(centred * centred, axis=1, keepdims=True)
        rstd = lax.rsqrt(variance + 1e-06)
        xhat = centred * rstd
        product = grad * xhat
        sums_ref[0:1] = jnp.sum(product, axis=0, keepdims=True)
        sums_ref[1:2] = jnp.sum(grad, axis=0, keepdims=True)
        pull = grad * rows_ref[0:1]
        back = pull - jnp.mean(pull, axis=1, keepdims=True)
        back = back - xhat * jnp.mean(pull * xhat, axis=1, keepdims=True)
        grad_ref[...] = (middle_ref[...] + rstd * back).astype(BF)


def project_back(img, x, mask, rows, grad_middle, grad_joint, near, far, *earlier):
    tokens, width = x.shape
    pairs = HEADS // 2
    half = width // 2

    def weight(part):
        return pl.BlockSpec((half, 128), lambda step: (0, part * pairs + step))

    return pl.pallas_call(
        project_back_kernel,
        grid=(pairs,),
        in_specs=[
            pl.BlockSpec(memory_space=pltpu.SMEM), whole((tokens, width)), whole((tokens, 1)),
            whole((8, width)), whole((tokens, width)),
            pl.BlockSpec((tokens, 384), lambda step: (0, step)),
            weight(0), weight(1), weight(2), weight(0), weight(1), weight(2),
        ] + [pl.BlockSpec(memory_space=pl.ANY)] * len(earlier),
        out_specs=[whole((tokens, width)), whole((2, width))],
        out_shape=[jax.ShapeDtypeStruct((tokens, width), BF), jax.ShapeDtypeStruct((2, width), F32)],
        scratch_shapes=[pltpu.VMEM((tokens, half), F32), pltpu.VMEM((tokens, half), F32)],
        compiler_params=pltpu.CompilerParams(vmem_limit_bytes=VMEM_LIMIT),
        cost_estimate=cost(11),
        name="project_back",
    )(
        img.reshape(1), x, mask, rows, grad_middle, grad_joint, near, near, near, far, far, far, *earlier
    )


def mix_kernel(img_ref, mixed_ref, near_ref, far_ref, rows_ref, x_ref, mask_ref, middle_ref, entry_ref):
    low = img_ref[0] == 0
    near, far = near_ref[...], far_ref[...]
    weight = jnp.concatenate([jnp.where(low, near, far), jnp.where(low, far, near)], 0)
    branch = dot_n(mixed_ref[...], weight) + rows_ref[2:3]
    middle = x_ref[...].astype(F32) + mask_ref[...] * branch
    middle_ref[...] = middle
    centred = middle - jnp.mean(middle, axis=1, keepdims=True)
    variance = jnp.mean(centred * centred, axis=1, keepdims=True)
    normed = centred * lax.rsqrt(variance + 1e-06) * rows_ref[4:5] + rows_ref[5:6]
    entry_ref[...] = normed.astype(BF)


def mix(img, mixed, near, far, rows, x, mask, *earlier):
    vmem = pl.BlockSpec(memory_space=pltpu.VMEM)
    return pl.pallas_call(
        ordered(mix_kernel, 7, earlier),
        in_specs=[pl.BlockSpec(memory_space=pltpu.SMEM)] + [vmem] * 6 + [ANY] * len(earlier),
        out_specs=[vmem] * 2,
        out_shape=[jax.ShapeDtypeStruct(x.shape, F32), jax.ShapeDtypeStruct(x.shape, BF)],
        compiler_params=pltpu.CompilerParams(vmem_limit_bytes=VMEM_LIMIT),
        cost_estimate=cost(4.6),
        name="mix",
    )(img.reshape(1), mixed, near, far, rows, x, mask, *earlier)


def mix_back_kernel(
    img_ref, back_ref, result_ref, middle_ref, incoming_ref, mask_ref, rows_ref, near_ref, far_ref, mixed_ref,
    grad_middle_ref, grad_mixed_ref, give_ref, keep_ref, out_ref, sums_ref,
):
    low = img_ref[0] == 0
    mask = mask_ref[...]
    middle = middle_ref[...]
    incoming = incoming_ref[...].astype(F32)
    out_ref[...] = (mask * (middle + (result_ref[...] + rows_ref[3:4]))).astype(BF)
    back = back_ref[...]
    centred = middle - jnp.mean(middle, axis=1, keepdims=True)
    variance = jnp.mean(centred * centred, axis=1, keepdims=True)
    rstd = lax.rsqrt(variance + 1e-06)
    xhat = centred * rstd
    sums_ref[1:2] = jnp.sum(back * xhat, axis=0, keepdims=True)
    sums_ref[2:3] = jnp.sum(back, axis=0, keepdims=True)
    sums_ref[3:4] = jnp.sum(incoming, axis=0, keepdims=True)
    pull = back * rows_ref[4:5]
    inner = pull - jnp.mean(pull, axis=1, keepdims=True)
    inner = inner - xhat * jnp.mean(pull * xhat, axis=1, keepdims=True)
    grad_middle = incoming + rstd * inner
    grad_middle_ref[...] = grad_middle
    branch = (mask * grad_middle).astype(BF)
    sums_ref[0:1] = jnp.sum(branch.astype(F32), axis=0, keepdims=True)
    near, far = near_ref[...], far_ref[...]
    weight = jnp.concatenate([jnp.where(low, near, far), jnp.where(low, far, near)], 0)
    grad_mixed_ref[...] = dot_t(branch, weight).astype(BF)
    half = keep_ref.shape[0]
    total = dot_f(mixed_ref[...], branch)
    give_ref[...] = jnp.where(low, total[half:], total[:half]).astype(BF)
    keep_ref[...] = jnp.where(low, total[:half], total[half:]).astype(BF)


def mix_back(img, back, result, middle, incoming, mask, rows, near, far, mixed, *earlier):
    tokens, width = middle.shape
    vmem = pl.BlockSpec(memory_space=pltpu.VMEM)
    return pl.pallas_call(
        ordered(mix_back_kernel, 10, earlier),
        in_specs=[pl.BlockSpec(memory_space=pltpu.SMEM)] + [vmem] * 9 + [ANY] * len(earlier),
        out_specs=[vmem] * 6,
        out_shape=[
            jax.ShapeDtypeStruct((tokens, width), F32), jax.ShapeDtypeStruct((tokens, width), BF),
            jax.ShapeDtypeStruct((width // 2, width), BF), jax.ShapeDtypeStruct((width // 2, width), BF),
            jax.ShapeDtypeStruct((tokens, width), BF), jax.ShapeDtypeStruct((4, width), F32),
        ],
        compiler_params=pltpu.CompilerParams(vmem_limit_bytes=VMEM_LIMIT),
        cost_estimate=cost(8.8),
        name="mix_back",
    )(img.reshape(1), back, result, middle, incoming, mask, rows, near, far, mixed, *earlier)


def entry_grads_kernel(img_ref, entry_ref, grad_ref, give_ref, keep_ref, turned_ref):
    @pl.when(pl.program_id(0) == 0)
    def _():
        turned_ref[...] = entry_ref[...].T

    low = img_ref[0] == 0
    half = keep_ref.shape[0]
    total = dot_n(turned_ref[...], grad_ref[...])
    give_ref[...] = jnp.where(low, total[half:], total[:half]).astype(BF)
    keep_ref[...] = jnp.where(low, total[:half], total[half:]).astype(BF)


def entry_grads(img, entry, grad, *earlier, chunk=768):
    tokens, width = entry.shape
    total = grad.shape[1]

    def across(rows):
        return pl.BlockSpec((rows, chunk), lambda step: (0, step))

    return pl.pallas_call(
        ordered(entry_grads_kernel, 3, earlier),
        grid=(total // chunk,),
        in_specs=[pl.BlockSpec(memory_space=pltpu.SMEM), whole((tokens, width)), across(tokens)]
        + [ANY] * len(earlier),
        out_specs=[across(width // 2), across(width // 2)],
        out_shape=[
            jax.ShapeDtypeStruct((width // 2, total), BF), jax.ShapeDtypeStruct((width // 2, total), BF),
        ],
        scratch_shapes=[pltpu.VMEM((width, tokens), BF)],
        compiler_params=pltpu.CompilerParams(vmem_limit_bytes=VMEM_LIMIT),
        cost_estimate=cost(7.2),
        name="entry_grads",
    )(img.reshape(1), entry, grad, *earlier)


def sums_kernel(norm_ref, joint_ref, mix_ref, expand_ref, tables_ref, out_ref):
    width = norm_ref.shape[1]
    out_ref[0:2] = norm_ref[...]
    out_ref[2:4] = joint_ref[...]
    out_ref[4:8] = mix_ref[...]
    for part in range(4):
        out_ref[8 + part : 9 + part] = expand_ref[:, part * width : (part + 1) * width]
    out_ref[12:] = jnp.zeros((out_ref.shape[0] - 12, width), F32)
    total = tables_ref[0]
    for pair in range(1, tables_ref.shape[0]):
        total = total + tables_ref[pair]
    height = total[0:32, :64] + total[32:64, 64:]
    across = total[64:96, :64] + total[96:128, 64:]
    both = jnp.concatenate([height, across], 1)
    for part in range(4):
        out_ref[16:24, part * 128 : (part + 1) * 128] = both[part * 8 : (part + 1) * 8]


def sums(norm, joint, mixed, expand, tables, *earlier):
    vmem = pl.BlockSpec(memory_space=pltpu.VMEM)
    return pl.pallas_call(
        ordered(sums_kernel, 5, earlier),
        in_specs=[vmem] * 5 + [ANY] * len(earlier),
        out_specs=vmem,
        out_shape=jax.ShapeDtypeStruct((24, norm.shape[1]), F32),
        cost_estimate=cost(1.9),
        name="sums",
    )(norm, joint, mixed, expand, tables, *earlier)


def add_kernel(one_ref, two_ref, out_ref):
    out_ref[...] = one_ref[...] + two_ref[...]


def add(one, two, *earlier):
    vmem = pl.BlockSpec(memory_space=pltpu.VMEM)
    return pl.pallas_call(
        ordered(add_kernel, 2, earlier),
        in_specs=[vmem] * 2 + [ANY] * len(earlier),
        out_specs=vmem,
        out_shape=jax.ShapeDtypeStruct(one.shape, F32),
        cost_estimate=cost(1),
        name="add",
    )(one, two, *earlier)


def share_kernel(block, slots, place_ref, *refs):
    parts, outs = refs[:-10], refs[-10:]
    depth = len(parts)
    total = None
    for level in range(depth):
        found = parts[0][...]
        for step in range(1, depth):
            found = jnp.where(lax.rem(place_ref[1] - level + depth, depth) == step, parts[step][...], found)
        total = found if total is None else total + found
    width = total.shape[1]
    begin = place_ref[0] * block

    def own(array, size, first):
        return pltpu.roll(array, lax.rem(2 * array.shape[1] - first, array.shape[1]), 1)[:, :size]

    for number, row in enumerate((0, 1, 4, 5, 6, 7)):
        outs[number][...] = own(total[row : row + 1], block, begin)
    joint = jnp.concatenate([total[2:3], total[3:4]], 1)
    outs[6][...] = own(joint, 2 * block, 2 * begin)
    hidden = jnp.concatenate([total[8 + part : 9 + part] for part in range(4)], 1)
    outs[7][...] = own(hidden, 4 * block, 4 * begin)
    for slot in range(slots):
        place = slots - 1 - slot
        line = total[16 + place % 8 : 17 + place % 8, place // 8 * 128 : place // 8 * 128 + 128]
        outs[8][slot : slot + 1] = line[:, :64]
        outs[9][slot : slot + 1] = line[:, 64:]


def share(number, parts, block, slots, *earlier):
    vmem = pl.BlockSpec(memory_space=pltpu.VMEM)
    shapes = [(1, block)] * 6 + [(1, 2 * block), (1, 4 * block)] + [(slots, HEAD_DIM)] * 2
    return pl.pallas_call(
        ordered(partial(share_kernel, block, slots), 1 + len(parts), earlier),
        in_specs=[pl.BlockSpec(memory_space=pltpu.SMEM)] + [vmem] * len(parts) + [ANY] * len(earlier),
        out_specs=[vmem] * len(shapes),
        out_shape=[jax.ShapeDtypeStruct(shape, F32) for shape in shapes],
        cost_estimate=cost(1.8),
        name="share",
    )(number, *parts, *earlier)


def place_kernel(depth, *refs):
    parts, triple_ref = refs[:depth], refs[depth]
    pairs = HEADS // 2
    for pair in range(pairs):
        for part in range(3):
            begin, spot = (pair * 3 + part) * 128, (part * pairs + pair) * 128
            value = parts[0][:, begin : begin + 128]
            for other in parts[1:]:
                value = value + other[:, begin : begin + 128].astype(F32)
            triple_ref[:, spot : spot + 128] = value


def place(parts, *earlier):
    vmem = pl.BlockSpec(memory_space=pltpu.VMEM)
    return pl.pallas_call(
        ordered(partial(place_kernel, len(parts)), len(parts), earlier),
        in_specs=[vmem] * len(parts) + [ANY] * len(earlier),
        out_specs=vmem,
        out_shape=jax.ShapeDtypeStruct(parts[0].shape, F32),
        compiler_params=pltpu.CompilerParams(vmem_limit_bytes=VMEM_LIMIT),
        name="place",
    )(*parts, *earlier)


def settle_kernel(cut, *refs):
    parts, (left_ref, right_ref) = refs[:-2], refs[-2:]
    for out_ref, lanes in ((left_ref, slice(0, cut)), (right_ref, slice(cut, None))):
        value = parts[0][:, lanes]
        for part in parts[1:]:
            value = value + part[:, lanes].astype(F32)
        out_ref[...] = value


def settle(parts, cut, *earlier):
    vmem = pl.BlockSpec(memory_space=pltpu.VMEM)
    rows, columns = parts[0].shape
    return pl.pallas_call(
        ordered(partial(settle_kernel, cut), len(parts), earlier),
        in_specs=[vmem] * len(parts) + [ANY] * len(earlier),
        out_specs=[vmem] * 2,
        out_shape=[
            jax.ShapeDtypeStruct((rows, cut), F32), jax.ShapeDtypeStruct((rows, columns - cut), F32),
        ],
        cost_estimate=cost(2),
        name="settle",
    )(*parts, *earlier)


def rows_place():
    me = lax.axis_index("rows")
    return me % 2, me // 2 % 2, me // 4


def swap_rows(block, bit):
    count = lax.axis_size("rows")
    return lax.ppermute(block, "rows", [(place, place ^ (1 << bit)) for place in range(count)])


def swap_img(block):
    return lax.ppermute(block, "img", [(0, 1), (1, 0)])


def shift_depth(block, step):
    count = lax.axis_size("rows")
    return lax.ppermute(
        block, "rows", [(place, (place + 4 * step) % count) for place in range(count)]
    )


def in_order(bit, mine, other, axis):
    return jnp.where(
        bit == 0, jnp.stack([mine, other], axis), jnp.stack([other, mine], axis)
    )


def gather_depth(block):
    depth = lax.axis_size("rows") // 4
    place = rows_place()[2]
    parts = [block] + [shift_depth(block, step) for step in range(1, depth)]
    turned = [parts[-step % depth] for step in range(depth)]
    twice = jnp.stack(turned + turned)
    return lax.dynamic_slice_in_dim(twice, depth - place, depth, 0)


def halves(block):
    cut = block.shape[-1] // 256 * 128
    return block[..., :cut], block[..., cut:]


def join_one_kernel(depth, count, bits_ref, *refs):
    place = bits_ref[2]
    ins, outs = refs[: depth * count], refs[len(refs) - 2 * count :]
    for number in range(count):
        first, second = outs[2 * number : 2 * number + 2]
        cut = first.shape[-1]
        for step in range(depth):
            spot = lax.rem(place - step + depth, depth)
            part = ins[number * depth + step][...]
            first[spot] = part[:, :cut]
            second[spot] = part[:, cut:]


def join_two_kernel(count, bits_ref, *refs):
    x, y = bits_ref[0], bits_ref[1]
    ins, outs = refs[: 4 * count], refs[len(refs) - 2 * count :]
    for number in range(count):
        first, first_far, second, second_far = ins[4 * number : 4 * number + 4]
        joined, joined_two = outs[2 * number : 2 * number + 2]
        for level in range(first.shape[0]):
            joined[level, x] = first[level]
            joined[level, 1 - x] = first_far[level]
            joined_two[level, y] = second[level]
            joined_two[level, 1 - y] = second_far[level]


def join_three_kernel(splits, bits_ref, first, first_far, second, second_far, *refs):
    x, y = bits_ref[0], bits_ref[1]
    outs = refs[len(refs) - len(splits) :]
    cut = first.shape[-1]
    begin = 0
    for size, joined in zip(splits, outs):
        rows = slice(begin, begin + size)
        for level in range(first.shape[0]):
            for side in range(2):
                joined[level, y, side, :, :cut] = first[level, side, rows]
                joined[level, 1 - y, side, :, :cut] = first_far[level, side, rows]
                joined[level, side, x, :, cut:] = second[level, side, rows]
                joined[level, side, 1 - x, :, cut:] = second_far[level, side, rows]
        begin += size


def carry_kernel(weight_ref, *refs):
    out_ref = refs[-1]
    columns = weight_ref.shape[1]
    out_ref[:, :columns] = weight_ref[...]
    pre_gain, pre_bias, triple_bias, output_bias, post_gain, post_bias, expand_bias, reduce_bias = [
        ref[...].astype(F32) for ref in refs[:8]
    ]
    lines = []
    for parts in ((pre_gain, pre_bias, triple_bias, output_bias), (expand_bias, reduce_bias), (post_gain, post_bias)):
        size = sum(part.shape[1] for part in parts)
        lines.append(jnp.concatenate(parts + (jnp.zeros((1, 128 - size), F32),), 1))
    rest = out_ref.shape[0] - len(lines)
    if rest:
        lines.append(jnp.zeros((rest, 128), F32))
    out_ref[:, columns:] = jnp.concatenate(lines, 0).astype(out_ref.dtype)


def carry(weight, vectors, *earlier):
    vmem = pl.BlockSpec(memory_space=pltpu.VMEM)
    return pl.pallas_call(
        ordered(carry_kernel, 1 + len(vectors), earlier),
        in_specs=[vmem] * (1 + len(vectors)) + [ANY] * len(earlier),
        out_specs=vmem,
        out_shape=jax.ShapeDtypeStruct((weight.shape[0], weight.shape[1] + 128), weight.dtype),
        cost_estimate=cost(2),
        name="carry",
    )(weight, *[vector.reshape(1, -1) for vector in vectors], *earlier)


def spread_kernel(block, img_ref, near_ref, far_ref, rows_ref, offsets_ref, fill_ref, expand_ref):
    low = img_ref[0] == 0
    near, far = near_ref[...].astype(F32), far_ref[...].astype(F32)
    count = near.shape[0] // block
    width = rows_ref.shape[1]
    rows_ref[6:8] = jnp.zeros((2, width), F32)
    offsets_ref[...] = jnp.zeros_like(offsets_ref)
    plan = (
        (0, 0, 1, rows_ref, 0), (0, 1, 1, rows_ref, 1), (0, 4, 1, rows_ref, 2),
        (1, 4, 1, rows_ref, 3), (2, 0, 1, rows_ref, 4), (2, 1, 1, rows_ref, 5),
        (1, 0, 4, expand_ref, 0),
    )
    for half in range(2):
        part = jnp.where(low, near, far) if half == 0 else jnp.where(low, far, near)
        for number in range(count):
            spot = half * count + number
            lines = part[number * block : number * block + 3]
            for line, first, size, out_ref, row in plan:
                size = size * block
                out_ref[row : row + 1, spot * size : (spot + 1) * size] = lines[
                    line : line + 1, first * block : first * block + size
                ]
            size = 2 * block
            begin = spot * size + (width if half else 0)
            offsets_ref[:, begin : begin + size] = lines[0:1, size : 2 * size]
    fill_ref[...] = offsets_ref[:, 2 * width :].astype(BF)


def spread(img, near, far, block, *earlier):
    width = 2 * near.shape[0]
    place = near.shape[1] // 128 - 1
    last = pl.BlockSpec((near.shape[0], 128), lambda step: (0, place))
    shapes = [((8, width), F32), ((1, 3 * width), F32), ((1, width), BF), ((1, 4 * width), F32)]
    return pl.pallas_call(
        ordered(partial(spread_kernel, block), 3, earlier),
        grid=(1,),
        in_specs=[pl.BlockSpec(memory_space=pltpu.SMEM), last, last] + [ANY] * len(earlier),
        out_specs=[whole(shape) for shape, _ in shapes],
        out_shape=[jax.ShapeDtypeStruct(shape, kind) for shape, kind in shapes],
        cost_estimate=cost(2),
        name="spread",
    )(img.reshape(1), near, far, *earlier)


def stack_kernel(*refs):
    refs[-1][...] = jnp.concatenate([ref[...].astype(F32) for ref in refs[:-1]], 0).astype(BF)


def stack(blocks, *earlier):
    vmem = pl.BlockSpec(memory_space=pltpu.VMEM)
    rows = sum(block.shape[0] for block in blocks)
    return pl.pallas_call(
        ordered(stack_kernel, len(blocks), earlier),
        in_specs=[vmem] * len(blocks) + [ANY] * len(earlier),
        out_specs=vmem,
        out_shape=jax.ShapeDtypeStruct((rows,) + blocks[0].shape[1:], BF),
        cost_estimate=cost(1.6),
        name="stack",
    )(*blocks, *earlier)


class Gather:
    def __init__(self, block, splits=None):
        self.depth = lax.axis_size("rows") // 4
        self.bits = jnp.stack(rows_place()).astype(jnp.int32)
        self.rows, self.columns = block.shape
        self.splits = splits or (self.rows,)
        self.cut = self.columns // 256 * 128
        self.held = [block]

    def call(self, kernel, name, values, shapes, earlier):
        vmem = pl.BlockSpec(memory_space=pltpu.VMEM)
        return pl.pallas_call(
            kernel,
            in_specs=[pl.BlockSpec(memory_space=pltpu.SMEM)] + [vmem] * len(values) + [ANY] * len(earlier),
            out_specs=[vmem] * len(shapes),
            out_shape=[jax.ShapeDtypeStruct(shape, BF) for shape in shapes],
            compiler_params=pltpu.CompilerParams(vmem_limit_bytes=VMEM_LIMIT),
            cost_estimate=cost(2.3),
            name=name,
        )(self.bits, *values, *earlier)

    def shapes(self, *lead):
        return [lead + (self.rows, self.cut), lead + (self.rows, self.columns - self.cut)]

    def shift(self):
        self.far = [shift_depth(self.held[0], step) for step in range(1, self.depth)]

    def join_one(self, *earlier):
        kernel = partial(join_one_kernel, self.depth, 1)
        self.held = self.call(kernel, "join_one", self.held + self.far, self.shapes(self.depth), earlier)
        return self.held

    def swap_near(self):
        self.far = [swap_rows(part, number) for number, part in enumerate(self.held)]

    def swap_far(self):
        self.far = [swap_rows(part, 1 - number) for number, part in enumerate(self.held)]

    def pairs(self):
        return [array for pair in zip(self.held, self.far) for array in pair]

    def join_two(self, *earlier):
        kernel = partial(join_two_kernel, 1)
        self.held = self.call(kernel, "join_two", self.pairs(), self.shapes(self.depth, 2), earlier)
        return self.held

    def join_three(self, *earlier):
        shapes = [(self.depth, 2, 2, rows, self.columns) for rows in self.splits]
        kernel = partial(join_three_kernel, self.splits)
        self.held = self.call(kernel, "join_three", self.pairs(), shapes, earlier)
        return self.held

    def swap_cores(self):
        flat = [block.reshape(-1, self.columns) for block in self.held]
        return [(block, swap_img(block)) for block in flat]


def fold_one_kernel(count, bits_ref, *refs):
    ins = refs[: 2 * count]
    a_give, a_keep, b_give, b_keep = refs[-4:]
    x, y = bits_ref[0], bits_ref[1]
    cut = a_keep.shape[-1]
    begin = 0
    for near_ref, far_ref in zip(ins[:count], ins[count:]):
        columns = near_ref.shape[-1]
        pieces = [(max(begin, 0), min(begin + columns, cut), True), (max(begin, cut), begin + columns, False)]
        for low, high, first in pieces:
            if low >= high:
                continue
            here = slice(low - begin, high - begin)
            there = slice(low, high) if first else slice(low - cut, high - cut)
            for level in range(near_ref.shape[0]):
                for side in range(2):
                    if first:
                        kept, given = (level, side, x), (level, side, 1 - x)
                    else:
                        kept, given = (level, y, side), (level, 1 - y, side)
                    keep, give = (a_keep, a_give) if first else (b_keep, b_give)
                    value = near_ref[kept + (slice(None), here)].astype(F32) + far_ref[kept + (slice(None), here)].astype(F32)
                    keep[level, side, :, there] = value
                    value = near_ref[given + (slice(None), here)].astype(F32) + far_ref[given + (slice(None), here)].astype(F32)
                    give[level, side, :, there] = value.astype(BF)
        begin += columns


def fold_two_kernel(bits_ref, a_near, a_far, b_near, b_far, *refs):
    a_give, a_keep, b_give, b_keep = refs[-4:]
    x, y = bits_ref[0], bits_ref[1]
    for level in range(a_near.shape[0]):
        a_keep[level] = a_near[level, y] + a_far[level, y].astype(F32)
        a_give[level] = (a_near[level, 1 - y] + a_far[level, 1 - y].astype(F32)).astype(BF)
        b_keep[level] = b_near[level, x] + b_far[level, x].astype(F32)
        b_give[level] = (b_near[level, 1 - x] + b_far[level, 1 - x].astype(F32)).astype(BF)


def fold_three_kernel(depth, bits_ref, a_near, a_far, b_near, b_far, *refs):
    place = bits_ref[2]
    keep, gives = refs[-depth], refs[len(refs) - depth + 1 :]
    cut = a_near.shape[-1]
    for step, out in enumerate((keep,) + tuple(gives)):
        spot = lax.rem(place + step, depth)
        out[:, :cut] = (a_near[spot] + a_far[spot].astype(F32)).astype(out.dtype)
        out[:, cut:] = (b_near[spot] + b_far[spot].astype(F32)).astype(out.dtype)


def fold_call(kernel, name, bits, values, outs, earlier):
    vmem = pl.BlockSpec(memory_space=pltpu.VMEM)
    return pl.pallas_call(
        kernel,
        in_specs=[pl.BlockSpec(memory_space=pltpu.SMEM)] + [vmem] * len(values)
        + [pl.BlockSpec(memory_space=pl.ANY)] * len(earlier),
        out_specs=[vmem] * len(outs),
        out_shape=[jax.ShapeDtypeStruct(shape, kind) for shape, kind in outs],
        compiler_params=pltpu.CompilerParams(vmem_limit_bytes=VMEM_LIMIT),
        cost_estimate=cost(2.3),
        name=name,
    )(bits, *values, *earlier)


class Scatter:
    def __init__(self, give, keep):
        self.depth = lax.axis_size("rows") // 4
        self.columns = sum(part.shape[-1] for part in keep)
        self.cut = self.columns // 256 * 128
        self.bits = jnp.stack(rows_place()).astype(jnp.int32)
        self.shape = (self.depth, 2, 2, keep[0].shape[0] // lax.axis_size("rows"), -1)
        self.give, self.keep = give, keep

    def swap_near(self):
        self.far = [swap_img(part) for part in self.give]

    def outs(self, *lead):
        rows = self.shape[3]
        first, second = lead + (rows, self.cut), lead + (rows, self.columns - self.cut)
        return [(first, BF), (first, F32), (second, BF), (second, F32)]

    def fold_one(self, *earlier):
        values = [part.reshape(self.shape) for part in list(self.keep) + self.far]
        kernel = partial(fold_one_kernel, len(self.keep))
        self.out = fold_call(kernel, "fold_one", self.bits, values, self.outs(self.depth, 2), earlier)
        return self.out

    def swap_middle(self):
        self.far = swap_rows(self.out[0], 0), swap_rows(self.out[2], 1)
        return self.far

    def fold_two(self, *earlier):
        values = [self.out[1], self.far[0], self.out[3], self.far[1]]
        self.out = fold_call(
            fold_two_kernel, "fold_two", self.bits, values, self.outs(self.depth), earlier
        )
        return self.out

    def swap_far(self):
        self.far = swap_rows(self.out[0], 1), swap_rows(self.out[2], 0)
        return self.far

    def fold_three(self, *earlier):
        depth, rows = self.depth, self.shape[3]
        block = (rows, self.columns)
        vmem = pl.BlockSpec(memory_space=pltpu.VMEM)
        self.out = pl.pallas_call(
            partial(fold_three_kernel, depth),
            in_specs=[pl.BlockSpec(memory_space=pltpu.SMEM)] + [vmem] * 4
            + [pl.BlockSpec(memory_space=pl.ANY)] * len(earlier),
            out_specs=[vmem] * depth,
            out_shape=[jax.ShapeDtypeStruct(block, F32)]
            + [jax.ShapeDtypeStruct(block, BF) for _ in range(depth - 1)],
            compiler_params=pltpu.CompilerParams(vmem_limit_bytes=VMEM_LIMIT),
            cost_estimate=cost(2.5),
            name="fold_three",
        )(self.bits, self.out[1], self.far[0], self.out[3], self.far[1], *earlier)
        return self.out

    def swap_last(self):
        return [self.out[0]] + [shift_depth(self.out[step], step) for step in range(1, self.depth)]

    def last(self):
        parts = self.swap_last()
        return sum((part.astype(F32) for part in parts[1:]), parts[0])


def sum_all(value):
    value = value + swap_img(value)
    value = value + swap_rows(value, 0)
    value = value + swap_rows(value, 1)
    return jnp.sum(gather_depth(value), axis=0)


def layer_norm(value, gain, bias):
    center = jnp.mean(value, axis=-1, keepdims=True)
    centred = value - center
    variance = jnp.mean(centred * centred, axis=-1, keepdims=True)
    return centred * lax.rsqrt(variance + 1e-06) * gain + bias


def to_odd(block):
    count = lax.axis_size("rows")
    return lax.ppermute(block, "rows", [(place, place + 1) for place in range(0, count, 2)])


def to_even(block):
    count = lax.axis_size("rows")
    return lax.ppermute(block, "rows", [(place + 1, place) for place in range(0, count, 2)])


def local(
    tokens,
    extent,
    pre_gain,
    pre_bias,
    triple_weight,
    triple_bias,
    height_table,
    width_table,
    output_weight,
    output_bias,
    post_gain,
    post_bias,
    expand_weight,
    expand_bias,
    reduce_weight,
    reduce_bias,
    cotangent,
):
    rows_dev, _, width = tokens.shape
    moved = rows_dev - WIN
    block = pre_gain.shape[0]
    parity = lax.axis_index("rows") % 2
    image = lax.axis_index("img") * (lax.axis_size("rows") // 2) + lax.axis_index("rows") // 2
    sides = lax.dynamic_slice(extent, (image, 0), (1, 2))

    img = lax.axis_index("img")
    last = []

    def then(result):
        arrays = result if isinstance(result, (list, tuple)) else [result]
        last[:] = [min(arrays, key=lambda array: array.size)]
        return result

    band_row, column_of = jnp.asarray(BAND_ROW), jnp.asarray(COLUMN)
    real_row = jnp.where(parity == 0, band_row, band_row + WIN)
    inside = (real_row < sides[0, 0]) & (column_of < sides[0, 1]) & (jnp.asarray(VALID) == 1)
    inside = inside & ((parity == 1) | (band_row < WIN))
    mask = inside.astype(F32)[:, None]
    table = reversed_table(height_table, width_table)
    vectors = (
        pre_gain, pre_bias, triple_bias, output_bias, post_gain, post_bias, expand_bias, reduce_bias,
    )

    far_tokens = to_odd(tokens[WIN:, :REAL])
    one = Gather(then(carry(triple_weight, vectors)))
    one.shift()
    two = Gather(
        then(stack([reduce_weight, output_weight], *last)), (reduce_weight.shape[0], block)
    )
    then(one.join_one(*last))
    one.swap_near()
    two.shift()
    x = then(pack(parity, tokens, far_tokens, mask, False, *last))
    three = Gather(then(stack([expand_weight], *last)))
    then(one.join_two(*last, *two.far[::2]))
    one.swap_far()
    far_pulls = to_odd(cotangent[WIN:, :REAL])
    then(one.join_three(*last, *two.far[1::2]))
    (triple_pair,) = one.swap_cores()
    then(two.join_one(*last))
    two.swap_near()
    rows, offsets, fill, hidden_bias = then(spread(img, *triple_pair, block, *last))
    three.shift()
    incoming = then(pack(parity, cotangent, far_pulls, mask, True, *last))
    then(two.join_two(*last))
    two.swap_far()
    entry, joint = then(project(img, x, mask, rows, *triple_pair, offsets, *last))
    heads = then(attend(joint, fill, table, 0, 3, (), *last, *three.far[::2]))
    then(three.join_one(*last))
    three.swap_near()
    mixed, lse, features = then(attend(joint, fill, table, 3, 3, heads, *last))
    then(two.join_three(*last))
    reduce_pair, output_pair = two.swap_cores()
    then(three.join_two(*last))
    three.swap_far()
    middle, entry_two = then(mix(img, mixed, *output_pair, rows, x, mask, *last))
    then(three.join_three(*last))
    (expand_pair,) = three.swap_cores()

    result, grad_entry_two, reduce_grad, expand_far, expand_near, hidden_sums = then(
        mlp(img, entry_two, incoming, *expand_pair, hidden_bias, *reduce_pair, *last)
    )
    reduce_shard = lax.psum_scatter(reduce_grad, ("img", "rows"), scatter_dimension=0, tiled=True).astype(F32)
    grad_middle, grad_mixed, output_far, output_near, out_win, mix_sums = then(
        mix_back(img, grad_entry_two, result, middle, incoming, mask, rows, *output_pair, mixed, *last)
    )
    first_sum = Scatter([expand_far, output_far], [expand_near, output_near])
    first_sum.swap_near()
    then(first_sum.fold_one(*last))
    first_sum.swap_middle()
    out_rows = to_even(then(send_rows(out_win, moved, *last)))
    grad_joint, tables, joint_sums = then(
        attend_back(joint, grad_mixed, lse, features, fill, table, 0, HEADS // 2, *last)
    )
    joint_far, joint_near = then(entry_grads(img, entry, grad_joint, *last))
    last_sum = Scatter([joint_far], [joint_near])
    last_sum.swap_near()
    then(first_sum.fold_two(*last))
    first_sum.swap_far()
    grad_win, norm_sums = then(
        project_back(img, x, mask, rows, grad_middle, grad_joint, *triple_pair, *last)
    )
    then(last_sum.fold_one(*last, out_rows))
    last_sum.swap_middle()
    then(first_sum.fold_three(*last))
    first_parts = first_sum.swap_last()
    small = then(sums(norm_sums, joint_sums, mix_sums, hidden_sums, tables, *last))
    grad_rows = to_even(then(send_rows(grad_win, moved, *last)))
    small = then(add(small, swap_img(small), *last))
    block_output = then(unpack(parity, out_win, out_rows, tokens.shape, *last))
    then(last_sum.fold_two(*last))
    last_sum.swap_far()
    small = then(add(small, swap_rows(small, 0), *last))
    expand_shard, output_shard = then(settle(first_parts, expand_far.shape[1], *last))
    then(last_sum.fold_three(*last))
    last_parts = last_sum.swap_last()
    small = then(add(small, swap_rows(small, 1), *last))
    depths = [small] + [shift_depth(small, step) for step in range(1, lax.axis_size("rows") // 4)]
    input_grad = then(unpack(parity, grad_win, grad_rows, tokens.shape, *last))
    triple_shard = then(place(last_parts, *last))
    number = img * lax.axis_size("rows") + lax.axis_index("rows")
    number = jnp.stack([number, rows_place()[2]]).astype(jnp.int32)
    shares = share(number, depths, block, height_table.shape[0], *last)
    pre_gain_grad, pre_bias_grad, output_bias_grad, post_gain_grad, post_bias_grad, reduce_bias_grad = [
        array.reshape(-1) for array in shares[:6]
    ]
    return (
        block_output,
        input_grad,
        pre_gain_grad,
        pre_bias_grad,
        triple_shard,
        shares[6].reshape(-1),
        shares[8],
        shares[9],
        output_shard,
        output_bias_grad,
        post_gain_grad,
        post_bias_grad,
        expand_shard,
        shares[7].reshape(-1),
        reduce_shard,
        reduce_bias_grad,
    )


def solution(mesh):
    split = P(("img", "rows"))
    flat = P(("img", "rows"), None)
    grids = P(("img", "rows"), None, None)
    in_specs = (
        grids, P(), split, split, flat, split, P(), P(), flat, split, split, split, flat, split,
        flat, split, grids,
    )
    out_specs = (
        grids, grids, split, split, flat, split, P(), P(), flat, split, split, split, flat, split,
        flat, split,
    )
    return jax.shard_map(local, mesh=mesh, in_specs=in_specs, out_specs=out_specs, check_vma=False)
```

```python
from functools import partial

import jax
import jax.numpy as jnp
import numpy as np
from jax import lax
from jax.experimental import pallas as pl
from jax.experimental.pallas import tpu as pltpu
from jax.sharding import PartitionSpec as P

HEADS = 12
HEAD_DIM = 64
WIN = 14
REAL = 32
KEYS = 208
BF = jnp.bfloat16
F32 = jnp.float32
VMEM_LIMIT = 60 * 2**20


def cost(microseconds):
    return pl.CostEstimate(flops=int(microseconds * 1e9), bytes_accessed=1, transcendentals=0)


ANY = pl.BlockSpec(memory_space=pl.ANY)

SEGMENTS = []
_offset = 0
for _row, _rows in ((0, WIN), (WIN, REAL - 2 * WIN)):
    for _col, _cols in ((0, WIN), (WIN, WIN), (2 * WIN, REAL - 2 * WIN)):
        _padded = -(-_rows * _cols // 16) * 16
        SEGMENTS.append((_row, _rows, _col, _cols, _padded, _offset))
        _offset += _padded
TOKENS = _offset
BAND = REAL - WIN


def ordered(kernel, count, earlier):
    def body(*refs):
        kernel(*refs[:count], *refs[count + len(earlier) :])

    return body


def window_constants():
    band_row = np.full((TOKENS,), 0, np.int32)
    column = np.full((TOKENS,), 0, np.int32)
    valid = np.zeros((TOKENS,), np.int32)
    along = np.zeros((TOKENS,), np.int32)
    across = np.zeros((TOKENS,), np.int32)
    onehots = np.zeros((len(SEGMENTS), KEYS, 128), np.float32)
    for number, (row, rows, col, cols, padded, offset) in enumerate(SEGMENTS):
        spots = [(a, b) for a in range(rows) for b in range(cols)]
        for place, (a, b) in enumerate(spots):
            band_row[offset + place] = row + a
            column[offset + place] = col + b
            valid[offset + place] = 1
            along[offset + place] = a
            across[offset + place] = b
        rest = [(s, t) for s in range(WIN) for t in range(WIN) if s >= rows or t >= cols]
        slots = spots + [None] * (padded - len(spots)) + rest
        slots = slots + [None] * (KEYS - len(slots))
        for place, spot in enumerate(slots):
            for head in range(2):
                if spot is None:
                    onehots[number, place, 32 * head + 15] = -1e30
                else:
                    for part in range(2):
                        onehots[number, place, 32 * head + 16 * part + spot[0]] = 1
                        onehots[number, place, 64 + 32 * head + 16 * part + spot[1]] = 1
    return band_row, column, valid, along, across, onehots


BAND_ROW, COLUMN, VALID, ALONG, ACROSS, ONEHOTS = window_constants()


def shift_amounts():
    amounts = np.zeros((TOKENS, 128), np.int32)
    amounts[:, :64] = (WIN - 1 - ALONG)[:, None]
    amounts[:, 64:] = (WIN - 1 - ACROSS)[:, None]
    return amounts


SHIFTS = shift_amounts()


def dot_t(left, right):
    return lax.dot_general(left, right, (((1,), (1,)), ((), ())), preferred_element_type=F32)


def dot_f(left, right):
    return lax.dot_general(left, right, (((0,), (0,)), ((), ())), preferred_element_type=F32)


def dot_n(left, right):
    return lax.dot_general(left, right, (((1,), (0,)), ((), ())), preferred_element_type=F32)


def lanes_of(shape):
    return lax.broadcasted_iota(jnp.int32, shape, len(shape) - 1)


def relative_features(queries, table, shifts):
    terms = dot_n(queries, table)
    for bit in range(4):
        rolled = pltpu.roll(terms, 128 - (1 << bit), 1)
        terms = jnp.where((shifts & (1 << bit)) != 0, rolled, terms)
    high = terms.astype(BF).astype(F32)
    low = pltpu.roll(terms - high, 16, 1)
    lane = lanes_of(terms.shape) & 31
    mixed = jnp.where(lane < WIN, high, jnp.where((lane >= 16) & (lane < 16 + WIN), low, 0.0))
    return jnp.where(lane == 15, 1.0, mixed).astype(BF)


def stacked_queries(queries, features, start, count):
    lane = lanes_of((count, 128))
    first = lane < 64
    even = (lane & 32) == 0
    part = queries[start : start + count] * jnp.asarray(0.125, BF)
    extra = features[start : start + count]
    zero = jnp.zeros_like(part)
    top = jnp.concatenate([jnp.where(first, part, zero), jnp.where(even, extra, zero)], 1)
    low = jnp.concatenate([jnp.where(first, zero, part), jnp.where(even, zero, extra)], 1)
    return jnp.concatenate([top, low], 0)


def window_keys(array, start, count, fill):
    if count == KEYS:
        return array[start : start + count]
    rest = jnp.broadcast_to(fill, (KEYS - count, 128)).astype(BF)
    return jnp.concatenate([array[start : start + count], rest], 0)


def tiles_of(total):
    return [(begin, min(128, total - begin)) for begin in range(0, total, 128)]


def lane_spots():
    spots = []
    base = 0
    for _, _, _, _, count, _ in SEGMENTS:
        spots.append((base, 2 * count))
        base += -(-2 * count // 128) * 128
    return spots


def window_sides(number, queries, features, keys, onehots_ref):
    _, _, _, _, count, start = SEGMENTS[number]
    left = stacked_queries(queries, features, start, count)
    none = jnp.zeros((1, 128), BF)
    right = jnp.concatenate([window_keys(keys, start, count, none), onehots_ref[number]], 1)
    return left, right


def attend_kernel(
    q_ref, k_ref, v_ref, fill_ref, table_ref, shifts_ref, onehots_ref,
    mixed_ref, lse_ref, features_ref, scores_ref, weights_ref,
):
    queries = q_ref[...]
    features = relative_features(queries, table_ref[...], shifts_ref[...])
    features_ref[...] = features
    keys, values = k_ref[...], v_ref[...]
    fill = fill_ref[...]
    spots = lane_spots()
    for number, (base, size) in enumerate(spots):
        left, right = window_sides(number, queries, features, keys, onehots_ref)
        scores_ref[:, base : base + size] = dot_t(right, left)
    totals = []
    for base, size in spots:
        scores = scores_ref[:, base : base + size]
        top = jnp.max(scores, axis=0, keepdims=True)
        weights = jnp.exp(scores - top)
        total = jnp.sum(weights, axis=0, keepdims=True)
        lse_ref[0, 0:1, base : base + size] = top + jnp.log(total)
        weights_ref[:, base : base + size] = weights.astype(BF)
        totals.append(1.0 / total)
    for (_, _, _, _, count, start), (base, size), scale in zip(SEGMENTS, spots, totals):
        held = window_keys(values, start, count, fill).T
        both = (dot_n(held, weights_ref[:, base : base + size]) * scale).T
        lane = lanes_of((count, 128))
        mixed = jnp.where(lane < 64, both[:count], both[count:])
        mixed_ref[start : start + count, :] = mixed.astype(BF)


LSE = sum(-(-2 * segment[4] // 128) * 128 for segment in SEGMENTS)


def attend_back_kernel(
    q_ref, k_ref, v_ref, g_ref, lse_ref, features_ref, fill_ref, table_ref, shifts_ref, onehots_ref,
    dqkv_ref, dtable_ref, dbias_ref,
    scores_ref, dprobs_ref, probs_ref, dscores_ref, back_ref, slots_ref,
):
    queries = q_ref[...]
    shifts = shifts_ref[...]
    table = table_ref[...]
    features = features_ref[...]
    keys, values, grads = k_ref[...], v_ref[...], g_ref[...]
    fill = fill_ref[...]
    spots = lane_spots()

    def stacked_pulls(start, count):
        first = lanes_of((count, 128)) < 64
        part = grads[start : start + count]
        zero = jnp.zeros_like(part)
        return jnp.concatenate([jnp.where(first, part, zero), jnp.where(first, zero, part)], 0)

    for number, (base, size) in enumerate(spots):
        _, _, _, _, count, start = SEGMENTS[number]
        left, right = window_sides(number, queries, features, keys, onehots_ref)
        scores_ref[:, base : base + size] = dot_t(right, left)
        held = window_keys(values, start, count, fill)
        dprobs_ref[:, base : base + size] = dot_t(held, stacked_pulls(start, count))
    for base, size in spots:
        lanes = slice(base, base + size)
        probs = jnp.exp(scores_ref[:, lanes] - lse_ref[0, 0:1, lanes])
        product = probs * dprobs_ref[:, lanes]
        delta = jnp.sum(product, axis=0, keepdims=True)
        probs_ref[:, lanes] = probs.astype(BF)
        dscores_ref[:, lanes] = (product - probs * delta).astype(BF)
    bias_sum = jnp.zeros((1, 128), F32)
    for number, (base, size) in enumerate(spots):
        _, _, _, _, count, start = SEGMENTS[number]
        left, right = window_sides(number, queries, features, keys, onehots_ref)
        dscores = dscores_ref[:, base : base + size]
        dvalues = dot_n(probs_ref[:, base : base + size], stacked_pulls(start, count))
        dkeys = dot_n(dscores, left[:, :128])
        dqkv_ref[start : start + count, 256:] = dvalues[:count].astype(BF)
        dqkv_ref[start : start + count, 128:256] = dkeys[:count].astype(BF)
        bias_sum = bias_sum + jnp.sum(dvalues, axis=0, keepdims=True)
        both = dot_f(dscores, right)
        lane = lanes_of((count, 128))
        back_ref[start : start + count, :128] = jnp.where(lane < 64, both[:count, :128], both[count:, :128])
        back_ref[start : start + count, 128:] = jnp.where(
            (lane & 32) == 0, both[:count, 128:], both[count:, 128:]
        )
    lane = lanes_of((TOKENS, 128)) & 31
    slots = jnp.where(lane < WIN, back_ref[:, 128:], 0.0)
    for bit in range(4):
        rolled = pltpu.roll(slots, 1 << bit, 1)
        slots = jnp.where((shifts & (1 << bit)) != 0, rolled, slots)
    high = slots.astype(BF)
    low = (slots - high.astype(F32)).astype(BF)
    slots_ref[:, :128] = high
    slots_ref[:, 128:] = low
    dq = back_ref[:, :128] * 0.125 + dot_t(slots_ref[...], jnp.concatenate([table, table], 1))
    dq = dq.astype(BF)
    dqkv_ref[:, :128] = dq
    found = dot_f(slots_ref[...], queries)
    dtable_ref[0] = found[:128] + found[128:]
    query_sum = jnp.sum(dq.astype(F32), axis=0, keepdims=True)
    dbias_ref[...] = jnp.concatenate([query_sum, bias_sum], 0)


def whole(shape):
    return pl.BlockSpec(shape, lambda step: (0,) * len(shape))


def column(offset, rows=TOKENS):
    return pl.BlockSpec((rows, 128), lambda step: (0, offset + step))


def reversed_table(height_table, width_table):
    slots = height_table.shape[0]
    pad = ((0, 0), (0, 32 - slots))
    height = jnp.pad(height_table[::-1].T, pad)
    width = jnp.pad(width_table[::-1].T, pad)
    none = jnp.zeros_like(height)
    top = jnp.concatenate([height, none, width, none], 1)
    low = jnp.concatenate([none, height, none, width], 1)
    return jnp.concatenate([top, low], 0)


def attend(joint, fill, table, begin, count, given, *earlier):
    pairs = HEADS // 2
    shapes = [
        jax.ShapeDtypeStruct((TOKENS, pairs * 128), BF),
        jax.ShapeDtypeStruct((pairs, 8, LSE), F32),
        jax.ShapeDtypeStruct((TOKENS, pairs * 128), BF),
    ]
    return pl.pallas_call(
        ordered(attend_kernel, 7, tuple(given) + earlier),
        grid=(count,),
        in_specs=[
            column(begin), column(pairs + begin), column(2 * pairs + begin), column(begin, 1),
            whole((128, 128)), whole((TOKENS, 128)), whole((len(SEGMENTS), KEYS, 128)),
        ] + [ANY] * (len(given) + len(earlier)),
        out_specs=[
            column(begin), pl.BlockSpec((1, 8, LSE), lambda step: (begin + step, 0, 0)), column(begin),
        ],
        out_shape=shapes,
        input_output_aliases={7 + place: place for place in range(len(given))},
        scratch_shapes=[pltpu.VMEM((KEYS, LSE), F32), pltpu.VMEM((KEYS, LSE), BF)],
        compiler_params=pltpu.CompilerParams(vmem_limit_bytes=VMEM_LIMIT),
        cost_estimate=cost(11),
        name="attend",
    )(joint, joint, joint, fill, table, jnp.asarray(SHIFTS), jnp.asarray(ONEHOTS, BF), *given, *earlier)


def attend_back(joint, grad_mixed, lse, features, fill, table, begin, count, *earlier):
    pairs = HEADS // 2

    def kernel(*refs):
        attend_back_kernel(*refs[:10], *refs[10 + len(earlier) :])

    return pl.pallas_call(
        kernel,
        grid=(count,),
        in_specs=[
            column(begin), column(pairs + begin), column(2 * pairs + begin), column(begin),
            pl.BlockSpec((1, 8, LSE), lambda step: (begin + step, 0, 0)), column(begin), column(begin, 1),
            whole((128, 128)), whole((TOKENS, 128)), whole((len(SEGMENTS), KEYS, 128)),
        ] + [pl.BlockSpec(memory_space=pl.ANY)] * len(earlier),
        out_specs=[
            pl.BlockSpec((TOKENS, 384), lambda step: (0, step)),
            pl.BlockSpec((1, 128, 128), lambda step: (step, 0, 0)), column(0, 2),
        ],
        out_shape=[
            jax.ShapeDtypeStruct((TOKENS, count * 384), BF),
            jax.ShapeDtypeStruct((count, 128, 128), F32),
            jax.ShapeDtypeStruct((2, count * 128), F32),
        ],
        scratch_shapes=[
            pltpu.VMEM((KEYS, LSE), F32), pltpu.VMEM((KEYS, LSE), F32),
            pltpu.VMEM((KEYS, LSE), BF), pltpu.VMEM((KEYS, LSE), BF),
            pltpu.VMEM((TOKENS, 256), F32), pltpu.VMEM((TOKENS, 256), BF),
        ],
        compiler_params=pltpu.CompilerParams(vmem_limit_bytes=VMEM_LIMIT),
        cost_estimate=cost(9),
        name="attend_back",
    )(
        joint, joint, joint, grad_mixed, lse, features, fill, table, jnp.asarray(SHIFTS), jnp.asarray(ONEHOTS, BF),
        *earlier,
    )


def tie(value, *earlier):
    def kernel(*refs):
        pass

    return pl.pallas_call(
        kernel,
        in_specs=[pl.BlockSpec(memory_space=pl.ANY)] * (1 + len(earlier)),
        out_specs=pl.BlockSpec(memory_space=pl.ANY),
        out_shape=jax.ShapeDtypeStruct(value.shape, value.dtype),
        input_output_aliases={0: 0},
        name="tie",
    )(value, *earlier)


def table_grads(found, slots):
    total = jnp.sum(found, axis=0)
    height = total[0:32, :64] + total[32:64, 64:]
    width = total[64:96, :64] + total[96:128, 64:]
    return height[:slots][::-1], width[:slots][::-1]


def pack_kernel(begin, moved, parity_ref, own_ref, far_ref, mask_ref, out_ref, stage_ref):
    parity = parity_ref[0]
    stage_ref[...] = jnp.zeros_like(stage_ref)
    for row in range(BAND):
        if row < moved:
            line = jnp.where(parity == 0, own_ref[row, :REAL], far_ref[begin + row]).astype(F32)
        else:
            line = own_ref[row - moved * parity, :REAL].astype(F32)
        for first, rows, col, cols, _, offset in SEGMENTS:
            if first <= row < first + rows:
                place = offset + (row - first) * cols
                stage_ref[place : place + cols, :] = line[col : col + cols]
    if begin:
        out_ref[...] = (stage_ref[...] * mask_ref[...]).astype(out_ref.dtype)
    else:
        out_ref[...] = stage_ref[...].astype(out_ref.dtype)


def pack(parity, own, far, mask, begin, *earlier):
    width = own.shape[2]
    vmem = pl.BlockSpec(memory_space=pltpu.VMEM)
    return pl.pallas_call(
        ordered(partial(pack_kernel, begin, far.shape[0] // 2), 4, earlier),
        in_specs=[pl.BlockSpec(memory_space=pltpu.SMEM), vmem, vmem, vmem] + [ANY] * len(earlier),
        out_specs=vmem,
        out_shape=jax.ShapeDtypeStruct((TOKENS, width), BF),
        scratch_shapes=[pltpu.VMEM((TOKENS, width), F32)],
        compiler_params=pltpu.CompilerParams(vmem_limit_bytes=VMEM_LIMIT),
        cost_estimate=cost(3),
        name="pack",
    )(parity.reshape(1), own, far, mask, *earlier)


def unpack_kernel(moved, parity_ref, win_ref, far_ref, out_ref, wide_ref, stage_ref):
    parity = parity_ref[0]
    wide_ref[...] = win_ref[...].astype(F32)
    for row in range(BAND):
        for first, rows, col, cols, _, offset in SEGMENTS:
            if first <= row < first + rows:
                place = offset + (row - first) * cols
                stage_ref[row, col : col + cols, :] = wide_ref[place : place + cols, :]
    out_ref[...] = jnp.zeros_like(out_ref)
    for row in range(out_ref.shape[0]):
        near = stage_ref[row] if row < WIN else far_ref[row - WIN].astype(F32)
        other = stage_ref[row + moved] if row + moved < BAND else jnp.zeros_like(near)
        out_ref[row, :REAL, :] = jnp.where(parity == 0, near, other).astype(out_ref.dtype)


def unpack(parity, win, far, shape, *earlier):
    width = win.shape[1]
    return pl.pallas_call(
        ordered(partial(unpack_kernel, far.shape[0]), 3, earlier),
        in_specs=[
            pl.BlockSpec(memory_space=pltpu.SMEM),
            pl.BlockSpec(memory_space=pltpu.VMEM),
            pl.BlockSpec(memory_space=pltpu.VMEM),
        ] + [ANY] * len(earlier),
        out_specs=pl.BlockSpec(memory_space=pltpu.VMEM),
        out_shape=jax.ShapeDtypeStruct(shape, BF),
        scratch_shapes=[pltpu.VMEM((TOKENS, width), F32), pltpu.VMEM((BAND, REAL, width), F32)],
        compiler_params=pltpu.CompilerParams(vmem_limit_bytes=VMEM_LIMIT),
        cost_estimate=cost(0.5),
        name="unpack",
    )(parity.reshape(1), win, far, *earlier)


def send_rows_kernel(win_ref, out_ref, wide_ref, stage_ref):
    wide_ref[...] = win_ref[...].astype(F32)
    for row in range(out_ref.shape[0]):
        for first, rows, col, cols, _, offset in SEGMENTS:
            if first <= row < first + rows:
                place = offset + (row - first) * cols
                stage_ref[row, col : col + cols, :] = wide_ref[place : place + cols, :]
    out_ref[...] = stage_ref[...].astype(out_ref.dtype)


def send_rows(win, moved, *earlier):
    width = win.shape[1]
    vmem = pl.BlockSpec(memory_space=pltpu.VMEM)
    return pl.pallas_call(
        ordered(send_rows_kernel, 1, earlier),
        in_specs=[vmem] + [ANY] * len(earlier),
        out_specs=vmem,
        out_shape=jax.ShapeDtypeStruct((moved, REAL, width), BF),
        scratch_shapes=[pltpu.VMEM((TOKENS, width), F32), pltpu.VMEM((moved, REAL, width), F32)],
        compiler_params=pltpu.CompilerParams(vmem_limit_bytes=VMEM_LIMIT),
        cost_estimate=cost(0.5),
        name="send_rows",
    )(win, *earlier)


def gelu_parts(hidden):
    bell = jnp.exp(hidden * hidden * -0.5)
    size = jnp.abs(hidden)
    turn = pl.reciprocal(1.0 + 0.3275911 * 0.7071067811865476 * size)
    poly = turn * (
        0.5 * 0.254829592
        + turn
        * (
            0.5 * -0.284496736
            + turn * (0.5 * 1.421413741 + turn * (0.5 * -1.453152027 + turn * (0.5 * 1.061405429)))
        )
    )
    tail = poly * bell
    below = jnp.where(hidden >= 0, 1.0 - tail, tail)
    return hidden * below, below + hidden * (0.3989422804014327 * bell)


def mlp_kernel(
    img_ref, entry_ref, pull_ref, expand_ref, bias_ref, reduce_ref, reduce_far_ref,
    result_ref, back_ref, dreduce_ref, dexpand_far_ref, dexpand_ref, dbias_ref, turned_ref,
):
    step = pl.program_id(0)
    first_half = step < pl.num_programs(0) // 2
    low = img_ref[0] == 0

    @pl.when(step == 0)
    def _():
        result_ref[...] = jnp.zeros_like(result_ref)
        back_ref[...] = jnp.zeros_like(back_ref)
        turned_ref[...] = entry_ref[...].T

    expand = expand_ref[...]
    reduce = jnp.where(first_half, reduce_far_ref[...], reduce_ref[...])
    pull = pull_ref[...]
    hidden = dot_n(entry_ref[...], expand) + bias_ref[...]
    active, slope = gelu_parts(hidden)
    active = active.astype(BF)
    grad = (dot_t(pull, reduce) * slope).astype(BF)
    result_ref[...] += dot_n(active, reduce)
    back_ref[...] += dot_t(grad, expand)
    dexpand = dot_n(turned_ref[...], grad)
    half = dexpand_ref.shape[0]
    dexpand_far_ref[...] = jnp.where(low, dexpand[half:], dexpand[:half]).astype(BF)
    dexpand_ref[...] = jnp.where(low, dexpand[:half], dexpand[half:]).astype(BF)
    dbias_ref[...] = jnp.sum(grad.astype(F32), axis=0, keepdims=True)
    dreduce_ref[...] = dot_f(active, pull).astype(BF)


def mlp(img, entry_two, incoming, expand, bias, reduce, reduce_far, *earlier, chunk=768):
    width = entry_two.shape[1]
    hidden = bias.shape[1]
    tokens = entry_two.shape[0]
    steps = hidden // chunk
    half = steps // 2

    def place(step, img):
        return (step + (1 - img[0]) * half) % steps

    def fixed(rows, columns):
        return pl.BlockSpec((rows, columns), lambda step, img: (0, 0))

    def across(rows):
        return pl.BlockSpec((rows, chunk), lambda step, img: (0, place(step, img)))

    return pl.pallas_call(
        ordered(mlp_kernel, 7, earlier),
        grid_spec=pltpu.PrefetchScalarGridSpec(
            num_scalar_prefetch=1,
            grid=(steps,),
            in_specs=[
                fixed(tokens, width), fixed(tokens, width), across(width), across(1),
                pl.BlockSpec((chunk, width), lambda step, img: (jnp.maximum(step - half, 0), 0)),
                pl.BlockSpec((chunk, width), lambda step, img: (jnp.minimum(step, half - 1), 0)),
            ] + [ANY] * len(earlier),
            out_specs=[
                fixed(tokens, width), fixed(tokens, width),
                pl.BlockSpec((chunk, width), lambda step, img: (place(step, img), 0)),
                across(width // 2), across(width // 2), across(1),
            ],
            scratch_shapes=[pltpu.VMEM((width, tokens), BF)],
        ),
        out_shape=[
            jax.ShapeDtypeStruct((tokens, width), F32),
            jax.ShapeDtypeStruct((tokens, width), F32),
            jax.ShapeDtypeStruct((hidden, width), BF),
            jax.ShapeDtypeStruct((width // 2, hidden), BF),
            jax.ShapeDtypeStruct((width // 2, hidden), BF),
            jax.ShapeDtypeStruct((1, hidden), F32),
        ],
        compiler_params=pltpu.CompilerParams(vmem_limit_bytes=VMEM_LIMIT),
        cost_estimate=cost(29),
        name="mlp",
    )(img.reshape(1), entry_two, incoming, expand, bias, reduce, reduce_far, *earlier)


def project_kernel(img_ref, x_ref, mask_ref, rows_ref, near_ref, far_ref, bias_ref, entry_ref, joint_ref):
    @pl.when(pl.program_id(0) == 0)
    def _():
        value = x_ref[...].astype(F32)
        centred = value - jnp.mean(value, axis=1, keepdims=True)
        variance = jnp.mean(centred * centred, axis=1, keepdims=True)
        normed = centred * lax.rsqrt(variance + 1e-06) * rows_ref[0:1] + rows_ref[1:2]
        entry_ref[...] = (mask_ref[...] * normed).astype(BF)

    low = img_ref[0] == 0
    near, far = near_ref[...], far_ref[...]
    weight = jnp.concatenate([jnp.where(low, near, far), jnp.where(low, far, near)], 0)
    joint_ref[...] = (dot_n(entry_ref[...], weight) + bias_ref[...]).astype(BF)


def project(img, x, mask, rows, near, far, bias, *earlier, chunk=768):
    tokens, width = x.shape
    total = bias.shape[1]

    def across(rows):
        return pl.BlockSpec((rows, chunk), lambda step: (0, step))

    return pl.pallas_call(
        ordered(project_kernel, 7, earlier),
        grid=(total // chunk,),
        in_specs=[
            pl.BlockSpec(memory_space=pltpu.SMEM), whole((tokens, width)), whole((tokens, 1)),
            whole((8, width)), across(width // 2), across(width // 2), across(1),
        ] + [ANY] * len(earlier),
        out_specs=[whole((tokens, width)), across(tokens)],
        out_shape=[
            jax.ShapeDtypeStruct((tokens, width), BF), jax.ShapeDtypeStruct((tokens, total), BF),
        ],
        compiler_params=pltpu.CompilerParams(vmem_limit_bytes=VMEM_LIMIT),
        cost_estimate=cost(7),
        name="project",
    )(img.reshape(1), x, mask, rows, near, far, bias, *earlier)


def project_back_kernel(
    img_ref, x_ref, mask_ref, rows_ref, middle_ref, pull_ref,
    nq_ref, nk_ref, nv_ref, fq_ref, fk_ref, fv_ref, *refs,
):
    grad_ref, sums_ref, near_ref, far_ref = refs[-4:]
    step = pl.program_id(0)

    @pl.when(step == 0)
    def _():
        near_ref[...] = jnp.zeros_like(near_ref)
        far_ref[...] = jnp.zeros_like(far_ref)

    pull = pull_ref[...]
    near_ref[...] += dot_t(pull, jnp.concatenate([nq_ref[...], nk_ref[...], nv_ref[...]], 1))
    far_ref[...] += dot_t(pull, jnp.concatenate([fq_ref[...], fk_ref[...], fv_ref[...]], 1))

    @pl.when(step == pl.num_programs(0) - 1)
    def _():
        low = img_ref[0] == 0
        near, far = near_ref[...], far_ref[...]
        grad = jnp.concatenate([jnp.where(low, near, far), jnp.where(low, far, near)], 1) * mask_ref[...]
        value = x_ref[...].astype(F32)
        centred = value - jnp.mean(value, axis=1, keepdims=True)
        variance = jnp.mean(centred * centred, axis=1, keepdims=True)
        rstd = lax.rsqrt(variance + 1e-06)
        xhat = centred * rstd
        product = grad * xhat
        sums_ref[0:1] = jnp.sum(product, axis=0, keepdims=True)
        sums_ref[1:2] = jnp.sum(grad, axis=0, keepdims=True)
        pull = grad * rows_ref[0:1]
        back = pull - jnp.mean(pull, axis=1, keepdims=True)
        back = back - xhat * jnp.mean(pull * xhat, axis=1, keepdims=True)
        grad_ref[...] = (middle_ref[...] + rstd * back).astype(BF)


def project_back(img, x, mask, rows, grad_middle, grad_joint, near, far, *earlier):
    tokens, width = x.shape
    pairs = HEADS // 2
    half = width // 2

    def weight(part):
        return pl.BlockSpec((half, 128), lambda step: (0, part * pairs + step))

    return pl.pallas_call(
        project_back_kernel,
        grid=(pairs,),
        in_specs=[
            pl.BlockSpec(memory_space=pltpu.SMEM), whole((tokens, width)), whole((tokens, 1)),
            whole((8, width)), whole((tokens, width)),
            pl.BlockSpec((tokens, 384), lambda step: (0, step)),
            weight(0), weight(1), weight(2), weight(0), weight(1), weight(2),
        ] + [pl.BlockSpec(memory_space=pl.ANY)] * len(earlier),
        out_specs=[whole((tokens, width)), whole((2, width))],
        out_shape=[jax.ShapeDtypeStruct((tokens, width), BF), jax.ShapeDtypeStruct((2, width), F32)],
        scratch_shapes=[pltpu.VMEM((tokens, half), F32), pltpu.VMEM((tokens, half), F32)],
        compiler_params=pltpu.CompilerParams(vmem_limit_bytes=VMEM_LIMIT),
        cost_estimate=cost(11),
        name="project_back",
    )(
        img.reshape(1), x, mask, rows, grad_middle, grad_joint, near, near, near, far, far, far, *earlier
    )


def mix_kernel(mixed_ref, weight_ref, rows_ref, x_ref, mask_ref, middle_ref, entry_ref):
    branch = dot_n(mixed_ref[...], weight_ref[...]) + rows_ref[2:3]
    middle = x_ref[...].astype(F32) + mask_ref[...] * branch
    middle_ref[...] = middle
    centred = middle - jnp.mean(middle, axis=1, keepdims=True)
    variance = jnp.mean(centred * centred, axis=1, keepdims=True)
    normed = centred * lax.rsqrt(variance + 1e-06) * rows_ref[4:5] + rows_ref[5:6]
    entry_ref[...] = normed.astype(BF)


def last_columns(array, width):
    place = array.shape[1] // width - 1
    return pl.BlockSpec((array.shape[0], width), lambda step: (0, place))


def mix(mixed, weights, rows, x, mask, *earlier):
    tokens, width = x.shape
    return pl.pallas_call(
        ordered(mix_kernel, 5, earlier),
        grid=(1,),
        in_specs=[
            whole((tokens, width)), last_columns(weights, width), whole(rows.shape), whole((tokens, width)),
            whole(mask.shape),
        ] + [ANY] * len(earlier),
        out_specs=[whole((tokens, width))] * 2,
        out_shape=[jax.ShapeDtypeStruct(x.shape, F32), jax.ShapeDtypeStruct(x.shape, BF)],
        compiler_params=pltpu.CompilerParams(vmem_limit_bytes=VMEM_LIMIT),
        cost_estimate=cost(4.6),
        name="mix",
    )(mixed, weights, rows, x, mask, *earlier)


def mix_back_kernel(
    img_ref, back_ref, result_ref, middle_ref, incoming_ref, mask_ref, rows_ref, weight_ref, mixed_ref,
    grad_middle_ref, grad_mixed_ref, give_ref, keep_ref, out_ref, sums_ref,
):
    low = img_ref[0] == 0
    mask = mask_ref[...]
    middle = middle_ref[...]
    incoming = incoming_ref[...].astype(F32)
    out_ref[...] = (mask * (middle + (result_ref[...] + rows_ref[3:4]))).astype(BF)
    back = back_ref[...]
    centred = middle - jnp.mean(middle, axis=1, keepdims=True)
    variance = jnp.mean(centred * centred, axis=1, keepdims=True)
    rstd = lax.rsqrt(variance + 1e-06)
    xhat = centred * rstd
    sums_ref[1:2] = jnp.sum(back * xhat, axis=0, keepdims=True)
    sums_ref[2:3] = jnp.sum(back, axis=0, keepdims=True)
    sums_ref[3:4] = jnp.sum(incoming, axis=0, keepdims=True)
    pull = back * rows_ref[4:5]
    inner = pull - jnp.mean(pull, axis=1, keepdims=True)
    inner = inner - xhat * jnp.mean(pull * xhat, axis=1, keepdims=True)
    grad_middle = incoming + rstd * inner
    grad_middle_ref[...] = grad_middle
    branch = (mask * grad_middle).astype(BF)
    sums_ref[0:1] = jnp.sum(branch.astype(F32), axis=0, keepdims=True)
    grad_mixed_ref[...] = dot_t(branch, weight_ref[...]).astype(BF)
    half = keep_ref.shape[0]
    total = dot_f(mixed_ref[...], branch)
    give_ref[...] = jnp.where(low, total[half:], total[:half]).astype(BF)
    keep_ref[...] = jnp.where(low, total[:half], total[half:]).astype(BF)


def mix_back(img, back, result, middle, incoming, mask, rows, weights, mixed, *earlier):
    tokens, width = middle.shape
    half = (width // 2, width)
    full = whole((tokens, width))
    return pl.pallas_call(
        ordered(mix_back_kernel, 9, earlier),
        grid=(1,),
        in_specs=[
            pl.BlockSpec(memory_space=pltpu.SMEM), full, full, full, full, whole(mask.shape),
            whole(rows.shape), last_columns(weights, width), full,
        ] + [ANY] * len(earlier),
        out_specs=[full, full, whole(half), whole(half), full, whole((4, width))],
        out_shape=[
            jax.ShapeDtypeStruct((tokens, width), F32), jax.ShapeDtypeStruct((tokens, width), BF),
            jax.ShapeDtypeStruct(half, BF), jax.ShapeDtypeStruct(half, BF),
            jax.ShapeDtypeStruct((tokens, width), BF), jax.ShapeDtypeStruct((4, width), F32),
        ],
        compiler_params=pltpu.CompilerParams(vmem_limit_bytes=VMEM_LIMIT),
        cost_estimate=cost(7),
        name="mix_back",
    )(img.reshape(1), back, result, middle, incoming, mask, rows, weights, mixed, *earlier)


def entry_grads_kernel(img_ref, entry_ref, grad_ref, give_ref, keep_ref, turned_ref):
    @pl.when(pl.program_id(0) == 0)
    def _():
        turned_ref[...] = entry_ref[...].T

    low = img_ref[0] == 0
    half = keep_ref.shape[0]
    total = dot_n(turned_ref[...], grad_ref[...])
    give_ref[...] = jnp.where(low, total[half:], total[:half]).astype(BF)
    keep_ref[...] = jnp.where(low, total[:half], total[half:]).astype(BF)


def entry_grads(img, entry, grad, *earlier, chunk=768):
    tokens, width = entry.shape
    total = grad.shape[1]

    def across(rows):
        return pl.BlockSpec((rows, chunk), lambda step: (0, step))

    return pl.pallas_call(
        ordered(entry_grads_kernel, 3, earlier),
        grid=(total // chunk,),
        in_specs=[pl.BlockSpec(memory_space=pltpu.SMEM), whole((tokens, width)), across(tokens)]
        + [ANY] * len(earlier),
        out_specs=[across(width // 2), across(width // 2)],
        out_shape=[
            jax.ShapeDtypeStruct((width // 2, total), BF), jax.ShapeDtypeStruct((width // 2, total), BF),
        ],
        scratch_shapes=[pltpu.VMEM((width, tokens), BF)],
        compiler_params=pltpu.CompilerParams(vmem_limit_bytes=VMEM_LIMIT),
        cost_estimate=cost(5),
        name="entry_grads",
    )(img.reshape(1), entry, grad, *earlier)


def sums_kernel(norm_ref, joint_ref, mix_ref, expand_ref, tables_ref, out_ref):
    width = norm_ref.shape[1]
    out_ref[0:2] = norm_ref[...]
    out_ref[2:4] = joint_ref[...]
    out_ref[4:8] = mix_ref[...]
    for part in range(4):
        out_ref[8 + part : 9 + part] = expand_ref[:, part * width : (part + 1) * width]
    out_ref[12:] = jnp.zeros((out_ref.shape[0] - 12, width), F32)
    total = tables_ref[0]
    for pair in range(1, tables_ref.shape[0]):
        total = total + tables_ref[pair]
    height = total[0:32, :64] + total[32:64, 64:]
    across = total[64:96, :64] + total[96:128, 64:]
    both = jnp.concatenate([height, across], 1)
    for part in range(4):
        out_ref[16:24, part * 128 : (part + 1) * 128] = both[part * 8 : (part + 1) * 8]


def sums(norm, joint, mixed, expand, tables, *earlier):
    vmem = pl.BlockSpec(memory_space=pltpu.VMEM)
    return pl.pallas_call(
        ordered(sums_kernel, 5, earlier),
        in_specs=[vmem] * 5 + [ANY] * len(earlier),
        out_specs=vmem,
        out_shape=jax.ShapeDtypeStruct((24, norm.shape[1]), F32),
        cost_estimate=cost(1.0),
        name="sums",
    )(norm, joint, mixed, expand, tables, *earlier)


def add_kernel(one_ref, two_ref, out_ref):
    out_ref[...] = one_ref[...] + two_ref[...]


def add(one, two, *earlier):
    vmem = pl.BlockSpec(memory_space=pltpu.VMEM)
    return pl.pallas_call(
        ordered(add_kernel, 2, earlier),
        in_specs=[vmem] * 2 + [ANY] * len(earlier),
        out_specs=vmem,
        out_shape=jax.ShapeDtypeStruct(one.shape, F32),
        cost_estimate=cost(0.5),
        name="add",
    )(one, two, *earlier)


def add_depth_kernel(depth, place_ref, *refs):
    parts, out_ref = refs[:depth], refs[-1]
    total = None
    for level in range(depth):
        found = parts[0][...]
        for step in range(1, depth):
            found = jnp.where((place_ref[2] ^ step) == level, parts[step][...], found)
        total = found if total is None else total + found
    out_ref[...] = total


def add_depth(bits, parts, *earlier):
    vmem = pl.BlockSpec(memory_space=pltpu.VMEM)
    return pl.pallas_call(
        ordered(partial(add_depth_kernel, len(parts)), 1 + len(parts), earlier),
        in_specs=[pl.BlockSpec(memory_space=pltpu.SMEM)] + [vmem] * len(parts) + [ANY] * len(earlier),
        out_specs=vmem,
        out_shape=jax.ShapeDtypeStruct(parts[0].shape, F32),
        cost_estimate=cost(0.5),
        name="add_depth",
    )(bits, *parts, *earlier)


def share_kernel(block, slots, place_ref, one_ref, two_ref, *outs):
    total = one_ref[...] + two_ref[...]
    width = total.shape[1]
    begin = place_ref[0] * block

    def own(array, size, first):
        return pltpu.roll(array, lax.rem(2 * array.shape[1] - first, array.shape[1]), 1)[:, :size]

    for number, row in enumerate((0, 1, 4, 5, 6, 7)):
        outs[number][...] = own(total[row : row + 1], block, begin)
    joint = jnp.concatenate([total[2:3], total[3:4]], 1)
    outs[6][...] = own(joint, 2 * block, 2 * begin)
    hidden = jnp.concatenate([total[8 + part : 9 + part] for part in range(4)], 1)
    outs[7][...] = own(hidden, 4 * block, 4 * begin)
    for slot in range(slots):
        place = slots - 1 - slot
        line = total[16 + place % 8 : 17 + place % 8, place // 8 * 128 : place // 8 * 128 + 128]
        outs[8][slot : slot + 1] = line[:, :64]
        outs[9][slot : slot + 1] = line[:, 64:]


def share(number, one, two, block, slots, *earlier):
    vmem = pl.BlockSpec(memory_space=pltpu.VMEM)
    shapes = [(1, block)] * 6 + [(1, 2 * block), (1, 4 * block)] + [(slots, HEAD_DIM)] * 2
    return pl.pallas_call(
        ordered(partial(share_kernel, block, slots), 3, earlier),
        in_specs=[pl.BlockSpec(memory_space=pltpu.SMEM)] + [vmem] * 2 + [ANY] * len(earlier),
        out_specs=[vmem] * len(shapes),
        out_shape=[jax.ShapeDtypeStruct(shape, F32) for shape in shapes],
        cost_estimate=cost(1.8),
        name="share",
    )(number.reshape(1), one, two, *earlier)


def place_kernel(depth, *refs):
    parts, triple_ref = refs[:depth], refs[depth]
    pairs = HEADS // 2
    for pair in range(pairs):
        for part in range(3):
            begin, spot = (pair * 3 + part) * 128, (part * pairs + pair) * 128
            value = parts[0][:, begin : begin + 128]
            for other in parts[1:]:
                value = value + other[:, begin : begin + 128].astype(F32)
            triple_ref[:, spot : spot + 128] = value


def place(parts, *earlier):
    vmem = pl.BlockSpec(memory_space=pltpu.VMEM)
    return pl.pallas_call(
        ordered(partial(place_kernel, len(parts)), len(parts), earlier),
        in_specs=[vmem] * len(parts) + [ANY] * len(earlier),
        out_specs=vmem,
        out_shape=jax.ShapeDtypeStruct(parts[0].shape, F32),
        compiler_params=pltpu.CompilerParams(vmem_limit_bytes=VMEM_LIMIT),
        name="place",
    )(*parts, *earlier)


def settle_kernel(cut, *refs):
    parts, (left_ref, right_ref) = refs[:-2], refs[-2:]
    for out_ref, lanes in ((left_ref, slice(0, cut)), (right_ref, slice(cut, None))):
        value = parts[0][:, lanes]
        for part in parts[1:]:
            value = value + part[:, lanes].astype(F32)
        out_ref[...] = value


def settle(parts, cut, *earlier):
    vmem = pl.BlockSpec(memory_space=pltpu.VMEM)
    rows, columns = parts[0].shape
    return pl.pallas_call(
        ordered(partial(settle_kernel, cut), len(parts), earlier),
        in_specs=[vmem] * len(parts) + [ANY] * len(earlier),
        out_specs=[vmem] * 2,
        out_shape=[
            jax.ShapeDtypeStruct((rows, cut), F32), jax.ShapeDtypeStruct((rows, columns - cut), F32),
        ],
        cost_estimate=cost(1),
        name="settle",
    )(*parts, *earlier)


def rows_place():
    me = lax.axis_index("rows")
    return me % 2, me // 2 % 2, me // 4


def swap_rows(block, bit):
    count = lax.axis_size("rows")
    return lax.ppermute(block, "rows", [(place, place ^ (1 << bit)) for place in range(count)])


def swap_img(block):
    return lax.ppermute(block, "img", [(0, 1), (1, 0)])


def swap_depth(block, step):
    count = lax.axis_size("rows")
    return lax.ppermute(block, "rows", [(place, place ^ (4 * step)) for place in range(count)])


def halves(block):
    cut = block.shape[-1] // 256 * 128
    return block[..., :cut], block[..., cut:]


def join_one_kernel(offsets, bits_ref, *refs):
    place = bits_ref[2]
    ins, (first, second) = refs[: len(offsets)], refs[-2:]
    cut = first.shape[-1]
    for offset, part_ref in zip(offsets, ins):
        part = part_ref[...]
        first[place ^ offset] = part[:, :cut]
        second[place ^ offset] = part[:, cut:]


def join_two_kernel(count, bits_ref, *refs):
    x, y = bits_ref[0], bits_ref[1]
    ins, outs = refs[: 4 * count], refs[len(refs) - 2 * count :]
    for number in range(count):
        first, first_far, second, second_far = ins[4 * number : 4 * number + 4]
        joined, joined_two = outs[2 * number : 2 * number + 2]
        for level in range(first.shape[0]):
            joined[level, x] = first[level]
            joined[level, 1 - x] = first_far[level]
            joined_two[level, y] = second[level]
            joined_two[level, 1 - y] = second_far[level]


def join_three_kernel(begin, bits_ref, first, first_far, second, second_far, *refs):
    x, y = bits_ref[0], bits_ref[1]
    joined = refs[-1]
    cut = first.shape[-1]
    rows = slice(begin, begin + joined.shape[3])
    for level in range(first.shape[0]):
        for side in range(2):
            joined[level, y, side, :, :cut] = first[level, side, rows]
            joined[level, 1 - y, side, :, :cut] = first_far[level, side, rows]
            joined[level, side, x, :, cut:] = second[level, side, rows]
            joined[level, side, 1 - x, :, cut:] = second_far[level, side, rows]


def carry_kernel(weight_ref, *refs):
    out_ref = refs[-1]
    columns = weight_ref.shape[1]
    out_ref[:, :columns] = weight_ref[...]
    pre_gain, pre_bias, triple_bias, output_bias, post_gain, post_bias, expand_bias, reduce_bias = [
        ref[...].astype(F32) for ref in refs[:8]
    ]
    lines = []
    for parts in ((pre_gain, pre_bias, triple_bias, output_bias), (expand_bias, reduce_bias), (post_gain, post_bias)):
        size = sum(part.shape[1] for part in parts)
        lines.append(jnp.concatenate(parts + (jnp.zeros((1, 128 - size), F32),), 1))
    rest = out_ref.shape[0] - len(lines)
    if rest:
        lines.append(jnp.zeros((rest, 128), F32))
    out_ref[:, columns:] = jnp.concatenate(lines, 0).astype(out_ref.dtype)


def carry(weight, vectors, *earlier):
    vmem = pl.BlockSpec(memory_space=pltpu.VMEM)
    return pl.pallas_call(
        ordered(carry_kernel, 1 + len(vectors), earlier),
        in_specs=[vmem] * (1 + len(vectors)) + [ANY] * len(earlier),
        out_specs=vmem,
        out_shape=jax.ShapeDtypeStruct((weight.shape[0], weight.shape[1] + 128), weight.dtype),
        cost_estimate=cost(2),
        name="carry",
    )(weight, *[vector.reshape(1, -1) for vector in vectors], *earlier)


def spread_kernel(block, img_ref, near_ref, far_ref, rows_ref, offsets_ref, fill_ref, expand_ref):
    low = img_ref[0] == 0
    near, far = near_ref[...].astype(F32), far_ref[...].astype(F32)
    count = near.shape[0] // block
    width = rows_ref.shape[1]
    rows_ref[6:8] = jnp.zeros((2, width), F32)
    offsets_ref[...] = jnp.zeros_like(offsets_ref)
    plan = (
        (0, 0, 1, rows_ref, 0), (0, 1, 1, rows_ref, 1), (0, 4, 1, rows_ref, 2),
        (1, 4, 1, rows_ref, 3), (2, 0, 1, rows_ref, 4), (2, 1, 1, rows_ref, 5),
        (1, 0, 4, expand_ref, 0),
    )
    for half in range(2):
        part = jnp.where(low, near, far) if half == 0 else jnp.where(low, far, near)
        for number in range(count):
            spot = half * count + number
            lines = part[number * block : number * block + 3]
            for line, first, size, out_ref, row in plan:
                size = size * block
                out_ref[row : row + 1, spot * size : (spot + 1) * size] = lines[
                    line : line + 1, first * block : first * block + size
                ]
            size = 2 * block
            begin = spot * size + (width if half else 0)
            offsets_ref[:, begin : begin + size] = lines[0:1, size : 2 * size]
    fill_ref[...] = offsets_ref[:, 2 * width :].astype(BF)


def spread(img, near, far, block, *earlier):
    width = 2 * near.shape[0]
    place = near.shape[1] // 128 - 1
    last = pl.BlockSpec((near.shape[0], 128), lambda step: (0, place))
    shapes = [((8, width), F32), ((1, 3 * width), F32), ((1, width), BF), ((1, 4 * width), F32)]
    return pl.pallas_call(
        ordered(partial(spread_kernel, block), 3, earlier),
        grid=(1,),
        in_specs=[pl.BlockSpec(memory_space=pltpu.SMEM), last, last] + [ANY] * len(earlier),
        out_specs=[whole(shape) for shape, _ in shapes],
        out_shape=[jax.ShapeDtypeStruct(shape, kind) for shape, kind in shapes],
        cost_estimate=cost(2),
        name="spread",
    )(img.reshape(1), near, far, *earlier)


def stack_kernel(*refs):
    refs[-1][...] = jnp.concatenate([ref[...].astype(F32) for ref in refs[:-1]], 0).astype(BF)


def stack(blocks, *earlier):
    vmem = pl.BlockSpec(memory_space=pltpu.VMEM)
    rows = sum(block.shape[0] for block in blocks)
    return pl.pallas_call(
        ordered(stack_kernel, len(blocks), earlier),
        in_specs=[vmem] * len(blocks) + [ANY] * len(earlier),
        out_specs=vmem,
        out_shape=jax.ShapeDtypeStruct((rows,) + blocks[0].shape[1:], BF),
        cost_estimate=cost(1.6),
        name="stack",
    )(*blocks, *earlier)


class Gather:
    def __init__(self, block):
        self.depth = lax.axis_size("rows") // 4
        self.bits = jnp.stack(rows_place()).astype(jnp.int32)
        self.rows, self.columns = block.shape
        self.cut = self.columns // 256 * 128
        self.held = [block]

    def call(self, kernel, name, values, shapes, earlier):
        vmem = pl.BlockSpec(memory_space=pltpu.VMEM)
        return pl.pallas_call(
            kernel,
            in_specs=[pl.BlockSpec(memory_space=pltpu.SMEM)] + [vmem] * len(values) + [ANY] * len(earlier),
            out_specs=[vmem] * len(shapes),
            out_shape=[jax.ShapeDtypeStruct(shape, BF) for shape in shapes],
            compiler_params=pltpu.CompilerParams(vmem_limit_bytes=VMEM_LIMIT),
            cost_estimate=cost(2.3),
            name=name,
        )(self.bits, *values, *earlier)

    def shapes(self, *lead):
        return [lead + (self.rows, self.cut), lead + (self.rows, self.columns - self.cut)]

    def shift(self):
        held = [(0, self.held[0])]
        bit = self.depth // 2
        while bit:
            held += [(offset ^ bit, swap_depth(block, bit)) for offset, block in held]
            bit //= 2
        self.offsets = [offset for offset, _ in held]
        self.far = [block for _, block in held[1:]]

    def join_one(self, *earlier):
        kernel = partial(join_one_kernel, self.offsets)
        self.held = self.call(kernel, "join_one", self.held + self.far, self.shapes(self.depth), earlier)
        return self.held

    def swap_near(self):
        self.far = [swap_rows(part, number) for number, part in enumerate(self.held)]

    def swap_far(self):
        self.far = [swap_rows(part, 1 - number) for number, part in enumerate(self.held)]

    def pairs(self):
        return [array for pair in zip(self.held, self.far) for array in pair]

    def join_two(self, *earlier):
        kernel = partial(join_two_kernel, 1)
        self.held = self.call(kernel, "join_two", self.pairs(), self.shapes(self.depth, 2), earlier)
        return self.held

    def join_three(self, begin, rows, *earlier):
        shapes = [(self.depth, 2, 2, rows, self.columns)]
        kernel = partial(join_three_kernel, begin)
        return self.call(kernel, "join_three", self.pairs(), shapes, earlier)[0].reshape(-1, self.columns)


def fold_one_kernel(count, bits_ref, *refs):
    ins = refs[: 2 * count]
    a_give, a_keep, b_give, b_keep = refs[-4:]
    x, y = bits_ref[0], bits_ref[1]
    cut = a_keep.shape[-1]
    begin = 0
    for near_ref, far_ref in zip(ins[:count], ins[count:]):
        columns = near_ref.shape[-1]
        pieces = [(max(begin, 0), min(begin + columns, cut), True), (max(begin, cut), begin + columns, False)]
        for low, high, first in pieces:
            if low >= high:
                continue
            here = slice(low - begin, high - begin)
            there = slice(low, high) if first else slice(low - cut, high - cut)
            for level in range(near_ref.shape[0]):
                for side in range(2):
                    if first:
                        kept, given = (level, side, x), (level, side, 1 - x)
                    else:
                        kept, given = (level, y, side), (level, 1 - y, side)
                    keep, give = (a_keep, a_give) if first else (b_keep, b_give)
                    value = near_ref[kept + (slice(None), here)].astype(F32) + far_ref[kept + (slice(None), here)].astype(F32)
                    keep[level, side, :, there] = value
                    value = near_ref[given + (slice(None), here)].astype(F32) + far_ref[given + (slice(None), here)].astype(F32)
                    give[level, side, :, there] = value.astype(BF)
        begin += columns


def fold_two_kernel(bits_ref, a_near, a_far, b_near, b_far, *refs):
    a_give, a_keep, b_give, b_keep = refs[-4:]
    x, y = bits_ref[0], bits_ref[1]
    for level in range(a_near.shape[0]):
        a_keep[level] = a_near[level, y] + a_far[level, y].astype(F32)
        a_give[level] = (a_near[level, 1 - y] + a_far[level, 1 - y].astype(F32)).astype(BF)
        b_keep[level] = b_near[level, x] + b_far[level, x].astype(F32)
        b_give[level] = (b_near[level, 1 - x] + b_far[level, 1 - x].astype(F32)).astype(BF)


def fold_three_kernel(depth, bits_ref, a_near, a_far, b_near, b_far, *refs):
    place = bits_ref[2]
    keep, gives = refs[-depth], refs[len(refs) - depth + 1 :]
    cut = a_near.shape[-1]
    for step, out in enumerate((keep,) + tuple(gives)):
        spot = place ^ step
        out[:, :cut] = (a_near[spot] + a_far[spot].astype(F32)).astype(out.dtype)
        out[:, cut:] = (b_near[spot] + b_far[spot].astype(F32)).astype(out.dtype)


def fold_call(kernel, name, bits, values, outs, earlier, estimate):
    vmem = pl.BlockSpec(memory_space=pltpu.VMEM)
    return pl.pallas_call(
        kernel,
        in_specs=[pl.BlockSpec(memory_space=pltpu.SMEM)] + [vmem] * len(values)
        + [pl.BlockSpec(memory_space=pl.ANY)] * len(earlier),
        out_specs=[vmem] * len(outs),
        out_shape=[jax.ShapeDtypeStruct(shape, kind) for shape, kind in outs],
        compiler_params=pltpu.CompilerParams(vmem_limit_bytes=VMEM_LIMIT),
        cost_estimate=cost(estimate),
        name=name,
    )(bits, *values, *earlier)


class Scatter:
    def __init__(self, give, keep, costs):
        self.costs = costs
        self.depth = lax.axis_size("rows") // 4
        self.columns = sum(part.shape[-1] for part in keep)
        self.cut = self.columns // 256 * 128
        self.bits = jnp.stack(rows_place()).astype(jnp.int32)
        self.shape = (self.depth, 2, 2, keep[0].shape[0] // lax.axis_size("rows"), -1)
        self.give, self.keep = give, keep

    def swap_near(self):
        self.far = [swap_img(part) for part in self.give]

    def outs(self, *lead):
        rows = self.shape[3]
        first, second = lead + (rows, self.cut), lead + (rows, self.columns - self.cut)
        return [(first, BF), (first, F32), (second, BF), (second, F32)]

    def fold_one(self, *earlier):
        values = [part.reshape(self.shape) for part in list(self.keep) + self.far]
        kernel = partial(fold_one_kernel, len(self.keep))
        self.out = fold_call(kernel, "fold_one", self.bits, values, self.outs(self.depth, 2), earlier, self.costs[0])
        return self.out

    def swap_middle(self):
        self.far = swap_rows(self.out[0], 0), swap_rows(self.out[2], 1)
        return self.far

    def fold_two(self, *earlier):
        values = [self.out[1], self.far[0], self.out[3], self.far[1]]
        self.out = fold_call(
            fold_two_kernel, "fold_two", self.bits, values, self.outs(self.depth), earlier, self.costs[1]
        )
        return self.out

    def swap_far(self):
        self.far = swap_rows(self.out[0], 1), swap_rows(self.out[2], 0)
        return self.far

    def fold_three(self, *earlier):
        depth, rows = self.depth, self.shape[3]
        block = (rows, self.columns)
        vmem = pl.BlockSpec(memory_space=pltpu.VMEM)
        self.out = pl.pallas_call(
            partial(fold_three_kernel, depth),
            in_specs=[pl.BlockSpec(memory_space=pltpu.SMEM)] + [vmem] * 4
            + [pl.BlockSpec(memory_space=pl.ANY)] * len(earlier),
            out_specs=[vmem] * depth,
            out_shape=[jax.ShapeDtypeStruct(block, F32)]
            + [jax.ShapeDtypeStruct(block, BF) for _ in range(depth - 1)],
            compiler_params=pltpu.CompilerParams(vmem_limit_bytes=VMEM_LIMIT),
            cost_estimate=cost(self.costs[2]),
            name="fold_three",
        )(self.bits, self.out[1], self.far[0], self.out[3], self.far[1], *earlier)
        return self.out

    def swap_last(self):
        return [self.out[0]] + [swap_depth(self.out[step], step) for step in range(1, self.depth)]

    def last(self):
        parts = self.swap_last()
        return sum((part.astype(F32) for part in parts[1:]), parts[0])


def sum_all(value):
    value = value + swap_img(value)
    value = value + swap_rows(value, 0)
    value = value + swap_rows(value, 1)
    return jnp.sum(gather_depth(value), axis=0)


def layer_norm(value, gain, bias):
    center = jnp.mean(value, axis=-1, keepdims=True)
    centred = value - center
    variance = jnp.mean(centred * centred, axis=-1, keepdims=True)
    return centred * lax.rsqrt(variance + 1e-06) * gain + bias


def to_odd(block):
    count = lax.axis_size("rows")
    return lax.ppermute(block, "rows", [(place, place + 1) for place in range(0, count, 2)])


def to_even(block):
    count = lax.axis_size("rows")
    return lax.ppermute(block, "rows", [(place + 1, place) for place in range(0, count, 2)])


def local(
    tokens,
    extent,
    pre_gain,
    pre_bias,
    triple_weight,
    triple_bias,
    height_table,
    width_table,
    output_weight,
    output_bias,
    post_gain,
    post_bias,
    expand_weight,
    expand_bias,
    reduce_weight,
    reduce_bias,
    cotangent,
):
    rows_dev, _, width = tokens.shape
    moved = rows_dev - WIN
    block = pre_gain.shape[0]
    parity = lax.axis_index("rows") % 2
    image = lax.axis_index("img") * (lax.axis_size("rows") // 2) + lax.axis_index("rows") // 2
    sides = lax.dynamic_slice(extent, (image, 0), (1, 2))

    img = lax.axis_index("img")
    last = []

    def then(result):
        arrays = result if isinstance(result, (list, tuple)) else [result]
        last[:] = [min(arrays, key=lambda array: array.size)]
        return result

    band_row, column_of = jnp.asarray(BAND_ROW), jnp.asarray(COLUMN)
    real_row = jnp.where(parity == 0, band_row, band_row + WIN)
    inside = (real_row < sides[0, 0]) & (column_of < sides[0, 1]) & (jnp.asarray(VALID) == 1)
    inside = inside & ((parity == 1) | (band_row < WIN))
    mask = inside.astype(F32)[:, None]
    table = reversed_table(height_table, width_table)
    vectors = (
        pre_gain, pre_bias, triple_bias, output_bias, post_gain, post_bias, expand_bias, reduce_bias,
    )

    far_rows = to_odd(jnp.concatenate([tokens[WIN:, :REAL], cotangent[WIN:, :REAL]]))
    later_all = lax.all_gather(
        jnp.concatenate([expand_weight, output_weight], 1), ("img", "rows"), axis=0, tiled=True
    )
    one = Gather(then(carry(triple_weight, vectors)))
    one.shift()
    two = Gather(then(stack([reduce_weight], *last)))
    then(one.join_one(*last))
    one.swap_near()
    two.shift()
    x = then(pack(parity, tokens, far_rows, mask, 0, *last))
    then(one.join_two(*last, *two.far[:-1]))
    one.swap_far()
    incoming = then(pack(parity, cotangent, far_rows, mask, moved, *last))
    triple_near = then(one.join_three(0, block, *last, two.far[-1]))
    triple_pair = triple_near, swap_img(triple_near)
    then(two.join_one(*last))
    two.swap_near()
    rows, offsets, fill, hidden_bias = then(spread(img, *triple_pair, block, *last))
    entry, joint = then(project(img, x, mask, rows, *triple_pair, offsets, *last))
    then(two.join_two(*last))
    two.swap_far()
    mixed, lse, features = then(attend(joint, fill, table, 0, HEADS // 2, (), *last))
    reduce_near = then(two.join_three(0, reduce_weight.shape[0], *last))
    reduce_pair = reduce_near, swap_img(reduce_near)
    middle, entry_two = then(mix(mixed, later_all, rows, x, mask, *last))

    result, grad_entry_two, reduce_grad, expand_far, expand_near, hidden_sums = then(
        mlp(img, entry_two, incoming, later_all, hidden_bias, *reduce_pair, *last)
    )
    reduce_shard = lax.psum_scatter(reduce_grad, ("img", "rows"), scatter_dimension=0, tiled=True).astype(F32)
    grad_middle, grad_mixed, output_far, output_near, out_win, mix_sums = then(
        mix_back(img, grad_entry_two, result, middle, incoming, mask, rows, later_all, mixed, *last)
    )
    first_sum = Scatter([expand_far, output_far], [expand_near, output_near], (2.3, 2.3, 1.5))
    first_sum.swap_near()
    then(first_sum.fold_one(*last))
    first_sum.swap_middle()
    out_rows = to_even(then(send_rows(out_win, moved, *last)))
    grad_joint, tables, joint_sums = then(
        attend_back(joint, grad_mixed, lse, features, fill, table, 0, HEADS // 2, *last)
    )
    joint_far, joint_near = then(entry_grads(img, entry, grad_joint, *last))
    last_sum = Scatter([joint_far], [joint_near], (2.3, 2.3, 1.5))
    last_sum.swap_near()
    then(first_sum.fold_two(*last))
    first_sum.swap_far()
    grad_win, norm_sums = then(
        project_back(img, x, mask, rows, grad_middle, grad_joint, *triple_pair, *last)
    )
    then(last_sum.fold_one(*last, out_rows))
    last_sum.swap_middle()
    then(first_sum.fold_three(*last))
    first_parts = first_sum.swap_last()
    small = then(sums(norm_sums, joint_sums, mix_sums, hidden_sums, tables, *last))
    depths = [small] + [swap_depth(small, step) for step in range(1, lax.axis_size("rows") // 4)]
    grad_rows = to_even(then(send_rows(grad_win, moved, *last)))
    block_output = then(unpack(parity, out_win, out_rows, tokens.shape, *last, *first_parts[1:2]))
    then(last_sum.fold_two(*last))
    last_sum.swap_far()
    small = then(add_depth(last_sum.bits, depths, *last))
    expand_shard, output_shard = then(settle(first_parts, expand_far.shape[1], *last))
    small = then(add(small, swap_rows(small, 0), *last))
    then(last_sum.fold_three(*last))
    last_parts = last_sum.swap_last()
    small = then(add(small, swap_rows(small, 1), *last))
    input_grad = then(unpack(parity, grad_win, grad_rows, tokens.shape, *last))
    triple_shard = then(place(last_parts, *last))
    number = (img * lax.axis_size("rows") + lax.axis_index("rows")).astype(jnp.int32)
    shares = share(number, small, swap_img(small), block, height_table.shape[0], *last)
    pre_gain_grad, pre_bias_grad, output_bias_grad, post_gain_grad, post_bias_grad, reduce_bias_grad = [
        array.reshape(-1) for array in shares[:6]
    ]
    return (
        block_output,
        input_grad,
        pre_gain_grad,
        pre_bias_grad,
        triple_shard,
        shares[6].reshape(-1),
        shares[8],
        shares[9],
        output_shard,
        output_bias_grad,
        post_gain_grad,
        post_bias_grad,
        expand_shard,
        shares[7].reshape(-1),
        reduce_shard,
        reduce_bias_grad,
    )


def solution(mesh):
    split = P(("img", "rows"))
    flat = P(("img", "rows"), None)
    grids = P(("img", "rows"), None, None)
    in_specs = (
        grids, P(), split, split, flat, split, P(), P(), flat, split, split, split, flat, split,
        flat, split, grids,
    )
    out_specs = (
        grids, grids, split, split, flat, split, P(), P(), flat, split, split, split, flat, split,
        flat, split,
    )
    return jax.shard_map(local, mesh=mesh, in_specs=in_specs, out_specs=out_specs, check_vma=False)
```

```python
from functools import partial

import jax
import jax.numpy as jnp
import numpy as np
from jax import lax
from jax.experimental import pallas as pl
from jax.experimental.pallas import tpu as pltpu
from jax.sharding import PartitionSpec as P

HEADS = 12
HEAD_DIM = 64
WIN = 14
REAL = 32
KEYS = 208
BF = jnp.bfloat16
F32 = jnp.float32
VMEM_LIMIT = 60 * 2**20


def cost(microseconds):
    return pl.CostEstimate(flops=int(microseconds * 1e9), bytes_accessed=1, transcendentals=0)


ANY = pl.BlockSpec(memory_space=pl.ANY)

SEGMENTS = []
_offset = 0
for _row, _rows in ((0, WIN), (WIN, REAL - 2 * WIN)):
    for _col, _cols in ((0, WIN), (WIN, WIN), (2 * WIN, REAL - 2 * WIN)):
        _padded = -(-_rows * _cols // 16) * 16
        SEGMENTS.append((_row, _rows, _col, _cols, _padded, _offset))
        _offset += _padded
TOKENS = _offset
BAND = REAL - WIN


def ordered(kernel, count, earlier):
    def body(*refs):
        kernel(*refs[:count], *refs[count + len(earlier) :])

    return body


def window_constants():
    band_row = np.full((TOKENS,), 0, np.int32)
    column = np.full((TOKENS,), 0, np.int32)
    valid = np.zeros((TOKENS,), np.int32)
    along = np.zeros((TOKENS,), np.int32)
    across = np.zeros((TOKENS,), np.int32)
    onehots = np.zeros((len(SEGMENTS), KEYS, 128), np.float32)
    for number, (row, rows, col, cols, padded, offset) in enumerate(SEGMENTS):
        spots = [(a, b) for a in range(rows) for b in range(cols)]
        for place, (a, b) in enumerate(spots):
            band_row[offset + place] = row + a
            column[offset + place] = col + b
            valid[offset + place] = 1
            along[offset + place] = a
            across[offset + place] = b
        rest = [(s, t) for s in range(WIN) for t in range(WIN) if s >= rows or t >= cols]
        slots = spots + [None] * (padded - len(spots)) + rest
        slots = slots + [None] * (KEYS - len(slots))
        for place, spot in enumerate(slots):
            for head in range(2):
                if spot is None:
                    onehots[number, place, 32 * head + 15] = -1e30
                else:
                    for part in range(2):
                        onehots[number, place, 32 * head + 16 * part + spot[0]] = 1
                        onehots[number, place, 64 + 32 * head + 16 * part + spot[1]] = 1
    return band_row, column, valid, along, across, onehots


BAND_ROW, COLUMN, VALID, ALONG, ACROSS, ONEHOTS = window_constants()


def shift_amounts():
    amounts = np.zeros((TOKENS, 128), np.int32)
    amounts[:, :64] = (WIN - 1 - ALONG)[:, None]
    amounts[:, 64:] = (WIN - 1 - ACROSS)[:, None]
    return amounts


SHIFTS = shift_amounts()


def dot_t(left, right):
    return lax.dot_general(left, right, (((1,), (1,)), ((), ())), preferred_element_type=F32)


def dot_f(left, right):
    return lax.dot_general(left, right, (((0,), (0,)), ((), ())), preferred_element_type=F32)


def dot_n(left, right):
    return lax.dot_general(left, right, (((1,), (0,)), ((), ())), preferred_element_type=F32)


def lanes_of(shape):
    return lax.broadcasted_iota(jnp.int32, shape, len(shape) - 1)


def relative_features(queries, table, shifts):
    terms = dot_n(queries, table)
    for bit in range(4):
        rolled = pltpu.roll(terms, 128 - (1 << bit), 1)
        terms = jnp.where((shifts & (1 << bit)) != 0, rolled, terms)
    high = terms.astype(BF).astype(F32)
    low = pltpu.roll(terms - high, 16, 1)
    lane = lanes_of(terms.shape) & 31
    mixed = jnp.where(lane < WIN, high, jnp.where((lane >= 16) & (lane < 16 + WIN), low, 0.0))
    return jnp.where(lane == 15, 1.0, mixed).astype(BF)


def stacked_queries(queries, features, start, count):
    lane = lanes_of((count, 128))
    first = lane < 64
    even = (lane & 32) == 0
    part = queries[start : start + count] * jnp.asarray(0.125, BF)
    extra = features[start : start + count]
    zero = jnp.zeros_like(part)
    top = jnp.concatenate([jnp.where(first, part, zero), jnp.where(even, extra, zero)], 1)
    low = jnp.concatenate([jnp.where(first, zero, part), jnp.where(even, zero, extra)], 1)
    return jnp.concatenate([top, low], 0)


def window_keys(array, start, count, fill):
    if count == KEYS:
        return array[start : start + count]
    rest = jnp.broadcast_to(fill, (KEYS - count, 128)).astype(BF)
    return jnp.concatenate([array[start : start + count], rest], 0)


def tiles_of(total):
    return [(begin, min(128, total - begin)) for begin in range(0, total, 128)]


def lane_spots():
    spots = []
    base = 0
    for _, _, _, _, count, _ in SEGMENTS:
        spots.append((base, 2 * count))
        base += -(-2 * count // 128) * 128
    return spots


def window_sides(number, queries, features, keys, onehots_ref):
    _, _, _, _, count, start = SEGMENTS[number]
    left = stacked_queries(queries, features, start, count)
    none = jnp.zeros((1, 128), BF)
    right = jnp.concatenate([window_keys(keys, start, count, none), onehots_ref[number]], 1)
    return left, right


def attend_kernel(
    q_ref, k_ref, v_ref, fill_ref, table_ref, shifts_ref, onehots_ref,
    mixed_ref, lse_ref, features_ref, scores_ref, weights_ref,
):
    queries = q_ref[...]
    features = relative_features(queries, table_ref[...], shifts_ref[...])
    features_ref[...] = features
    keys, values = k_ref[...], v_ref[...]
    fill = fill_ref[...]
    spots = lane_spots()
    for number, (base, size) in enumerate(spots):
        left, right = window_sides(number, queries, features, keys, onehots_ref)
        scores_ref[:, base : base + size] = dot_t(right, left)
    totals = []
    for base, size in spots:
        scores = scores_ref[:, base : base + size]
        top = jnp.max(scores, axis=0, keepdims=True)
        weights = jnp.exp(scores - top)
        total = jnp.sum(weights, axis=0, keepdims=True)
        lse_ref[0, 0:1, base : base + size] = top + jnp.log(total)
        weights_ref[:, base : base + size] = weights.astype(BF)
        totals.append(1.0 / total)
    for (_, _, _, _, count, start), (base, size), scale in zip(SEGMENTS, spots, totals):
        held = window_keys(values, start, count, fill).T
        both = (dot_n(held, weights_ref[:, base : base + size]) * scale).T
        lane = lanes_of((count, 128))
        mixed = jnp.where(lane < 64, both[:count], both[count:])
        mixed_ref[start : start + count, :] = mixed.astype(BF)


LSE = sum(-(-2 * segment[4] // 128) * 128 for segment in SEGMENTS)


def attend_back_kernel(
    q_ref, k_ref, v_ref, g_ref, lse_ref, features_ref, fill_ref, table_ref, shifts_ref, onehots_ref,
    dqkv_ref, dtable_ref, dbias_ref,
    scores_ref, dprobs_ref, probs_ref, dscores_ref, back_ref, slots_ref,
):
    queries = q_ref[...]
    shifts = shifts_ref[...]
    table = table_ref[...]
    features = features_ref[...]
    keys, values, grads = k_ref[...], v_ref[...], g_ref[...]
    fill = fill_ref[...]
    spots = lane_spots()

    def stacked_pulls(start, count):
        first = lanes_of((count, 128)) < 64
        part = grads[start : start + count]
        zero = jnp.zeros_like(part)
        return jnp.concatenate([jnp.where(first, part, zero), jnp.where(first, zero, part)], 0)

    for number, (base, size) in enumerate(spots):
        _, _, _, _, count, start = SEGMENTS[number]
        left, right = window_sides(number, queries, features, keys, onehots_ref)
        scores_ref[:, base : base + size] = dot_t(right, left)
        held = window_keys(values, start, count, fill)
        dprobs_ref[:, base : base + size] = dot_t(held, stacked_pulls(start, count))
    for base, size in spots:
        lanes = slice(base, base + size)
        probs = jnp.exp(scores_ref[:, lanes] - lse_ref[0, 0:1, lanes])
        product = probs * dprobs_ref[:, lanes]
        delta = jnp.sum(product, axis=0, keepdims=True)
        probs_ref[:, lanes] = probs.astype(BF)
        dscores_ref[:, lanes] = (product - probs * delta).astype(BF)
    bias_sum = jnp.zeros((1, 128), F32)
    for number, (base, size) in enumerate(spots):
        _, _, _, _, count, start = SEGMENTS[number]
        left, right = window_sides(number, queries, features, keys, onehots_ref)
        dscores = dscores_ref[:, base : base + size]
        dvalues = dot_n(probs_ref[:, base : base + size], stacked_pulls(start, count))
        dkeys = dot_n(dscores, left[:, :128])
        dqkv_ref[start : start + count, 256:] = dvalues[:count].astype(BF)
        dqkv_ref[start : start + count, 128:256] = dkeys[:count].astype(BF)
        bias_sum = bias_sum + jnp.sum(dvalues, axis=0, keepdims=True)
        both = dot_f(dscores, right)
        lane = lanes_of((count, 128))
        back_ref[start : start + count, :128] = jnp.where(lane < 64, both[:count, :128], both[count:, :128])
        back_ref[start : start + count, 128:] = jnp.where(
            (lane & 32) == 0, both[:count, 128:], both[count:, 128:]
        )
    lane = lanes_of((TOKENS, 128)) & 31
    slots = jnp.where(lane < WIN, back_ref[:, 128:], 0.0)
    for bit in range(4):
        rolled = pltpu.roll(slots, 1 << bit, 1)
        slots = jnp.where((shifts & (1 << bit)) != 0, rolled, slots)
    high = slots.astype(BF)
    low = (slots - high.astype(F32)).astype(BF)
    slots_ref[:, :128] = high
    slots_ref[:, 128:] = low
    dq = back_ref[:, :128] * 0.125 + dot_t(slots_ref[...], jnp.concatenate([table, table], 1))
    dq = dq.astype(BF)
    dqkv_ref[:, :128] = dq
    found = dot_f(slots_ref[...], queries)
    dtable_ref[0] = found[:128] + found[128:]
    query_sum = jnp.sum(dq.astype(F32), axis=0, keepdims=True)
    dbias_ref[...] = jnp.concatenate([query_sum, bias_sum], 0)


def whole(shape):
    return pl.BlockSpec(shape, lambda step: (0,) * len(shape))


def column(offset, rows=TOKENS):
    return pl.BlockSpec((rows, 128), lambda step: (0, offset + step))


def reversed_table(height_table, width_table):
    slots = height_table.shape[0]
    pad = ((0, 0), (0, 32 - slots))
    height = jnp.pad(height_table[::-1].T, pad)
    width = jnp.pad(width_table[::-1].T, pad)
    none = jnp.zeros_like(height)
    top = jnp.concatenate([height, none, width, none], 1)
    low = jnp.concatenate([none, height, none, width], 1)
    return jnp.concatenate([top, low], 0)


def attend(joint, fill, table, begin, count, given, *earlier):
    pairs = HEADS // 2
    shapes = [
        jax.ShapeDtypeStruct((TOKENS, pairs * 128), BF),
        jax.ShapeDtypeStruct((pairs, 8, LSE), F32),
        jax.ShapeDtypeStruct((TOKENS, pairs * 128), BF),
    ]
    return pl.pallas_call(
        ordered(attend_kernel, 7, tuple(given) + earlier),
        grid=(count,),
        in_specs=[
            column(begin), column(pairs + begin), column(2 * pairs + begin), column(begin, 1),
            whole((128, 128)), whole((TOKENS, 128)), whole((len(SEGMENTS), KEYS, 128)),
        ] + [ANY] * (len(given) + len(earlier)),
        out_specs=[
            column(begin), pl.BlockSpec((1, 8, LSE), lambda step: (begin + step, 0, 0)), column(begin),
        ],
        out_shape=shapes,
        input_output_aliases={7 + place: place for place in range(len(given))},
        scratch_shapes=[pltpu.VMEM((KEYS, LSE), F32), pltpu.VMEM((KEYS, LSE), BF)],
        compiler_params=pltpu.CompilerParams(vmem_limit_bytes=VMEM_LIMIT),
        cost_estimate=cost(11),
        name="attend",
    )(joint, joint, joint, fill, table, jnp.asarray(SHIFTS), jnp.asarray(ONEHOTS, BF), *given, *earlier)


def attend_back(joint, grad_mixed, lse, features, fill, table, begin, count, *earlier):
    pairs = HEADS // 2

    def kernel(*refs):
        attend_back_kernel(*refs[:10], *refs[10 + len(earlier) :])

    return pl.pallas_call(
        kernel,
        grid=(count,),
        in_specs=[
            column(begin), column(pairs + begin), column(2 * pairs + begin), column(begin),
            pl.BlockSpec((1, 8, LSE), lambda step: (begin + step, 0, 0)), column(begin), column(begin, 1),
            whole((128, 128)), whole((TOKENS, 128)), whole((len(SEGMENTS), KEYS, 128)),
        ] + [pl.BlockSpec(memory_space=pl.ANY)] * len(earlier),
        out_specs=[
            pl.BlockSpec((TOKENS, 384), lambda step: (0, step)),
            pl.BlockSpec((1, 128, 128), lambda step: (step, 0, 0)), column(0, 2),
        ],
        out_shape=[
            jax.ShapeDtypeStruct((TOKENS, count * 384), BF),
            jax.ShapeDtypeStruct((count, 128, 128), F32),
            jax.ShapeDtypeStruct((2, count * 128), F32),
        ],
        scratch_shapes=[
            pltpu.VMEM((KEYS, LSE), F32), pltpu.VMEM((KEYS, LSE), F32),
            pltpu.VMEM((KEYS, LSE), BF), pltpu.VMEM((KEYS, LSE), BF),
            pltpu.VMEM((TOKENS, 256), F32), pltpu.VMEM((TOKENS, 256), BF),
        ],
        compiler_params=pltpu.CompilerParams(vmem_limit_bytes=VMEM_LIMIT),
        cost_estimate=cost(9),
        name="attend_back",
    )(
        joint, joint, joint, grad_mixed, lse, features, fill, table, jnp.asarray(SHIFTS), jnp.asarray(ONEHOTS, BF),
        *earlier,
    )


def tie(value, *earlier):
    def kernel(*refs):
        pass

    return pl.pallas_call(
        kernel,
        in_specs=[pl.BlockSpec(memory_space=pl.ANY)] * (1 + len(earlier)),
        out_specs=pl.BlockSpec(memory_space=pl.ANY),
        out_shape=jax.ShapeDtypeStruct(value.shape, value.dtype),
        input_output_aliases={0: 0},
        name="tie",
    )(value, *earlier)


def table_grads(found, slots):
    total = jnp.sum(found, axis=0)
    height = total[0:32, :64] + total[32:64, 64:]
    width = total[64:96, :64] + total[96:128, 64:]
    return height[:slots][::-1], width[:slots][::-1]


def pack_kernel(begin, moved, parity_ref, own_ref, far_ref, mask_ref, out_ref, stage_ref):
    parity = parity_ref[0]
    stage_ref[...] = jnp.zeros_like(stage_ref)
    for row in range(BAND):
        if row < moved:
            line = jnp.where(parity == 0, own_ref[row, :REAL], far_ref[begin + row]).astype(F32)
        else:
            line = own_ref[row - moved * parity, :REAL].astype(F32)
        for first, rows, col, cols, _, offset in SEGMENTS:
            if first <= row < first + rows:
                place = offset + (row - first) * cols
                stage_ref[place : place + cols, :] = line[col : col + cols]
    if begin:
        out_ref[...] = (stage_ref[...] * mask_ref[...]).astype(out_ref.dtype)
    else:
        out_ref[...] = stage_ref[...].astype(out_ref.dtype)


def pack(parity, own, far, mask, begin, *earlier):
    width = own.shape[2]
    vmem = pl.BlockSpec(memory_space=pltpu.VMEM)
    return pl.pallas_call(
        ordered(partial(pack_kernel, begin, far.shape[0] // 2), 4, earlier),
        in_specs=[pl.BlockSpec(memory_space=pltpu.SMEM), vmem, vmem, vmem] + [ANY] * len(earlier),
        out_specs=vmem,
        out_shape=jax.ShapeDtypeStruct((TOKENS, width), BF),
        scratch_shapes=[pltpu.VMEM((TOKENS, width), F32)],
        compiler_params=pltpu.CompilerParams(vmem_limit_bytes=VMEM_LIMIT),
        cost_estimate=cost(3),
        name="pack",
    )(parity.reshape(1), own, far, mask, *earlier)


def unpack_kernel(moved, parity_ref, win_ref, far_ref, out_ref, wide_ref, stage_ref):
    parity = parity_ref[0]
    wide_ref[...] = win_ref[...].astype(F32)
    for row in range(BAND):
        for first, rows, col, cols, _, offset in SEGMENTS:
            if first <= row < first + rows:
                place = offset + (row - first) * cols
                stage_ref[row, col : col + cols, :] = wide_ref[place : place + cols, :]
    out_ref[...] = jnp.zeros_like(out_ref)
    for row in range(out_ref.shape[0]):
        near = stage_ref[row] if row < WIN else far_ref[row - WIN].astype(F32)
        other = stage_ref[row + moved] if row + moved < BAND else jnp.zeros_like(near)
        out_ref[row, :REAL, :] = jnp.where(parity == 0, near, other).astype(out_ref.dtype)


def unpack(parity, win, far, shape, *earlier):
    width = win.shape[1]
    return pl.pallas_call(
        ordered(partial(unpack_kernel, far.shape[0]), 3, earlier),
        in_specs=[
            pl.BlockSpec(memory_space=pltpu.SMEM),
            pl.BlockSpec(memory_space=pltpu.VMEM),
            pl.BlockSpec(memory_space=pltpu.VMEM),
        ] + [ANY] * len(earlier),
        out_specs=pl.BlockSpec(memory_space=pltpu.VMEM),
        out_shape=jax.ShapeDtypeStruct(shape, BF),
        scratch_shapes=[pltpu.VMEM((TOKENS, width), F32), pltpu.VMEM((BAND, REAL, width), F32)],
        compiler_params=pltpu.CompilerParams(vmem_limit_bytes=VMEM_LIMIT),
        cost_estimate=cost(0.5),
        name="unpack",
    )(parity.reshape(1), win, far, *earlier)


def send_rows_kernel(win_ref, out_ref, wide_ref, stage_ref):
    wide_ref[...] = win_ref[...].astype(F32)
    for row in range(out_ref.shape[0]):
        for first, rows, col, cols, _, offset in SEGMENTS:
            if first <= row < first + rows:
                place = offset + (row - first) * cols
                stage_ref[row, col : col + cols, :] = wide_ref[place : place + cols, :]
    out_ref[...] = stage_ref[...].astype(out_ref.dtype)


def send_rows(win, moved, *earlier):
    width = win.shape[1]
    vmem = pl.BlockSpec(memory_space=pltpu.VMEM)
    return pl.pallas_call(
        ordered(send_rows_kernel, 1, earlier),
        in_specs=[vmem] + [ANY] * len(earlier),
        out_specs=vmem,
        out_shape=jax.ShapeDtypeStruct((moved, REAL, width), BF),
        scratch_shapes=[pltpu.VMEM((TOKENS, width), F32), pltpu.VMEM((moved, REAL, width), F32)],
        compiler_params=pltpu.CompilerParams(vmem_limit_bytes=VMEM_LIMIT),
        cost_estimate=cost(0.5),
        name="send_rows",
    )(win, *earlier)


def gelu_parts(hidden):
    bell = jnp.exp(hidden * hidden * -0.5)
    size = jnp.abs(hidden)
    turn = pl.reciprocal(1.0 + 0.3275911 * 0.7071067811865476 * size)
    poly = turn * (
        0.5 * 0.254829592
        + turn
        * (
            0.5 * -0.284496736
            + turn * (0.5 * 1.421413741 + turn * (0.5 * -1.453152027 + turn * (0.5 * 1.061405429)))
        )
    )
    tail = poly * bell
    below = jnp.where(hidden >= 0, 1.0 - tail, tail)
    return hidden * below, below + hidden * (0.3989422804014327 * bell)


def mlp_kernel(
    img_ref, entry_ref, pull_ref, expand_ref, bias_ref, reduce_ref, reduce_far_ref,
    result_ref, back_ref, dreduce_ref, dexpand_far_ref, dexpand_ref, dbias_ref, turned_ref,
):
    step = pl.program_id(0)
    first_half = step < pl.num_programs(0) // 2

    @pl.when(step == 0)
    def _():
        result_ref[...] = jnp.zeros_like(result_ref)
        back_ref[...] = jnp.zeros_like(back_ref)
        turned_ref[...] = entry_ref[...].T

    expand = expand_ref[...]
    reduce = jnp.where(first_half, reduce_far_ref[...], reduce_ref[...])
    pull = pull_ref[...]
    hidden = dot_n(entry_ref[...], expand) + bias_ref[...]
    active, slope = gelu_parts(hidden)
    active = active.astype(BF)
    grad = (dot_t(pull, reduce) * slope).astype(BF)
    result_ref[...] += dot_n(active, reduce)
    back_ref[...] += dot_t(grad, expand)
    half = dexpand_ref.shape[0]
    here = pl.ds(pl.multiple_of(img_ref[0] * half, half), half)
    there = pl.ds(pl.multiple_of((1 - img_ref[0]) * half, half), half)
    dexpand_far_ref[...] = dot_n(turned_ref[there, :], grad).astype(BF)
    dexpand_ref[...] = dot_n(turned_ref[here, :], grad).astype(BF)
    dbias_ref[...] = jnp.sum(grad.astype(F32), axis=0, keepdims=True)
    dreduce_ref[...] = dot_f(active, pull).astype(BF)


def mlp(img, entry_two, incoming, expand, bias, reduce, reduce_far, *earlier, chunk=768):
    width = entry_two.shape[1]
    hidden = bias.shape[1]
    tokens = entry_two.shape[0]
    steps = hidden // chunk
    half = steps // 2

    def place(step, img):
        return (step + (1 - img[0]) * half) % steps

    def fixed(rows, columns):
        return pl.BlockSpec((rows, columns), lambda step, img: (0, 0))

    def across(rows):
        return pl.BlockSpec((rows, chunk), lambda step, img: (0, place(step, img)))

    return pl.pallas_call(
        ordered(mlp_kernel, 7, earlier),
        grid_spec=pltpu.PrefetchScalarGridSpec(
            num_scalar_prefetch=1,
            grid=(steps,),
            in_specs=[
                fixed(tokens, width), fixed(tokens, width), across(width), across(1),
                pl.BlockSpec((chunk, width), lambda step, img: (jnp.maximum(step - half, 0), 0)),
                pl.BlockSpec((chunk, width), lambda step, img: (jnp.minimum(step, half - 1), 0)),
            ] + [ANY] * len(earlier),
            out_specs=[
                fixed(tokens, width), fixed(tokens, width),
                pl.BlockSpec((chunk, width), lambda step, img: (place(step, img), 0)),
                across(width // 2), across(width // 2), across(1),
            ],
            scratch_shapes=[pltpu.VMEM((width, tokens), BF)],
        ),
        out_shape=[
            jax.ShapeDtypeStruct((tokens, width), F32),
            jax.ShapeDtypeStruct((tokens, width), F32),
            jax.ShapeDtypeStruct((hidden, width), BF),
            jax.ShapeDtypeStruct((width // 2, hidden), BF),
            jax.ShapeDtypeStruct((width // 2, hidden), BF),
            jax.ShapeDtypeStruct((1, hidden), F32),
        ],
        compiler_params=pltpu.CompilerParams(vmem_limit_bytes=VMEM_LIMIT),
        cost_estimate=cost(29),
        name="mlp",
    )(img.reshape(1), entry_two, incoming, expand, bias, reduce, reduce_far, *earlier)


def project_kernel(img_ref, x_ref, mask_ref, rows_ref, near_ref, far_ref, bias_ref, entry_ref, joint_ref):
    @pl.when(pl.program_id(0) == 0)
    def _():
        value = x_ref[...].astype(F32)
        centred = value - jnp.mean(value, axis=1, keepdims=True)
        variance = jnp.mean(centred * centred, axis=1, keepdims=True)
        normed = centred * lax.rsqrt(variance + 1e-06) * rows_ref[0:1] + rows_ref[1:2]
        entry_ref[...] = (mask_ref[...] * normed).astype(BF)

    low = img_ref[0] == 0
    near, far = near_ref[...], far_ref[...]
    weight = jnp.concatenate([jnp.where(low, near, far), jnp.where(low, far, near)], 0)
    joint_ref[...] = (dot_n(entry_ref[...], weight) + bias_ref[...]).astype(BF)


def project(img, x, mask, rows, near, far, bias, *earlier, chunk=768):
    tokens, width = x.shape
    total = bias.shape[1]

    def across(rows):
        return pl.BlockSpec((rows, chunk), lambda step: (0, step))

    return pl.pallas_call(
        ordered(project_kernel, 7, earlier),
        grid=(total // chunk,),
        in_specs=[
            pl.BlockSpec(memory_space=pltpu.SMEM), whole((tokens, width)), whole((tokens, 1)),
            whole((8, width)), across(width // 2), across(width // 2), across(1),
        ] + [ANY] * len(earlier),
        out_specs=[whole((tokens, width)), across(tokens)],
        out_shape=[
            jax.ShapeDtypeStruct((tokens, width), BF), jax.ShapeDtypeStruct((tokens, total), BF),
        ],
        compiler_params=pltpu.CompilerParams(vmem_limit_bytes=VMEM_LIMIT),
        cost_estimate=cost(7),
        name="project",
    )(img.reshape(1), x, mask, rows, near, far, bias, *earlier)


def project_back_kernel(
    img_ref, x_ref, mask_ref, rows_ref, middle_ref, pull_ref, near_ref, far_ref,
    grad_ref, sums_ref, weight_ref, entry_ref,
):
    img = img_ref[0]
    half = near_ref.shape[0]
    pairs = HEADS // 2
    here = pl.ds(pl.multiple_of(img * half, half), half)
    there = pl.ds(pl.multiple_of((1 - img) * half, half), half)
    for pair in range(pairs):
        for part in range(3):
            source = slice((part * pairs + pair) * 128, (part * pairs + pair + 1) * 128)
            target = slice((pair * 3 + part) * 128, (pair * 3 + part + 1) * 128)
            weight_ref[here, target] = near_ref[:, source]
            weight_ref[there, target] = far_ref[:, source]
    entry_ref[...] = dot_t(pull_ref[...], weight_ref[...])
    gain = rows_ref[0:1]
    width = x_ref.shape[1]

    def step(number, carry):
        spot = pl.ds(number * 48, 48)
        first, second = carry
        grad = entry_ref[spot, :] * mask_ref[spot, :]
        value = x_ref[spot, :].astype(F32)
        centred = value - jnp.mean(value, axis=1, keepdims=True)
        variance = jnp.mean(centred * centred, axis=1, keepdims=True)
        rstd = lax.rsqrt(variance + 1e-06)
        xhat = centred * rstd
        product = grad * xhat
        pull = grad * gain
        back = pull - jnp.mean(pull, axis=1, keepdims=True)
        back = back - xhat * jnp.mean(pull * xhat, axis=1, keepdims=True)
        grad_ref[spot, :] = (middle_ref[spot, :] + rstd * back).astype(BF)
        return first + jnp.sum(product.reshape(-1, 8, width), axis=0), second + jnp.sum(grad.reshape(-1, 8, width), axis=0)

    none = jnp.zeros((8, width), F32)
    carry = (none, none)
    for number in range(TOKENS // 48):
        carry = step(number, carry)
    first, second = carry
    sums_ref[0:1] = jnp.sum(first, axis=0, keepdims=True)
    sums_ref[1:2] = jnp.sum(second, axis=0, keepdims=True)


def project_back(img, x, mask, rows, grad_middle, grad_joint, near, far, *earlier):
    tokens, width = x.shape
    total = grad_joint.shape[1]
    full = whole((tokens, width))
    weight = whole((width // 2, total))
    return pl.pallas_call(
        ordered(project_back_kernel, 8, earlier),
        grid=(1,),
        in_specs=[
            pl.BlockSpec(memory_space=pltpu.SMEM), full, whole((tokens, 1)), whole((8, width)), full,
            whole((tokens, total)), weight, weight,
        ] + [ANY] * len(earlier),
        out_specs=[full, whole((2, width))],
        out_shape=[jax.ShapeDtypeStruct((tokens, width), BF), jax.ShapeDtypeStruct((2, width), F32)],
        scratch_shapes=[pltpu.VMEM((width, total), BF), pltpu.VMEM((tokens, width), F32)],
        compiler_params=pltpu.CompilerParams(vmem_limit_bytes=VMEM_LIMIT),
        cost_estimate=cost(11),
        name="project_back",
    )(img.reshape(1), x, mask, rows, grad_middle, grad_joint, near, far, *earlier)


def mix_kernel(mixed_ref, weight_ref, rows_ref, x_ref, mask_ref, middle_ref, entry_ref):
    branch = dot_n(mixed_ref[...], weight_ref[...]) + rows_ref[2:3]
    middle = x_ref[...].astype(F32) + mask_ref[...] * branch
    middle_ref[...] = middle
    centred = middle - jnp.mean(middle, axis=1, keepdims=True)
    variance = jnp.mean(centred * centred, axis=1, keepdims=True)
    normed = centred * lax.rsqrt(variance + 1e-06) * rows_ref[4:5] + rows_ref[5:6]
    entry_ref[...] = normed.astype(BF)


def last_columns(array, width):
    place = array.shape[1] // width - 1
    return pl.BlockSpec((array.shape[0], width), lambda step: (0, place))


def mix(mixed, weights, rows, x, mask, *earlier):
    tokens, width = x.shape
    return pl.pallas_call(
        ordered(mix_kernel, 5, earlier),
        grid=(1,),
        in_specs=[
            whole((tokens, width)), last_columns(weights, width), whole(rows.shape), whole((tokens, width)),
            whole(mask.shape),
        ] + [ANY] * len(earlier),
        out_specs=[whole((tokens, width))] * 2,
        out_shape=[jax.ShapeDtypeStruct(x.shape, F32), jax.ShapeDtypeStruct(x.shape, BF)],
        compiler_params=pltpu.CompilerParams(vmem_limit_bytes=VMEM_LIMIT),
        cost_estimate=cost(4.6),
        name="mix",
    )(mixed, weights, rows, x, mask, *earlier)


def mix_back_kernel(
    img_ref, back_ref, result_ref, middle_ref, incoming_ref, mask_ref, rows_ref, weight_ref, mixed_ref,
    grad_middle_ref, grad_mixed_ref, give_ref, keep_ref, out_ref, sums_ref,
):
    low = img_ref[0] == 0
    mask = mask_ref[...]
    middle = middle_ref[...]
    incoming = incoming_ref[...].astype(F32)
    out_ref[...] = (mask * (middle + (result_ref[...] + rows_ref[3:4]))).astype(BF)
    back = back_ref[...]
    centred = middle - jnp.mean(middle, axis=1, keepdims=True)
    variance = jnp.mean(centred * centred, axis=1, keepdims=True)
    rstd = lax.rsqrt(variance + 1e-06)
    xhat = centred * rstd
    sums_ref[1:2] = jnp.sum(back * xhat, axis=0, keepdims=True)
    sums_ref[2:3] = jnp.sum(back, axis=0, keepdims=True)
    sums_ref[3:4] = jnp.sum(incoming, axis=0, keepdims=True)
    pull = back * rows_ref[4:5]
    inner = pull - jnp.mean(pull, axis=1, keepdims=True)
    inner = inner - xhat * jnp.mean(pull * xhat, axis=1, keepdims=True)
    grad_middle = incoming + rstd * inner
    grad_middle_ref[...] = grad_middle
    branch = (mask * grad_middle).astype(BF)
    sums_ref[0:1] = jnp.sum(branch.astype(F32), axis=0, keepdims=True)
    grad_mixed_ref[...] = dot_t(branch, weight_ref[...]).astype(BF)
    half = keep_ref.shape[0]
    total = dot_f(mixed_ref[...], branch)
    give_ref[...] = jnp.where(low, total[half:], total[:half]).astype(BF)
    keep_ref[...] = jnp.where(low, total[:half], total[half:]).astype(BF)


def mix_back(img, back, result, middle, incoming, mask, rows, weights, mixed, *earlier):
    tokens, width = middle.shape
    half = (width // 2, width)
    full = whole((tokens, width))
    return pl.pallas_call(
        ordered(mix_back_kernel, 9, earlier),
        grid=(1,),
        in_specs=[
            pl.BlockSpec(memory_space=pltpu.SMEM), full, full, full, full, whole(mask.shape),
            whole(rows.shape), last_columns(weights, width), full,
        ] + [ANY] * len(earlier),
        out_specs=[full, full, whole(half), whole(half), full, whole((4, width))],
        out_shape=[
            jax.ShapeDtypeStruct((tokens, width), F32), jax.ShapeDtypeStruct((tokens, width), BF),
            jax.ShapeDtypeStruct(half, BF), jax.ShapeDtypeStruct(half, BF),
            jax.ShapeDtypeStruct((tokens, width), BF), jax.ShapeDtypeStruct((4, width), F32),
        ],
        compiler_params=pltpu.CompilerParams(vmem_limit_bytes=VMEM_LIMIT),
        cost_estimate=cost(7),
        name="mix_back",
    )(img.reshape(1), back, result, middle, incoming, mask, rows, weights, mixed, *earlier)


def entry_grads_kernel(img_ref, entry_ref, grad_ref, give_ref, keep_ref, turned_ref):
    @pl.when(pl.program_id(0) == 0)
    def _():
        turned_ref[...] = entry_ref[...].T

    half = keep_ref.shape[0]
    img = img_ref[0]
    grad = grad_ref[...]
    here = pl.ds(pl.multiple_of(img * half, half), half)
    there = pl.ds(pl.multiple_of((1 - img) * half, half), half)
    give_ref[...] = dot_n(turned_ref[there, :], grad).astype(BF)
    keep_ref[...] = dot_n(turned_ref[here, :], grad).astype(BF)


def entry_grads(img, entry, grad, *earlier, chunk=768):
    tokens, width = entry.shape
    total = grad.shape[1]

    def across(rows):
        return pl.BlockSpec((rows, chunk), lambda step: (0, step))

    return pl.pallas_call(
        ordered(entry_grads_kernel, 3, earlier),
        grid=(total // chunk,),
        in_specs=[pl.BlockSpec(memory_space=pltpu.SMEM), whole((tokens, width)), across(tokens)]
        + [ANY] * len(earlier),
        out_specs=[across(width // 2), across(width // 2)],
        out_shape=[
            jax.ShapeDtypeStruct((width // 2, total), BF), jax.ShapeDtypeStruct((width // 2, total), BF),
        ],
        scratch_shapes=[pltpu.VMEM((width, tokens), BF)],
        compiler_params=pltpu.CompilerParams(vmem_limit_bytes=VMEM_LIMIT),
        cost_estimate=cost(5),
        name="entry_grads",
    )(img.reshape(1), entry, grad, *earlier)


def sums_kernel(
    block, img_ref, norm_ref, joint_ref, mix_ref, expand_ref, tables_ref, give_ref, keep_ref, table_ref, turned_ref,
):
    width = norm_ref.shape[1]
    number = width // block
    joint = jnp.concatenate([joint_ref[0:1], joint_ref[1:2]], 1)

    def picked(line, count):
        return [
            jnp.concatenate(
                [
                    line[:, (count * owner + place) * block : (count * owner + place + 1) * block]
                    for owner in range(number)
                ],
                1,
            )
            for place in range(count)
        ]

    rows = [norm_ref[...], mix_ref[...]] + picked(joint, 2) + picked(expand_ref[...], 4)
    rows.append(jnp.zeros((128 - 12, width), F32))
    turned_ref[...] = jnp.concatenate(rows, 0).T
    half = give_ref.shape[0]
    img = img_ref[0]
    give_ref[...] = turned_ref[pl.ds(pl.multiple_of((1 - img) * half, half), half), :].astype(BF)
    keep_ref[...] = turned_ref[pl.ds(pl.multiple_of(img * half, half), half), :].astype(BF)
    total = tables_ref[0]
    for pair in range(1, tables_ref.shape[0]):
        total = total + tables_ref[pair]
    height = total[0:32, :64] + total[32:64, 64:]
    across = total[64:96, :64] + total[96:128, 64:]
    both = jnp.concatenate([height, across], 1)
    table_ref[...] = jnp.zeros_like(table_ref)
    for place in range(table_ref.shape[1] // 128):
        part = both[place * block : min((place + 1) * block, 32)]
        table_ref[: part.shape[0], place * 128 : (place + 1) * 128] = part.astype(BF)


def sums(img, norm, joint, mixed, expand, tables, block, *earlier):
    vmem = pl.BlockSpec(memory_space=pltpu.VMEM)
    width = norm.shape[1]
    shapes = [(width // 2, 128), (width // 2, 128), (block, -(-32 // block) * 128)]
    return pl.pallas_call(
        ordered(partial(sums_kernel, block), 6, earlier),
        in_specs=[pl.BlockSpec(memory_space=pltpu.SMEM)] + [vmem] * 5 + [ANY] * len(earlier),
        out_specs=[vmem] * 3,
        out_shape=[jax.ShapeDtypeStruct(shape, BF) for shape in shapes],
        scratch_shapes=[pltpu.VMEM((width, 128), F32)],
        compiler_params=pltpu.CompilerParams(vmem_limit_bytes=VMEM_LIMIT),
        cost_estimate=cost(0.3),
        name="sums",
    )(img.reshape(1), norm, joint, mixed, expand, tables, *earlier)


def place_kernel(depth, slots, place_ref, ready_ref, *refs):
    parts = refs[:depth]
    wide_ref, triple_ref, height_ref, width_ref = refs[depth : depth + 4]
    vector_refs = refs[depth + 4 :]
    wide_ref[...] = ready_ref[...].astype(F32)
    block = triple_ref.shape[0]
    pairs = HEADS // 2
    width = pairs * 128

    def total(lanes):
        value = parts[0][:, lanes]
        for part in parts[1:]:
            value = value + part[:, lanes].astype(F32)
        return value

    for pair in range(pairs):
        for part in range(3):
            begin, spot = (pair * 3 + part) * 128, (part * pairs + pair) * 128
            triple_ref[:, spot : spot + 128] = total(slice(begin, begin + 128))
    columns = total(slice(3 * width, 3 * width + 128))
    columns = jnp.concatenate([columns, jnp.zeros((128 - block, 128), F32)], 0).T
    begin = 0
    for out_ref in vector_refs:
        count = out_ref.shape[1] // block
        out_ref[...] = jnp.concatenate(
            [columns[begin + row : begin + row + 1, :block] for row in range(count)], 1
        )
        begin += count
    lanes = slice(3 * width + 128, None)
    tables = None
    for level in range(depth):
        found = parts[0][:, lanes]
        for step in range(1, depth):
            found = jnp.where((place_ref[2] ^ step) == level, parts[step][:, lanes].astype(F32), found)
        tables = found if tables is None else tables + found
    for slot in range(slots):
        spot = slots - 1 - slot
        first = spot // block * 128
        line = tables[spot % block : spot % block + 1, first : first + 128]
        height_ref[slot : slot + 1] = line[:, :64]
        width_ref[slot : slot + 1] = line[:, 64:]


def place(bits, ready, parts, slots, *earlier):
    vmem = pl.BlockSpec(memory_space=pltpu.VMEM)
    block = parts[0].shape[0]
    width = HEADS * HEAD_DIM
    shapes = [ready.shape, (block, 3 * width)] + [(slots, HEAD_DIM)] * 2
    shapes += [(1, block)] * 6 + [(1, 2 * block), (1, 4 * block)]
    return pl.pallas_call(
        ordered(partial(place_kernel, len(parts), slots), 2 + len(parts), earlier),
        in_specs=[pl.BlockSpec(memory_space=pltpu.SMEM)] + [vmem] * (1 + len(parts)) + [ANY] * len(earlier),
        out_specs=[vmem] * len(shapes),
        out_shape=[jax.ShapeDtypeStruct(shape, F32) for shape in shapes],
        compiler_params=pltpu.CompilerParams(vmem_limit_bytes=VMEM_LIMIT),
        cost_estimate=cost(1.9),
        name="place",
    )(bits, ready, *parts, *earlier)


def settle_kernel(cut, *refs):
    parts, (left_ref, right_ref) = refs[:-2], refs[-2:]
    for out_ref, lanes in ((left_ref, slice(0, cut)), (right_ref, slice(cut, None))):
        value = parts[0][:, lanes]
        for part in parts[1:]:
            value = value + part[:, lanes].astype(F32)
        out_ref[...] = value


def settle(parts, cut, *earlier):
    vmem = pl.BlockSpec(memory_space=pltpu.VMEM)
    rows, columns = parts[0].shape
    return pl.pallas_call(
        ordered(partial(settle_kernel, cut), len(parts), earlier),
        in_specs=[vmem] * len(parts) + [ANY] * len(earlier),
        out_specs=[vmem] * 2,
        out_shape=[
            jax.ShapeDtypeStruct((rows, cut), F32), jax.ShapeDtypeStruct((rows, columns - cut), F32),
        ],
        cost_estimate=cost(1),
        name="settle",
    )(*parts, *earlier)


def rows_place():
    me = lax.axis_index("rows")
    return me % 2, me // 2 % 2, me // 4


def swap_rows(block, bit):
    count = lax.axis_size("rows")
    return lax.ppermute(block, "rows", [(place, place ^ (1 << bit)) for place in range(count)])


def swap_img(block):
    return lax.ppermute(block, "img", [(0, 1), (1, 0)])


def swap_depth(block, step):
    count = lax.axis_size("rows")
    return lax.ppermute(block, "rows", [(place, place ^ (4 * step)) for place in range(count)])


def halves(block):
    cut = block.shape[-1] // 256 * 128
    return block[..., :cut], block[..., cut:]


def join_one_kernel(offsets, bits_ref, *refs):
    place = bits_ref[2]
    ins, (first, second) = refs[: len(offsets)], refs[-2:]
    cut = first.shape[-1]
    for offset, part_ref in zip(offsets, ins):
        part = part_ref[...]
        first[place ^ offset] = part[:, :cut]
        second[place ^ offset] = part[:, cut:]


def join_two_kernel(count, bits_ref, *refs):
    x, y = bits_ref[0], bits_ref[1]
    ins, outs = refs[: 4 * count], refs[len(refs) - 2 * count :]
    for number in range(count):
        first, first_far, second, second_far = ins[4 * number : 4 * number + 4]
        joined, joined_two = outs[2 * number : 2 * number + 2]
        for level in range(first.shape[0]):
            joined[level, x] = first[level]
            joined[level, 1 - x] = first_far[level]
            joined_two[level, y] = second[level]
            joined_two[level, 1 - y] = second_far[level]


def join_three_kernel(begin, bits_ref, first, first_far, second, second_far, *refs):
    x, y = bits_ref[0], bits_ref[1]
    joined = refs[-1]
    cut = first.shape[-1]
    rows = slice(begin, begin + joined.shape[3])
    for level in range(first.shape[0]):
        for side in range(2):
            joined[level, y, side, :, :cut] = first[level, side, rows]
            joined[level, 1 - y, side, :, :cut] = first_far[level, side, rows]
            joined[level, side, x, :, cut:] = second[level, side, rows]
            joined[level, side, 1 - x, :, cut:] = second_far[level, side, rows]


def carry_kernel(weight_ref, *refs):
    out_ref = refs[-1]
    columns = weight_ref.shape[1]
    out_ref[:, :columns] = weight_ref[...]
    pre_gain, pre_bias, triple_bias, output_bias, post_gain, post_bias, expand_bias, reduce_bias = [
        ref[...].astype(F32) for ref in refs[:8]
    ]
    lines = []
    for parts in ((pre_gain, pre_bias, triple_bias, output_bias), (expand_bias, reduce_bias), (post_gain, post_bias)):
        size = sum(part.shape[1] for part in parts)
        lines.append(jnp.concatenate(parts + (jnp.zeros((1, 128 - size), F32),), 1))
    rest = out_ref.shape[0] - len(lines)
    if rest:
        lines.append(jnp.zeros((rest, 128), F32))
    out_ref[:, columns:] = jnp.concatenate(lines, 0).astype(out_ref.dtype)


def carry(weight, vectors, *earlier):
    vmem = pl.BlockSpec(memory_space=pltpu.VMEM)
    return pl.pallas_call(
        ordered(carry_kernel, 1 + len(vectors), earlier),
        in_specs=[vmem] * (1 + len(vectors)) + [ANY] * len(earlier),
        out_specs=vmem,
        out_shape=jax.ShapeDtypeStruct((weight.shape[0], weight.shape[1] + 128), weight.dtype),
        cost_estimate=cost(2),
        name="carry",
    )(weight, *[vector.reshape(1, -1) for vector in vectors], *earlier)


def spread_kernel(block, img_ref, near_ref, far_ref, rows_ref, offsets_ref, fill_ref, expand_ref):
    low = img_ref[0] == 0
    near, far = near_ref[...].astype(F32), far_ref[...].astype(F32)
    count = near.shape[0] // block
    width = rows_ref.shape[1]
    rows_ref[6:8] = jnp.zeros((2, width), F32)
    offsets_ref[...] = jnp.zeros_like(offsets_ref)
    plan = (
        (0, 0, 1, rows_ref, 0), (0, 1, 1, rows_ref, 1), (0, 4, 1, rows_ref, 2),
        (1, 4, 1, rows_ref, 3), (2, 0, 1, rows_ref, 4), (2, 1, 1, rows_ref, 5),
        (1, 0, 4, expand_ref, 0),
    )
    for half in range(2):
        part = jnp.where(low, near, far) if half == 0 else jnp.where(low, far, near)
        for number in range(count):
            spot = half * count + number
            lines = part[number * block : number * block + 3]
            for line, first, size, out_ref, row in plan:
                size = size * block
                out_ref[row : row + 1, spot * size : (spot + 1) * size] = lines[
                    line : line + 1, first * block : first * block + size
                ]
            size = 2 * block
            begin = spot * size + (width if half else 0)
            offsets_ref[:, begin : begin + size] = lines[0:1, size : 2 * size]
    fill_ref[...] = offsets_ref[:, 2 * width :].astype(BF)


def spread(img, near, far, block, *earlier):
    width = 2 * near.shape[0]
    place = near.shape[1] // 128 - 1
    last = pl.BlockSpec((near.shape[0], 128), lambda step: (0, place))
    shapes = [((8, width), F32), ((1, 3 * width), F32), ((1, width), BF), ((1, 4 * width), F32)]
    return pl.pallas_call(
        ordered(partial(spread_kernel, block), 3, earlier),
        grid=(1,),
        in_specs=[pl.BlockSpec(memory_space=pltpu.SMEM), last, last] + [ANY] * len(earlier),
        out_specs=[whole(shape) for shape, _ in shapes],
        out_shape=[jax.ShapeDtypeStruct(shape, kind) for shape, kind in shapes],
        cost_estimate=cost(2),
        name="spread",
    )(img.reshape(1), near, far, *earlier)


def stack_kernel(*refs):
    refs[-1][...] = jnp.concatenate([ref[...].astype(F32) for ref in refs[:-1]], 0).astype(BF)


def stack(blocks, *earlier):
    vmem = pl.BlockSpec(memory_space=pltpu.VMEM)
    rows = sum(block.shape[0] for block in blocks)
    return pl.pallas_call(
        ordered(stack_kernel, len(blocks), earlier),
        in_specs=[vmem] * len(blocks) + [ANY] * len(earlier),
        out_specs=vmem,
        out_shape=jax.ShapeDtypeStruct((rows,) + blocks[0].shape[1:], BF),
        cost_estimate=cost(1.6),
        name="stack",
    )(*blocks, *earlier)


class Gather:
    def __init__(self, block):
        self.depth = lax.axis_size("rows") // 4
        self.bits = jnp.stack(rows_place()).astype(jnp.int32)
        self.rows, self.columns = block.shape
        self.cut = self.columns // 256 * 128
        self.held = [block]

    def call(self, kernel, name, values, shapes, earlier):
        vmem = pl.BlockSpec(memory_space=pltpu.VMEM)
        return pl.pallas_call(
            kernel,
            in_specs=[pl.BlockSpec(memory_space=pltpu.SMEM)] + [vmem] * len(values) + [ANY] * len(earlier),
            out_specs=[vmem] * len(shapes),
            out_shape=[jax.ShapeDtypeStruct(shape, BF) for shape in shapes],
            compiler_params=pltpu.CompilerParams(vmem_limit_bytes=VMEM_LIMIT),
            cost_estimate=cost(2.3),
            name=name,
        )(self.bits, *values, *earlier)

    def shapes(self, *lead):
        return [lead + (self.rows, self.cut), lead + (self.rows, self.columns - self.cut)]

    def shift(self):
        held = [(0, self.held[0])]
        bit = self.depth // 2
        while bit:
            held += [(offset ^ bit, swap_depth(block, bit)) for offset, block in held]
            bit //= 2
        self.offsets = [offset for offset, _ in held]
        self.far = [block for _, block in held[1:]]

    def join_one(self, *earlier):
        kernel = partial(join_one_kernel, self.offsets)
        self.held = self.call(kernel, "join_one", self.held + self.far, self.shapes(self.depth), earlier)
        return self.held

    def swap_near(self):
        self.far = [swap_rows(part, number) for number, part in enumerate(self.held)]

    def swap_far(self):
        self.far = [swap_rows(part, 1 - number) for number, part in enumerate(self.held)]

    def pairs(self):
        return [array for pair in zip(self.held, self.far) for array in pair]

    def join_two(self, *earlier):
        kernel = partial(join_two_kernel, 1)
        self.held = self.call(kernel, "join_two", self.pairs(), self.shapes(self.depth, 2), earlier)
        return self.held

    def join_three(self, begin, rows, *earlier):
        shapes = [(self.depth, 2, 2, rows, self.columns)]
        kernel = partial(join_three_kernel, begin)
        return self.call(kernel, "join_three", self.pairs(), shapes, earlier)[0].reshape(-1, self.columns)


def fold_one_kernel(count, ride, bits_ref, *refs):
    ins = refs[: 2 * count]
    a_give, a_keep, b_give, b_keep = refs[-4 - bool(ride) :][:4]
    x, y = bits_ref[0], bits_ref[1]
    cut = a_keep.shape[-1]
    begin = 0
    for near_ref, far_ref in zip(ins[:count], ins[count:]):
        columns = near_ref.shape[-1]
        pieces = [(max(begin, 0), min(begin + columns, cut), True), (max(begin, cut), begin + columns, False)]
        for low, high, first in pieces:
            if low >= high:
                continue
            here = slice(low - begin, high - begin)
            there = slice(low, high) if first else slice(low - cut, high - cut)
            for level in range(near_ref.shape[0]):
                for side in range(2):
                    if first:
                        kept, given = (level, side, x), (level, side, 1 - x)
                    else:
                        kept, given = (level, y, side), (level, 1 - y, side)
                    keep, give = (a_keep, a_give) if first else (b_keep, b_give)
                    value = near_ref[kept + (slice(None), here)].astype(F32) + far_ref[kept + (slice(None), here)].astype(F32)
                    keep[level, side, :, there] = value
                    value = near_ref[given + (slice(None), here)].astype(F32) + far_ref[given + (slice(None), here)].astype(F32)
                    give[level, side, :, there] = value.astype(BF)
        begin += columns
    if ride:
        near, far = refs[2 * count : 2 * count + 2]
        table = (near[...].astype(F32) + far[...].astype(F32)).astype(BF)
        refs[-1][...] = table
        a_give[:, :, :, cut:] = jnp.zeros(a_give.shape[:3] + (ride,), BF)
        a_give[0, 0, :, cut:] = table


def fold_two_kernel(ride, bits_ref, a_near, a_far, b_near, b_far, *refs):
    a_give, a_keep, b_give, b_keep = refs[-4 - bool(ride) :][:4]
    x, y = bits_ref[0], bits_ref[1]
    cut = a_keep.shape[-1]
    for level in range(a_near.shape[0]):
        a_keep[level] = a_near[level, y] + a_far[level, y, :, :cut].astype(F32)
        a_give[level, :, :cut] = (a_near[level, 1 - y] + a_far[level, 1 - y, :, :cut].astype(F32)).astype(BF)
        b_keep[level] = b_near[level, x] + b_far[level, x].astype(F32)
        b_give[level] = (b_near[level, 1 - x] + b_far[level, 1 - x].astype(F32)).astype(BF)
    if ride:
        table = (refs[0][...].astype(F32) + a_far[0, 0, :, cut:].astype(F32)).astype(BF)
        refs[-1][...] = table
        a_give[:, :, cut:] = jnp.zeros(a_give.shape[:2] + (ride,), BF)
        a_give[0, :, cut:] = table


def fold_three_kernel(depth, ride, bits_ref, a_near, a_far, b_near, b_far, *refs):
    place = bits_ref[2]
    keep, gives = refs[-depth], refs[len(refs) - depth + 1 :]
    cut = a_near.shape[-1]
    columns = cut + b_near.shape[-1]
    for step, out in enumerate((keep,) + tuple(gives)):
        spot = place ^ step
        out[:, :cut] = (a_near[spot] + a_far[spot, :, :cut].astype(F32)).astype(out.dtype)
        out[:, cut:columns] = (b_near[spot] + b_far[spot].astype(F32)).astype(out.dtype)
        if ride:
            table = (refs[0][...].astype(F32) + a_far[0, :, cut:].astype(F32)).astype(BF)
            out[:, columns:] = table.astype(out.dtype)


def fold_call(kernel, name, bits, values, outs, earlier, estimate):
    vmem = pl.BlockSpec(memory_space=pltpu.VMEM)
    return pl.pallas_call(
        kernel,
        in_specs=[pl.BlockSpec(memory_space=pltpu.SMEM)] + [vmem] * len(values)
        + [pl.BlockSpec(memory_space=pl.ANY)] * len(earlier),
        out_specs=[vmem] * len(outs),
        out_shape=[jax.ShapeDtypeStruct(shape, kind) for shape, kind in outs],
        compiler_params=pltpu.CompilerParams(vmem_limit_bytes=VMEM_LIMIT),
        cost_estimate=cost(estimate),
        name=name,
    )(bits, *values, *earlier)


class Scatter:
    def __init__(self, give, keep, costs, table=None):
        self.costs = costs
        self.depth = lax.axis_size("rows") // 4
        self.columns = sum(part.shape[-1] for part in keep)
        self.cut = self.columns // 256 * 128
        self.bits = jnp.stack(rows_place()).astype(jnp.int32)
        self.rows = keep[0].shape[0] // lax.axis_size("rows")
        self.give, self.keep = list(give), list(keep)
        self.table = table
        self.ride = table.shape[1] if table is not None else 0

    def swap_near(self):
        self.far = [swap_img(part) for part in self.give]

    def outs(self, *lead):
        first, second = lead + (self.rows, self.cut), lead + (self.rows, self.columns - self.cut)
        shapes = [(lead + (self.rows, self.cut + self.ride), BF), (first, F32), (second, BF), (second, F32)]
        if self.ride:
            shapes.append(((self.rows, self.ride), BF))
        return shapes

    def fold_one(self, *earlier):
        shape = (self.depth, 2, 2, self.rows, -1)
        values = [part.reshape(shape) for part in self.keep + self.far]
        if self.ride:
            values += [self.table, swap_img(self.table)]
        kernel = partial(fold_one_kernel, len(self.keep), self.ride)
        self.out = fold_call(
            kernel, "fold_one", self.bits, values, self.outs(self.depth, 2), earlier, self.costs[0]
        )
        return self.out

    def swap_middle(self):
        self.far = swap_rows(self.out[0], 0), swap_rows(self.out[2], 1)
        return self.far

    def fold_two(self, *earlier):
        values = [self.out[1], self.far[0], self.out[3], self.far[1]] + list(self.out[4:])
        kernel = partial(fold_two_kernel, self.ride)
        self.out = fold_call(
            kernel, "fold_two", self.bits, values, self.outs(self.depth), earlier, self.costs[1]
        )
        return self.out

    def swap_far(self):
        self.far = swap_rows(self.out[0], 1), swap_rows(self.out[2], 0)
        return self.far

    def fold_three(self, *earlier):
        block = (self.rows, self.columns + self.ride)
        values = [self.out[1], self.far[0], self.out[3], self.far[1]] + list(self.out[4:])
        outs = [(block, F32)] + [(block, BF)] * (self.depth - 1)
        kernel = partial(fold_three_kernel, self.depth, self.ride)
        self.out = fold_call(kernel, "fold_three", self.bits, values, outs, earlier, self.costs[2])
        return self.out

    def swap_last(self):
        return [self.out[0]] + [swap_depth(self.out[step], step) for step in range(1, self.depth)]

    def last(self):
        parts = self.swap_last()
        return sum((part.astype(F32) for part in parts[1:]), parts[0])


def to_odd(block):
    count = lax.axis_size("rows")
    return lax.ppermute(block, "rows", [(place, place + 1) for place in range(0, count, 2)])


def to_even(block):
    count = lax.axis_size("rows")
    return lax.ppermute(block, "rows", [(place + 1, place) for place in range(0, count, 2)])


def local(
    tokens,
    extent,
    pre_gain,
    pre_bias,
    triple_weight,
    triple_bias,
    height_table,
    width_table,
    output_weight,
    output_bias,
    post_gain,
    post_bias,
    expand_weight,
    expand_bias,
    reduce_weight,
    reduce_bias,
    cotangent,
):
    rows_dev, _, width = tokens.shape
    moved = rows_dev - WIN
    block = pre_gain.shape[0]
    parity = lax.axis_index("rows") % 2
    image = lax.axis_index("img") * (lax.axis_size("rows") // 2) + lax.axis_index("rows") // 2
    sides = lax.dynamic_slice(extent, (image, 0), (1, 2))

    img = lax.axis_index("img")
    last = []

    def then(result):
        arrays = result if isinstance(result, (list, tuple)) else [result]
        last[:] = [min(arrays, key=lambda array: array.size)]
        return result

    band_row, column_of = jnp.asarray(BAND_ROW), jnp.asarray(COLUMN)
    real_row = jnp.where(parity == 0, band_row, band_row + WIN)
    inside = (real_row < sides[0, 0]) & (column_of < sides[0, 1]) & (jnp.asarray(VALID) == 1)
    inside = inside & ((parity == 1) | (band_row < WIN))
    mask = inside.astype(F32)[:, None]
    table = reversed_table(height_table, width_table)
    vectors = (
        pre_gain, pre_bias, triple_bias, output_bias, post_gain, post_bias, expand_bias, reduce_bias,
    )

    far_rows = to_odd(jnp.concatenate([tokens[WIN:, :REAL], cotangent[WIN:, :REAL]]))
    later_all = lax.all_gather(
        jnp.concatenate([expand_weight, output_weight], 1), ("img", "rows"), axis=0, tiled=True
    )
    one = Gather(then(carry(triple_weight, vectors)))
    one.shift()
    two = Gather(then(stack([reduce_weight], *last)))
    then(one.join_one(*last))
    one.swap_near()
    two.shift()
    x = then(pack(parity, tokens, far_rows, mask, 0, *last))
    then(one.join_two(*last, *two.far[:-1]))
    one.swap_far()
    incoming = then(pack(parity, cotangent, far_rows, mask, moved, *last))
    triple_near = then(one.join_three(0, block, *last, two.far[-1]))
    triple_pair = triple_near, swap_img(triple_near)
    then(two.join_one(*last))
    two.swap_near()
    rows, offsets, fill, hidden_bias = then(spread(img, *triple_pair, block, *last))
    entry, joint = then(project(img, x, mask, rows, *triple_pair, offsets, *last))
    then(two.join_two(*last))
    two.swap_far()
    mixed, lse, features = then(attend(joint, fill, table, 0, HEADS // 2, (), *last))
    reduce_near = then(two.join_three(0, reduce_weight.shape[0], *last))
    reduce_pair = reduce_near, swap_img(reduce_near)
    middle, entry_two = then(mix(mixed, later_all, rows, x, mask, *last))

    result, grad_entry_two, reduce_grad, expand_far, expand_near, hidden_sums = then(
        mlp(img, entry_two, incoming, later_all, hidden_bias, *reduce_pair, *last)
    )
    reduce_part = lax.psum_scatter(reduce_grad, ("img", "rows"), scatter_dimension=0, tiled=True)
    grad_middle, grad_mixed, output_far, output_near, out_win, mix_sums = then(
        mix_back(img, grad_entry_two, result, middle, incoming, mask, rows, later_all, mixed, *last)
    )
    first_sum = Scatter([expand_far, output_far], [expand_near, output_near], (2.3, 2.3, 1.5))
    first_sum.swap_near()
    then(first_sum.fold_one(*last))
    first_sum.swap_middle()
    out_rows = to_even(then(send_rows(out_win, moved, *last)))
    grad_joint, tables, joint_sums = then(
        attend_back(joint, grad_mixed, lse, features, fill, table, 0, HEADS // 2, *last)
    )
    joint_far, joint_near = then(entry_grads(img, entry, grad_joint, *last))
    then(first_sum.fold_two(*last))
    first_sum.swap_far()
    grad_win, norm_sums = then(
        project_back(img, x, mask, rows, grad_middle, grad_joint, *triple_pair, *last)
    )
    vectors_far, vectors_near, table_sums = then(
        sums(img, norm_sums, joint_sums, mix_sums, hidden_sums, tables, block, *last)
    )
    last_sum = Scatter([joint_far, vectors_far], [joint_near, vectors_near], (0.3, 2.3, 1.5), table_sums)
    last_sum.swap_near()
    then(last_sum.fold_one(*last, out_rows))
    last_sum.swap_middle()
    then(first_sum.fold_three(*last))
    first_parts = first_sum.swap_last()
    block_output = then(unpack(parity, out_win, out_rows, tokens.shape, *last))
    grad_rows = to_even(then(send_rows(grad_win, moved, *last, *first_parts[1:2])))
    then(last_sum.fold_two(*last))
    last_sum.swap_far()
    expand_shard, output_shard = then(settle(first_parts, expand_far.shape[1], *last))
    then(last_sum.fold_three(*last))
    last_parts = last_sum.swap_last()
    input_grad = then(unpack(parity, grad_win, grad_rows, tokens.shape, *last))
    (
        reduce_shard, triple_shard, height_grad, width_grad, pre_gain_grad, pre_bias_grad, output_bias_grad,
        post_gain_grad, post_bias_grad, reduce_bias_grad, triple_bias_grad, expand_bias_grad,
    ) = place(last_sum.bits, reduce_part, last_parts, height_table.shape[0], *last)
    return (
        block_output,
        input_grad,
        pre_gain_grad.reshape(-1),
        pre_bias_grad.reshape(-1),
        triple_shard,
        triple_bias_grad.reshape(-1),
        height_grad,
        width_grad,
        output_shard,
        output_bias_grad.reshape(-1),
        post_gain_grad.reshape(-1),
        post_bias_grad.reshape(-1),
        expand_shard,
        expand_bias_grad.reshape(-1),
        reduce_shard,
        reduce_bias_grad.reshape(-1),
    )


def solution(mesh):
    split = P(("img", "rows"))
    flat = P(("img", "rows"), None)
    grids = P(("img", "rows"), None, None)
    in_specs = (
        grids, P(), split, split, flat, split, P(), P(), flat, split, split, split, flat, split,
        flat, split, grids,
    )
    out_specs = (
        grids, grids, split, split, flat, split, P(), P(), flat, split, split, split, flat, split,
        flat, split,
    )
    return jax.shard_map(local, mesh=mesh, in_specs=in_specs, out_specs=out_specs, check_vma=False)
```

```python
from functools import partial

import jax
import jax.numpy as jnp
import numpy as np
from jax import lax
from jax.experimental import pallas as pl
from jax.experimental.pallas import tpu as pltpu
from jax.sharding import PartitionSpec as P

HEADS = 12
HEAD_DIM = 64
WIN = 14
REAL = 32
KEYS = 208
BF = jnp.bfloat16
F32 = jnp.float32
VMEM_LIMIT = 60 * 2**20


def cost(microseconds):
    return pl.CostEstimate(flops=int(microseconds * 1e9), bytes_accessed=1, transcendentals=0)


ANY = pl.BlockSpec(memory_space=pl.ANY)

SEGMENTS = []
_offset = 0
for _row, _rows in ((0, WIN), (WIN, REAL - 2 * WIN)):
    for _col, _cols in ((0, WIN), (WIN, WIN), (2 * WIN, REAL - 2 * WIN)):
        _padded = -(-_rows * _cols // 16) * 16
        SEGMENTS.append((_row, _rows, _col, _cols, _padded, _offset))
        _offset += _padded
TOKENS = _offset
BAND = REAL - WIN


def ordered(kernel, count, earlier):
    def body(*refs):
        kernel(*refs[:count], *refs[count + len(earlier) :])

    return body


def window_constants():
    band_row = np.full((TOKENS,), 0, np.int32)
    column = np.full((TOKENS,), 0, np.int32)
    valid = np.zeros((TOKENS,), np.int32)
    along = np.zeros((TOKENS,), np.int32)
    across = np.zeros((TOKENS,), np.int32)
    onehots = np.zeros((len(SEGMENTS), KEYS, 128), np.float32)
    for number, (row, rows, col, cols, padded, offset) in enumerate(SEGMENTS):
        spots = [(a, b) for a in range(rows) for b in range(cols)]
        for place, (a, b) in enumerate(spots):
            band_row[offset + place] = row + a
            column[offset + place] = col + b
            valid[offset + place] = 1
            along[offset + place] = a
            across[offset + place] = b
        rest = [(s, t) for s in range(WIN) for t in range(WIN) if s >= rows or t >= cols]
        slots = spots + [None] * (padded - len(spots)) + rest
        slots = slots + [None] * (KEYS - len(slots))
        for place, spot in enumerate(slots):
            for head in range(2):
                if spot is None:
                    onehots[number, place, 32 * head + 15] = -1e30
                else:
                    for part in range(2):
                        onehots[number, place, 32 * head + 16 * part + spot[0]] = 1
                        onehots[number, place, 64 + 32 * head + 16 * part + spot[1]] = 1
    return band_row, column, valid, along, across, onehots


BAND_ROW, COLUMN, VALID, ALONG, ACROSS, ONEHOTS = window_constants()


def shift_amounts():
    amounts = np.zeros((TOKENS, 128), np.int32)
    amounts[:, :64] = (WIN - 1 - ALONG)[:, None]
    amounts[:, 64:] = (WIN - 1 - ACROSS)[:, None]
    return amounts


SHIFTS = shift_amounts()


def dot_t(left, right):
    return lax.dot_general(left, right, (((1,), (1,)), ((), ())), preferred_element_type=F32)


def dot_f(left, right):
    return lax.dot_general(left, right, (((0,), (0,)), ((), ())), preferred_element_type=F32)


def dot_n(left, right):
    return lax.dot_general(left, right, (((1,), (0,)), ((), ())), preferred_element_type=F32)


def lanes_of(shape):
    return lax.broadcasted_iota(jnp.int32, shape, len(shape) - 1)


def relative_features(queries, table, shifts):
    terms = dot_n(queries, table)
    for bit in range(4):
        rolled = pltpu.roll(terms, 128 - (1 << bit), 1)
        terms = jnp.where((shifts & (1 << bit)) != 0, rolled, terms)
    high = terms.astype(BF).astype(F32)
    low = pltpu.roll(terms - high, 16, 1)
    lane = lanes_of(terms.shape) & 31
    mixed = jnp.where(lane < WIN, high, jnp.where((lane >= 16) & (lane < 16 + WIN), low, 0.0))
    return jnp.where(lane == 15, 1.0, mixed).astype(BF)


def stacked_queries(queries, features, start, count):
    lane = lanes_of((count, 128))
    first = lane < 64
    even = (lane & 32) == 0
    part = queries[start : start + count] * jnp.asarray(0.125, BF)
    extra = features[start : start + count]
    zero = jnp.zeros_like(part)
    top = jnp.concatenate([jnp.where(first, part, zero), jnp.where(even, extra, zero)], 1)
    low = jnp.concatenate([jnp.where(first, zero, part), jnp.where(even, zero, extra)], 1)
    return jnp.concatenate([top, low], 0)


def window_keys(array, start, count, fill):
    if count == KEYS:
        return array[start : start + count]
    rest = jnp.broadcast_to(fill, (KEYS - count, 128)).astype(BF)
    return jnp.concatenate([array[start : start + count], rest], 0)


def tiles_of(total):
    return [(begin, min(128, total - begin)) for begin in range(0, total, 128)]


def lane_spots():
    spots = []
    base = 0
    for _, _, _, _, count, _ in SEGMENTS:
        spots.append((base, 2 * count))
        base += -(-2 * count // 128) * 128
    return spots


def window_sides(number, queries, features, keys, onehots_ref):
    _, _, _, _, count, start = SEGMENTS[number]
    left = stacked_queries(queries, features, start, count)
    none = jnp.zeros((1, 128), BF)
    right = jnp.concatenate([window_keys(keys, start, count, none), onehots_ref[number]], 1)
    return left, right


def attend_kernel(
    q_ref, k_ref, v_ref, fill_ref, table_ref, shifts_ref, onehots_ref,
    mixed_ref, lse_ref, features_ref, scores_ref, weights_ref,
):
    queries = q_ref[...]
    features = relative_features(queries, table_ref[...], shifts_ref[...])
    features_ref[...] = features
    keys, values = k_ref[...], v_ref[...]
    fill = fill_ref[...]
    spots = lane_spots()
    for number, (base, size) in enumerate(spots):
        left, right = window_sides(number, queries, features, keys, onehots_ref)
        scores_ref[:, base : base + size] = dot_t(right, left)
    totals = []
    for base, size in spots:
        scores = scores_ref[:, base : base + size]
        top = jnp.max(scores, axis=0, keepdims=True)
        weights = jnp.exp(scores - top)
        total = jnp.sum(weights, axis=0, keepdims=True)
        lse_ref[0, 0:1, base : base + size] = top + jnp.log(total)
        weights_ref[:, base : base + size] = weights.astype(BF)
        totals.append(1.0 / total)
    for (_, _, _, _, count, start), (base, size), scale in zip(SEGMENTS, spots, totals):
        held = window_keys(values, start, count, fill).T
        both = (dot_n(held, weights_ref[:, base : base + size]) * scale).T
        lane = lanes_of((count, 128))
        mixed = jnp.where(lane < 64, both[:count], both[count:])
        mixed_ref[start : start + count, :] = mixed.astype(BF)


LSE = sum(-(-2 * segment[4] // 128) * 128 for segment in SEGMENTS)


def attend_back_kernel(
    q_ref, k_ref, v_ref, g_ref, lse_ref, features_ref, fill_ref, table_ref, shifts_ref, onehots_ref,
    dqkv_ref, dtable_ref, dbias_ref,
    scores_ref, dprobs_ref, probs_ref, dscores_ref, back_ref, slots_ref,
):
    queries = q_ref[...]
    shifts = shifts_ref[...]
    table = table_ref[...]
    features = features_ref[...]
    keys, values, grads = k_ref[...], v_ref[...], g_ref[...]
    fill = fill_ref[...]
    spots = lane_spots()

    def stacked_pulls(start, count):
        first = lanes_of((count, 128)) < 64
        part = grads[start : start + count]
        zero = jnp.zeros_like(part)
        return jnp.concatenate([jnp.where(first, part, zero), jnp.where(first, zero, part)], 0)

    for number, (base, size) in enumerate(spots):
        _, _, _, _, count, start = SEGMENTS[number]
        left, right = window_sides(number, queries, features, keys, onehots_ref)
        scores_ref[:, base : base + size] = dot_t(right, left)
        held = window_keys(values, start, count, fill)
        dprobs_ref[:, base : base + size] = dot_t(held, stacked_pulls(start, count))
    for base, size in spots:
        lanes = slice(base, base + size)
        probs = jnp.exp(scores_ref[:, lanes] - lse_ref[0, 0:1, lanes])
        product = probs * dprobs_ref[:, lanes]
        delta = jnp.sum(product, axis=0, keepdims=True)
        probs_ref[:, lanes] = probs.astype(BF)
        dscores_ref[:, lanes] = (product - probs * delta).astype(BF)
    bias_sum = jnp.zeros((1, 128), F32)
    for number, (base, size) in enumerate(spots):
        _, _, _, _, count, start = SEGMENTS[number]
        left, right = window_sides(number, queries, features, keys, onehots_ref)
        dscores = dscores_ref[:, base : base + size]
        dvalues = dot_n(probs_ref[:, base : base + size], stacked_pulls(start, count))
        dkeys = dot_n(dscores, left[:, :128])
        dqkv_ref[start : start + count, 256:] = dvalues[:count].astype(BF)
        dqkv_ref[start : start + count, 128:256] = dkeys[:count].astype(BF)
        bias_sum = bias_sum + jnp.sum(dvalues, axis=0, keepdims=True)
        both = dot_f(dscores, right)
        lane = lanes_of((count, 128))
        back_ref[start : start + count, :128] = jnp.where(lane < 64, both[:count, :128], both[count:, :128])
        back_ref[start : start + count, 128:] = jnp.where(
            (lane & 32) == 0, both[:count, 128:], both[count:, 128:]
        )
    lane = lanes_of((TOKENS, 128)) & 31
    slots = jnp.where(lane < WIN, back_ref[:, 128:], 0.0)
    for bit in range(4):
        rolled = pltpu.roll(slots, 1 << bit, 1)
        slots = jnp.where((shifts & (1 << bit)) != 0, rolled, slots)
    high = slots.astype(BF)
    low = (slots - high.astype(F32)).astype(BF)
    slots_ref[:, :128] = high
    slots_ref[:, 128:] = low
    dq = back_ref[:, :128] * 0.125 + dot_t(slots_ref[...], jnp.concatenate([table, table], 1))
    dq = dq.astype(BF)
    dqkv_ref[:, :128] = dq
    found = dot_f(slots_ref[...], queries)
    dtable_ref[0] = found[:128] + found[128:]
    query_sum = jnp.sum(dq.astype(F32), axis=0, keepdims=True)
    dbias_ref[...] = jnp.concatenate([query_sum, bias_sum], 0)


def whole(shape):
    return pl.BlockSpec(shape, lambda step: (0,) * len(shape))


def column(offset, rows=TOKENS):
    return pl.BlockSpec((rows, 128), lambda step: (0, offset + step))


def reversed_table(height_table, width_table):
    slots = height_table.shape[0]
    pad = ((0, 0), (0, 32 - slots))
    height = jnp.pad(height_table[::-1].T, pad)
    width = jnp.pad(width_table[::-1].T, pad)
    none = jnp.zeros_like(height)
    top = jnp.concatenate([height, none, width, none], 1)
    low = jnp.concatenate([none, height, none, width], 1)
    return jnp.concatenate([top, low], 0)


def attend(joint, fill, table, begin, count, given, *earlier):
    pairs = HEADS // 2
    shapes = [
        jax.ShapeDtypeStruct((TOKENS, pairs * 128), BF),
        jax.ShapeDtypeStruct((pairs, 8, LSE), F32),
        jax.ShapeDtypeStruct((TOKENS, pairs * 128), BF),
    ]
    return pl.pallas_call(
        ordered(attend_kernel, 7, tuple(given) + earlier),
        grid=(count,),
        in_specs=[
            column(begin), column(pairs + begin), column(2 * pairs + begin), column(begin, 1),
            whole((128, 128)), whole((TOKENS, 128)), whole((len(SEGMENTS), KEYS, 128)),
        ] + [ANY] * (len(given) + len(earlier)),
        out_specs=[
            column(begin), pl.BlockSpec((1, 8, LSE), lambda step: (begin + step, 0, 0)), column(begin),
        ],
        out_shape=shapes,
        input_output_aliases={7 + place: place for place in range(len(given))},
        scratch_shapes=[pltpu.VMEM((KEYS, LSE), F32), pltpu.VMEM((KEYS, LSE), BF)],
        compiler_params=pltpu.CompilerParams(vmem_limit_bytes=VMEM_LIMIT),
        cost_estimate=cost(11),
        name="attend",
    )(joint, joint, joint, fill, table, jnp.asarray(SHIFTS), jnp.asarray(ONEHOTS, BF), *given, *earlier)


def attend_back(joint, grad_mixed, lse, features, fill, table, begin, count, *earlier):
    pairs = HEADS // 2

    def kernel(*refs):
        attend_back_kernel(*refs[:10], *refs[10 + len(earlier) :])

    return pl.pallas_call(
        kernel,
        grid=(count,),
        in_specs=[
            column(begin), column(pairs + begin), column(2 * pairs + begin), column(begin),
            pl.BlockSpec((1, 8, LSE), lambda step: (begin + step, 0, 0)), column(begin), column(begin, 1),
            whole((128, 128)), whole((TOKENS, 128)), whole((len(SEGMENTS), KEYS, 128)),
        ] + [pl.BlockSpec(memory_space=pl.ANY)] * len(earlier),
        out_specs=[
            pl.BlockSpec((TOKENS, 384), lambda step: (0, step)),
            pl.BlockSpec((1, 128, 128), lambda step: (step, 0, 0)), column(0, 2),
        ],
        out_shape=[
            jax.ShapeDtypeStruct((TOKENS, count * 384), BF),
            jax.ShapeDtypeStruct((count, 128, 128), F32),
            jax.ShapeDtypeStruct((2, count * 128), F32),
        ],
        scratch_shapes=[
            pltpu.VMEM((KEYS, LSE), F32), pltpu.VMEM((KEYS, LSE), F32),
            pltpu.VMEM((KEYS, LSE), BF), pltpu.VMEM((KEYS, LSE), BF),
            pltpu.VMEM((TOKENS, 256), F32), pltpu.VMEM((TOKENS, 256), BF),
        ],
        compiler_params=pltpu.CompilerParams(vmem_limit_bytes=VMEM_LIMIT),
        cost_estimate=cost(9),
        name="attend_back",
    )(
        joint, joint, joint, grad_mixed, lse, features, fill, table, jnp.asarray(SHIFTS), jnp.asarray(ONEHOTS, BF),
        *earlier,
    )


def tie(value, *earlier):
    def kernel(*refs):
        pass

    return pl.pallas_call(
        kernel,
        in_specs=[pl.BlockSpec(memory_space=pl.ANY)] * (1 + len(earlier)),
        out_specs=pl.BlockSpec(memory_space=pl.ANY),
        out_shape=jax.ShapeDtypeStruct(value.shape, value.dtype),
        input_output_aliases={0: 0},
        name="tie",
    )(value, *earlier)


def table_grads(found, slots):
    total = jnp.sum(found, axis=0)
    height = total[0:32, :64] + total[32:64, 64:]
    width = total[64:96, :64] + total[96:128, 64:]
    return height[:slots][::-1], width[:slots][::-1]


def pack_kernel(begin, moved, parity_ref, own_ref, far_ref, mask_ref, out_ref, stage_ref):
    parity = parity_ref[0]
    stage_ref[...] = jnp.zeros_like(stage_ref)
    for row in range(BAND):
        if row < moved:
            line = jnp.where(parity == 0, own_ref[row, :REAL], far_ref[begin + row]).astype(F32)
        else:
            line = own_ref[row - moved * parity, :REAL].astype(F32)
        for first, rows, col, cols, _, offset in SEGMENTS:
            if first <= row < first + rows:
                place = offset + (row - first) * cols
                stage_ref[place : place + cols, :] = line[col : col + cols]
    if begin:
        out_ref[...] = (stage_ref[...] * mask_ref[...]).astype(out_ref.dtype)
    else:
        out_ref[...] = stage_ref[...].astype(out_ref.dtype)


def pack(parity, own, far, mask, begin, *earlier):
    width = own.shape[2]
    vmem = pl.BlockSpec(memory_space=pltpu.VMEM)
    return pl.pallas_call(
        ordered(partial(pack_kernel, begin, far.shape[0] // 2), 4, earlier),
        in_specs=[pl.BlockSpec(memory_space=pltpu.SMEM), vmem, vmem, vmem] + [ANY] * len(earlier),
        out_specs=vmem,
        out_shape=jax.ShapeDtypeStruct((TOKENS, width), BF),
        scratch_shapes=[pltpu.VMEM((TOKENS, width), F32)],
        compiler_params=pltpu.CompilerParams(vmem_limit_bytes=VMEM_LIMIT),
        cost_estimate=cost(3),
        name="pack",
    )(parity.reshape(1), own, far, mask, *earlier)


def unpack_kernel(moved, parity_ref, win_ref, far_ref, out_ref, wide_ref, stage_ref):
    parity = parity_ref[0]
    wide_ref[...] = win_ref[...].astype(F32)
    for row in range(BAND):
        for first, rows, col, cols, _, offset in SEGMENTS:
            if first <= row < first + rows:
                place = offset + (row - first) * cols
                stage_ref[row, col : col + cols, :] = wide_ref[place : place + cols, :]
    out_ref[...] = jnp.zeros_like(out_ref)
    for row in range(out_ref.shape[0]):
        near = stage_ref[row] if row < WIN else far_ref[row - WIN].astype(F32)
        other = stage_ref[row + moved] if row + moved < BAND else jnp.zeros_like(near)
        out_ref[row, :REAL, :] = jnp.where(parity == 0, near, other).astype(out_ref.dtype)


def unpack(parity, win, far, shape, *earlier):
    width = win.shape[1]
    return pl.pallas_call(
        ordered(partial(unpack_kernel, far.shape[0]), 3, earlier),
        in_specs=[
            pl.BlockSpec(memory_space=pltpu.SMEM),
            pl.BlockSpec(memory_space=pltpu.VMEM),
            pl.BlockSpec(memory_space=pltpu.VMEM),
        ] + [ANY] * len(earlier),
        out_specs=pl.BlockSpec(memory_space=pltpu.VMEM),
        out_shape=jax.ShapeDtypeStruct(shape, BF),
        scratch_shapes=[pltpu.VMEM((TOKENS, width), F32), pltpu.VMEM((BAND, REAL, width), F32)],
        compiler_params=pltpu.CompilerParams(vmem_limit_bytes=VMEM_LIMIT),
        cost_estimate=cost(0.5),
        name="unpack",
    )(parity.reshape(1), win, far, *earlier)


def send_rows_kernel(win_ref, out_ref, wide_ref, stage_ref):
    wide_ref[...] = win_ref[...].astype(F32)
    for row in range(out_ref.shape[0]):
        for first, rows, col, cols, _, offset in SEGMENTS:
            if first <= row < first + rows:
                place = offset + (row - first) * cols
                stage_ref[row, col : col + cols, :] = wide_ref[place : place + cols, :]
    out_ref[...] = stage_ref[...].astype(out_ref.dtype)


def send_rows(win, moved, *earlier):
    width = win.shape[1]
    vmem = pl.BlockSpec(memory_space=pltpu.VMEM)
    return pl.pallas_call(
        ordered(send_rows_kernel, 1, earlier),
        in_specs=[vmem] + [ANY] * len(earlier),
        out_specs=vmem,
        out_shape=jax.ShapeDtypeStruct((moved, REAL, width), BF),
        scratch_shapes=[pltpu.VMEM((TOKENS, width), F32), pltpu.VMEM((moved, REAL, width), F32)],
        compiler_params=pltpu.CompilerParams(vmem_limit_bytes=VMEM_LIMIT),
        cost_estimate=cost(0.5),
        name="send_rows",
    )(win, *earlier)


def gelu_parts(hidden):
    bell = jnp.exp(hidden * hidden * -0.5)
    size = jnp.abs(hidden)
    turn = pl.reciprocal(1.0 + 0.3275911 * 0.7071067811865476 * size)
    poly = turn * (
        0.5 * 0.254829592
        + turn
        * (
            0.5 * -0.284496736
            + turn * (0.5 * 1.421413741 + turn * (0.5 * -1.453152027 + turn * (0.5 * 1.061405429)))
        )
    )
    tail = poly * bell
    below = jnp.where(hidden >= 0, 1.0 - tail, tail)
    return hidden * below, below + hidden * (0.3989422804014327 * bell)


def mlp_kernel(
    img_ref, entry_ref, pull_ref, expand_ref, bias_ref, reduce_ref, reduce_far_ref,
    result_ref, back_ref, dreduce_ref, dexpand_far_ref, dexpand_ref, dbias_ref, turned_ref,
):
    step = pl.program_id(0)
    first_half = step < pl.num_programs(0) // 2

    @pl.when(step == 0)
    def _():
        result_ref[...] = jnp.zeros_like(result_ref)
        back_ref[...] = jnp.zeros_like(back_ref)
        turned_ref[...] = entry_ref[...].T

    expand = expand_ref[...]
    reduce = jnp.where(first_half, reduce_far_ref[...], reduce_ref[...])
    pull = pull_ref[...]
    hidden = dot_n(entry_ref[...], expand) + bias_ref[...]
    active, slope = gelu_parts(hidden)
    active = active.astype(BF)
    grad = (dot_t(pull, reduce) * slope).astype(BF)
    result_ref[...] += dot_n(active, reduce)
    back_ref[...] += dot_t(grad, expand)
    half = dexpand_ref.shape[0]
    here = pl.ds(pl.multiple_of(img_ref[0] * half, half), half)
    there = pl.ds(pl.multiple_of((1 - img_ref[0]) * half, half), half)
    dexpand_far_ref[...] = dot_n(turned_ref[there, :], grad).astype(BF)
    dexpand_ref[...] = dot_n(turned_ref[here, :], grad).astype(BF)
    dbias_ref[...] = jnp.sum(grad.astype(F32), axis=0, keepdims=True)
    dreduce_ref[...] = dot_f(active, pull).astype(BF)


def mlp(img, entry_two, incoming, expand, bias, reduce, reduce_far, *earlier, chunk=768):
    width = entry_two.shape[1]
    hidden = bias.shape[1]
    tokens = entry_two.shape[0]
    steps = hidden // chunk
    half = steps // 2

    def place(step, img):
        return (step + (1 - img[0]) * half) % steps

    def fixed(rows, columns):
        return pl.BlockSpec((rows, columns), lambda step, img: (0, 0))

    def across(rows):
        return pl.BlockSpec((rows, chunk), lambda step, img: (0, place(step, img)))

    return pl.pallas_call(
        ordered(mlp_kernel, 7, earlier),
        grid_spec=pltpu.PrefetchScalarGridSpec(
            num_scalar_prefetch=1,
            grid=(steps,),
            in_specs=[
                fixed(tokens, width), fixed(tokens, width), across(width), across(1),
                pl.BlockSpec((chunk, width), lambda step, img: (jnp.maximum(step - half, 0), 0)),
                pl.BlockSpec((chunk, width), lambda step, img: (jnp.minimum(step, half - 1), 0)),
            ] + [ANY] * len(earlier),
            out_specs=[
                fixed(tokens, width), fixed(tokens, width),
                pl.BlockSpec((chunk, width), lambda step, img: (place(step, img), 0)),
                across(width // 2), across(width // 2), across(1),
            ],
            scratch_shapes=[pltpu.VMEM((width, tokens), BF)],
        ),
        out_shape=[
            jax.ShapeDtypeStruct((tokens, width), F32),
            jax.ShapeDtypeStruct((tokens, width), F32),
            jax.ShapeDtypeStruct((hidden, width), BF),
            jax.ShapeDtypeStruct((width // 2, hidden), BF),
            jax.ShapeDtypeStruct((width // 2, hidden), BF),
            jax.ShapeDtypeStruct((1, hidden), F32),
        ],
        compiler_params=pltpu.CompilerParams(vmem_limit_bytes=VMEM_LIMIT),
        cost_estimate=cost(29),
        name="mlp",
    )(img.reshape(1), entry_two, incoming, expand, bias, reduce, reduce_far, *earlier)


def project_kernel(img_ref, x_ref, mask_ref, rows_ref, near_ref, far_ref, bias_ref, entry_ref, joint_ref):
    @pl.when(pl.program_id(0) == 0)
    def _():
        value = x_ref[...].astype(F32)
        centred = value - jnp.mean(value, axis=1, keepdims=True)
        variance = jnp.mean(centred * centred, axis=1, keepdims=True)
        normed = centred * lax.rsqrt(variance + 1e-06) * rows_ref[0:1] + rows_ref[1:2]
        entry_ref[...] = (mask_ref[...] * normed).astype(BF)

    low = img_ref[0] == 0
    near, far = near_ref[...], far_ref[...]
    weight = jnp.concatenate([jnp.where(low, near, far), jnp.where(low, far, near)], 0)
    joint_ref[...] = (dot_n(entry_ref[...], weight) + bias_ref[...]).astype(BF)


def project(img, x, mask, rows, near, far, bias, *earlier, chunk=768):
    tokens, width = x.shape
    total = bias.shape[1]

    def across(rows):
        return pl.BlockSpec((rows, chunk), lambda step: (0, step))

    return pl.pallas_call(
        ordered(project_kernel, 7, earlier),
        grid=(total // chunk,),
        in_specs=[
            pl.BlockSpec(memory_space=pltpu.SMEM), whole((tokens, width)), whole((tokens, 1)),
            whole((8, width)), across(width // 2), across(width // 2), across(1),
        ] + [ANY] * len(earlier),
        out_specs=[whole((tokens, width)), across(tokens)],
        out_shape=[
            jax.ShapeDtypeStruct((tokens, width), BF), jax.ShapeDtypeStruct((tokens, total), BF),
        ],
        compiler_params=pltpu.CompilerParams(vmem_limit_bytes=VMEM_LIMIT),
        cost_estimate=cost(7),
        name="project",
    )(img.reshape(1), x, mask, rows, near, far, bias, *earlier)


def project_back_kernel(
    img_ref, x_ref, mask_ref, rows_ref, middle_ref, pull_ref, near_ref, far_ref,
    grad_ref, sums_ref, weight_ref, entry_ref,
):
    img = img_ref[0]
    half = near_ref.shape[0]
    pairs = HEADS // 2
    here = pl.ds(pl.multiple_of(img * half, half), half)
    there = pl.ds(pl.multiple_of((1 - img) * half, half), half)
    for pair in range(pairs):
        for part in range(3):
            source = slice((part * pairs + pair) * 128, (part * pairs + pair + 1) * 128)
            target = slice((pair * 3 + part) * 128, (pair * 3 + part + 1) * 128)
            weight_ref[here, target] = near_ref[:, source]
            weight_ref[there, target] = far_ref[:, source]
    entry_ref[...] = dot_t(pull_ref[...], weight_ref[...])
    gain = rows_ref[0:1]
    width = x_ref.shape[1]

    def step(number, carry):
        spot = pl.ds(number * 48, 48)
        first, second = carry
        grad = entry_ref[spot, :] * mask_ref[spot, :]
        value = x_ref[spot, :].astype(F32)
        centred = value - jnp.mean(value, axis=1, keepdims=True)
        variance = jnp.mean(centred * centred, axis=1, keepdims=True)
        rstd = lax.rsqrt(variance + 1e-06)
        xhat = centred * rstd
        product = grad * xhat
        pull = grad * gain
        back = pull - jnp.mean(pull, axis=1, keepdims=True)
        back = back - xhat * jnp.mean(pull * xhat, axis=1, keepdims=True)
        grad_ref[spot, :] = (middle_ref[spot, :] + rstd * back).astype(BF)
        return first + jnp.sum(product.reshape(-1, 8, width), axis=0), second + jnp.sum(grad.reshape(-1, 8, width), axis=0)

    none = jnp.zeros((8, width), F32)
    carry = (none, none)
    for number in range(TOKENS // 48):
        carry = step(number, carry)
    first, second = carry
    sums_ref[0:1] = jnp.sum(first, axis=0, keepdims=True)
    sums_ref[1:2] = jnp.sum(second, axis=0, keepdims=True)


def project_back(img, x, mask, rows, grad_middle, grad_joint, near, far, *earlier):
    tokens, width = x.shape
    total = grad_joint.shape[1]
    full = whole((tokens, width))
    weight = whole((width // 2, total))
    return pl.pallas_call(
        ordered(project_back_kernel, 8, earlier),
        grid=(1,),
        in_specs=[
            pl.BlockSpec(memory_space=pltpu.SMEM), full, whole((tokens, 1)), whole((8, width)), full,
            whole((tokens, total)), weight, weight,
        ] + [ANY] * len(earlier),
        out_specs=[full, whole((2, width))],
        out_shape=[jax.ShapeDtypeStruct((tokens, width), BF), jax.ShapeDtypeStruct((2, width), F32)],
        scratch_shapes=[pltpu.VMEM((width, total), BF), pltpu.VMEM((tokens, width), F32)],
        compiler_params=pltpu.CompilerParams(vmem_limit_bytes=VMEM_LIMIT),
        cost_estimate=cost(11),
        name="project_back",
    )(img.reshape(1), x, mask, rows, grad_middle, grad_joint, near, far, *earlier)


def mix_kernel(mixed_ref, weight_ref, rows_ref, x_ref, mask_ref, middle_ref, entry_ref):
    branch = dot_n(mixed_ref[...], weight_ref[...]) + rows_ref[2:3]
    middle = x_ref[...].astype(F32) + mask_ref[...] * branch
    middle_ref[...] = middle
    centred = middle - jnp.mean(middle, axis=1, keepdims=True)
    variance = jnp.mean(centred * centred, axis=1, keepdims=True)
    normed = centred * lax.rsqrt(variance + 1e-06) * rows_ref[4:5] + rows_ref[5:6]
    entry_ref[...] = normed.astype(BF)


def last_columns(array, width):
    place = array.shape[1] // width - 1
    return pl.BlockSpec((array.shape[0], width), lambda step: (0, place))


def mix(mixed, weights, rows, x, mask, *earlier):
    tokens, width = x.shape
    return pl.pallas_call(
        ordered(mix_kernel, 5, earlier),
        grid=(1,),
        in_specs=[
            whole((tokens, width)), last_columns(weights, width), whole(rows.shape), whole((tokens, width)),
            whole(mask.shape),
        ] + [ANY] * len(earlier),
        out_specs=[whole((tokens, width))] * 2,
        out_shape=[jax.ShapeDtypeStruct(x.shape, F32), jax.ShapeDtypeStruct(x.shape, BF)],
        compiler_params=pltpu.CompilerParams(vmem_limit_bytes=VMEM_LIMIT),
        cost_estimate=cost(4.6),
        name="mix",
    )(mixed, weights, rows, x, mask, *earlier)


def mix_back_kernel(
    img_ref, back_ref, result_ref, middle_ref, incoming_ref, mask_ref, rows_ref, weight_ref, mixed_ref,
    grad_middle_ref, grad_mixed_ref, give_ref, keep_ref, out_ref, sums_ref,
):
    low = img_ref[0] == 0
    mask = mask_ref[...]
    middle = middle_ref[...]
    incoming = incoming_ref[...].astype(F32)
    out_ref[...] = (mask * (middle + (result_ref[...] + rows_ref[3:4]))).astype(BF)
    back = back_ref[...]
    centred = middle - jnp.mean(middle, axis=1, keepdims=True)
    variance = jnp.mean(centred * centred, axis=1, keepdims=True)
    rstd = lax.rsqrt(variance + 1e-06)
    xhat = centred * rstd
    sums_ref[1:2] = jnp.sum(back * xhat, axis=0, keepdims=True)
    sums_ref[2:3] = jnp.sum(back, axis=0, keepdims=True)
    sums_ref[3:4] = jnp.sum(incoming, axis=0, keepdims=True)
    pull = back * rows_ref[4:5]
    inner = pull - jnp.mean(pull, axis=1, keepdims=True)
    inner = inner - xhat * jnp.mean(pull * xhat, axis=1, keepdims=True)
    grad_middle = incoming + rstd * inner
    grad_middle_ref[...] = grad_middle
    branch = (mask * grad_middle).astype(BF)
    sums_ref[0:1] = jnp.sum(branch.astype(F32), axis=0, keepdims=True)
    grad_mixed_ref[...] = dot_t(branch, weight_ref[...]).astype(BF)
    half = keep_ref.shape[0]
    total = dot_f(mixed_ref[...], branch)
    give_ref[...] = jnp.where(low, total[half:], total[:half]).astype(BF)
    keep_ref[...] = jnp.where(low, total[:half], total[half:]).astype(BF)


def mix_back(img, back, result, middle, incoming, mask, rows, weights, mixed, *earlier):
    tokens, width = middle.shape
    half = (width // 2, width)
    full = whole((tokens, width))
    return pl.pallas_call(
        ordered(mix_back_kernel, 9, earlier),
        grid=(1,),
        in_specs=[
            pl.BlockSpec(memory_space=pltpu.SMEM), full, full, full, full, whole(mask.shape),
            whole(rows.shape), last_columns(weights, width), full,
        ] + [ANY] * len(earlier),
        out_specs=[full, full, whole(half), whole(half), full, whole((4, width))],
        out_shape=[
            jax.ShapeDtypeStruct((tokens, width), F32), jax.ShapeDtypeStruct((tokens, width), BF),
            jax.ShapeDtypeStruct(half, BF), jax.ShapeDtypeStruct(half, BF),
            jax.ShapeDtypeStruct((tokens, width), BF), jax.ShapeDtypeStruct((4, width), F32),
        ],
        compiler_params=pltpu.CompilerParams(vmem_limit_bytes=VMEM_LIMIT),
        cost_estimate=cost(7),
        name="mix_back",
    )(img.reshape(1), back, result, middle, incoming, mask, rows, weights, mixed, *earlier)


def entry_grads_kernel(img_ref, entry_ref, grad_ref, give_ref, keep_ref, turned_ref):
    @pl.when(pl.program_id(0) == 0)
    def _():
        turned_ref[...] = entry_ref[...].T

    half = keep_ref.shape[0]
    img = img_ref[0]
    grad = grad_ref[...]
    here = pl.ds(pl.multiple_of(img * half, half), half)
    there = pl.ds(pl.multiple_of((1 - img) * half, half), half)
    give_ref[...] = dot_n(turned_ref[there, :], grad).astype(BF)
    keep_ref[...] = dot_n(turned_ref[here, :], grad).astype(BF)


def entry_grads(img, entry, grad, *earlier, chunk=768):
    tokens, width = entry.shape
    total = grad.shape[1]

    def across(rows):
        return pl.BlockSpec((rows, chunk), lambda step: (0, step))

    return pl.pallas_call(
        ordered(entry_grads_kernel, 3, earlier),
        grid=(total // chunk,),
        in_specs=[pl.BlockSpec(memory_space=pltpu.SMEM), whole((tokens, width)), across(tokens)]
        + [ANY] * len(earlier),
        out_specs=[across(width // 2), across(width // 2)],
        out_shape=[
            jax.ShapeDtypeStruct((width // 2, total), BF), jax.ShapeDtypeStruct((width // 2, total), BF),
        ],
        scratch_shapes=[pltpu.VMEM((width, tokens), BF)],
        compiler_params=pltpu.CompilerParams(vmem_limit_bytes=VMEM_LIMIT),
        cost_estimate=cost(5),
        name="entry_grads",
    )(img.reshape(1), entry, grad, *earlier)


def sums_kernel(
    block, img_ref, norm_ref, joint_ref, mix_ref, expand_ref, tables_ref, give_ref, keep_ref, table_ref, turned_ref,
):
    width = norm_ref.shape[1]
    number = width // block
    joint = jnp.concatenate([joint_ref[0:1], joint_ref[1:2]], 1)

    def picked(line, count):
        return [
            jnp.concatenate(
                [
                    line[:, (count * owner + place) * block : (count * owner + place + 1) * block]
                    for owner in range(number)
                ],
                1,
            )
            for place in range(count)
        ]

    rows = [norm_ref[...], mix_ref[...]] + picked(joint, 2) + picked(expand_ref[...], 4)
    rows.append(jnp.zeros((128 - 12, width), F32))
    turned_ref[...] = jnp.concatenate(rows, 0).T
    half = give_ref.shape[0]
    img = img_ref[0]
    give_ref[...] = turned_ref[pl.ds(pl.multiple_of((1 - img) * half, half), half), :].astype(BF)
    keep_ref[...] = turned_ref[pl.ds(pl.multiple_of(img * half, half), half), :].astype(BF)
    total = tables_ref[0]
    for pair in range(1, tables_ref.shape[0]):
        total = total + tables_ref[pair]
    height = total[0:32, :64] + total[32:64, 64:]
    across = total[64:96, :64] + total[96:128, 64:]
    both = jnp.concatenate([height, across], 1)
    table_ref[...] = jnp.zeros_like(table_ref)
    for place in range(table_ref.shape[1] // 128):
        part = both[place * block : min((place + 1) * block, 32)]
        table_ref[: part.shape[0], place * 128 : (place + 1) * 128] = part.astype(BF)


def sums(img, norm, joint, mixed, expand, tables, block, *earlier):
    vmem = pl.BlockSpec(memory_space=pltpu.VMEM)
    width = norm.shape[1]
    shapes = [(width // 2, 128), (width // 2, 128), (block, -(-32 // block) * 128)]
    return pl.pallas_call(
        ordered(partial(sums_kernel, block), 6, earlier),
        in_specs=[pl.BlockSpec(memory_space=pltpu.SMEM)] + [vmem] * 5 + [ANY] * len(earlier),
        out_specs=[vmem] * 3,
        out_shape=[jax.ShapeDtypeStruct(shape, BF) for shape in shapes],
        scratch_shapes=[pltpu.VMEM((width, 128), F32)],
        compiler_params=pltpu.CompilerParams(vmem_limit_bytes=VMEM_LIMIT),
        cost_estimate=cost(0.3),
        name="sums",
    )(img.reshape(1), norm, joint, mixed, expand, tables, *earlier)


def wide_kernel(part_ref, out_ref):
    out_ref[...] = part_ref[...].astype(F32)


def wide(part, *earlier):
    vmem = pl.BlockSpec(memory_space=pltpu.VMEM)
    return pl.pallas_call(
        ordered(wide_kernel, 1, earlier),
        in_specs=[vmem] + [ANY] * len(earlier),
        out_specs=vmem,
        out_shape=jax.ShapeDtypeStruct(part.shape, F32),
        cost_estimate=cost(0.3),
        name="wide",
    )(part, *earlier)


def place_kernel(depth, slots, place_ref, *refs):
    parts = refs[:depth]
    triple_ref, height_ref, width_ref = refs[depth : depth + 3]
    vector_refs = refs[depth + 3 :]
    block = triple_ref.shape[0]
    pairs = HEADS // 2
    width = pairs * 128

    def total(lanes):
        value = parts[0][:, lanes]
        for part in parts[1:]:
            value = value + part[:, lanes].astype(F32)
        return value

    for pair in range(pairs):
        for part in range(3):
            begin, spot = (pair * 3 + part) * 128, (part * pairs + pair) * 128
            triple_ref[:, spot : spot + 128] = total(slice(begin, begin + 128))
    columns = total(slice(3 * width, 3 * width + 128))
    columns = jnp.concatenate([columns, jnp.zeros((128 - block, 128), F32)], 0).T
    begin = 0
    for out_ref in vector_refs:
        count = out_ref.shape[1] // block
        out_ref[...] = jnp.concatenate(
            [columns[begin + row : begin + row + 1, :block] for row in range(count)], 1
        )
        begin += count
    lanes = slice(3 * width + 128, None)
    tables = None
    for level in range(depth):
        found = parts[0][:, lanes]
        for step in range(1, depth):
            found = jnp.where((place_ref[2] ^ step) == level, parts[step][:, lanes].astype(F32), found)
        tables = found if tables is None else tables + found
    for slot in range(slots):
        spot = slots - 1 - slot
        first = spot // block * 128
        line = tables[spot % block : spot % block + 1, first : first + 128]
        height_ref[slot : slot + 1] = line[:, :64]
        width_ref[slot : slot + 1] = line[:, 64:]


def place(bits, parts, slots, *earlier):
    vmem = pl.BlockSpec(memory_space=pltpu.VMEM)
    block = parts[0].shape[0]
    width = HEADS * HEAD_DIM
    shapes = [(block, 3 * width)] + [(slots, HEAD_DIM)] * 2
    shapes += [(1, block)] * 6 + [(1, 2 * block), (1, 4 * block)]
    return pl.pallas_call(
        ordered(partial(place_kernel, len(parts), slots), 1 + len(parts), earlier),
        in_specs=[pl.BlockSpec(memory_space=pltpu.SMEM)] + [vmem] * len(parts) + [ANY] * len(earlier),
        out_specs=[vmem] * len(shapes),
        out_shape=[jax.ShapeDtypeStruct(shape, F32) for shape in shapes],
        compiler_params=pltpu.CompilerParams(vmem_limit_bytes=VMEM_LIMIT),
        cost_estimate=cost(1.9),
        name="place",
    )(bits, *parts, *earlier)


def settle_kernel(cut, *refs):
    parts, (left_ref, right_ref) = refs[:-2], refs[-2:]
    for out_ref, lanes in ((left_ref, slice(0, cut)), (right_ref, slice(cut, None))):
        value = parts[0][:, lanes]
        for part in parts[1:]:
            value = value + part[:, lanes].astype(F32)
        out_ref[...] = value


def settle(parts, cut, *earlier):
    vmem = pl.BlockSpec(memory_space=pltpu.VMEM)
    rows, columns = parts[0].shape
    return pl.pallas_call(
        ordered(partial(settle_kernel, cut), len(parts), earlier),
        in_specs=[vmem] * len(parts) + [ANY] * len(earlier),
        out_specs=[vmem] * 2,
        out_shape=[
            jax.ShapeDtypeStruct((rows, cut), F32), jax.ShapeDtypeStruct((rows, columns - cut), F32),
        ],
        cost_estimate=cost(1),
        name="settle",
    )(*parts, *earlier)


def rows_place():
    me = lax.axis_index("rows")
    return me % 2, me // 2 % 2, me // 4


def swap_rows(block, bit):
    count = lax.axis_size("rows")
    return lax.ppermute(block, "rows", [(place, place ^ (1 << bit)) for place in range(count)])


def swap_img(block):
    return lax.ppermute(block, "img", [(0, 1), (1, 0)])


def swap_depth(block, step):
    count = lax.axis_size("rows")
    return lax.ppermute(block, "rows", [(place, place ^ (4 * step)) for place in range(count)])


def halves(block):
    cut = block.shape[-1] // 256 * 128
    return block[..., :cut], block[..., cut:]


def join_one_kernel(offsets, bits_ref, *refs):
    place = bits_ref[2]
    ins, (first, second) = refs[: len(offsets)], refs[-2:]
    cut = first.shape[-1]
    for offset, part_ref in zip(offsets, ins):
        part = part_ref[...]
        first[place ^ offset] = part[:, :cut]
        second[place ^ offset] = part[:, cut:]


def join_two_kernel(count, bits_ref, *refs):
    x, y = bits_ref[0], bits_ref[1]
    ins, outs = refs[: 4 * count], refs[len(refs) - 2 * count :]
    for number in range(count):
        first, first_far, second, second_far = ins[4 * number : 4 * number + 4]
        joined, joined_two = outs[2 * number : 2 * number + 2]
        for level in range(first.shape[0]):
            joined[level, x] = first[level]
            joined[level, 1 - x] = first_far[level]
            joined_two[level, y] = second[level]
            joined_two[level, 1 - y] = second_far[level]


def join_three_kernel(begin, bits_ref, first, first_far, second, second_far, *refs):
    x, y = bits_ref[0], bits_ref[1]
    joined = refs[-1]
    cut = first.shape[-1]
    rows = slice(begin, begin + joined.shape[3])
    for level in range(first.shape[0]):
        for side in range(2):
            joined[level, y, side, :, :cut] = first[level, side, rows]
            joined[level, 1 - y, side, :, :cut] = first_far[level, side, rows]
            joined[level, side, x, :, cut:] = second[level, side, rows]
            joined[level, side, 1 - x, :, cut:] = second_far[level, side, rows]


def carry_kernel(weight_ref, *refs):
    out_ref = refs[-1]
    columns = weight_ref.shape[1]
    out_ref[:, :columns] = weight_ref[...]
    pre_gain, pre_bias, triple_bias, output_bias, post_gain, post_bias, expand_bias, reduce_bias = [
        ref[...].astype(F32) for ref in refs[:8]
    ]
    lines = []
    for parts in ((pre_gain, pre_bias, triple_bias, output_bias), (expand_bias, reduce_bias), (post_gain, post_bias)):
        size = sum(part.shape[1] for part in parts)
        lines.append(jnp.concatenate(parts + (jnp.zeros((1, 128 - size), F32),), 1))
    rest = out_ref.shape[0] - len(lines)
    if rest:
        lines.append(jnp.zeros((rest, 128), F32))
    out_ref[:, columns:] = jnp.concatenate(lines, 0).astype(out_ref.dtype)


def carry(weight, vectors, *earlier):
    vmem = pl.BlockSpec(memory_space=pltpu.VMEM)
    return pl.pallas_call(
        ordered(carry_kernel, 1 + len(vectors), earlier),
        in_specs=[vmem] * (1 + len(vectors)) + [ANY] * len(earlier),
        out_specs=vmem,
        out_shape=jax.ShapeDtypeStruct((weight.shape[0], weight.shape[1] + 128), weight.dtype),
        cost_estimate=cost(2),
        name="carry",
    )(weight, *[vector.reshape(1, -1) for vector in vectors], *earlier)


def spread_kernel(block, img_ref, near_ref, far_ref, rows_ref, offsets_ref, fill_ref, expand_ref):
    low = img_ref[0] == 0
    near, far = near_ref[...].astype(F32), far_ref[...].astype(F32)
    count = near.shape[0] // block
    width = rows_ref.shape[1]
    rows_ref[6:8] = jnp.zeros((2, width), F32)
    offsets_ref[...] = jnp.zeros_like(offsets_ref)
    plan = (
        (0, 0, 1, rows_ref, 0), (0, 1, 1, rows_ref, 1), (0, 4, 1, rows_ref, 2),
        (1, 4, 1, rows_ref, 3), (2, 0, 1, rows_ref, 4), (2, 1, 1, rows_ref, 5),
        (1, 0, 4, expand_ref, 0),
    )
    for half in range(2):
        part = jnp.where(low, near, far) if half == 0 else jnp.where(low, far, near)
        for number in range(count):
            spot = half * count + number
            lines = part[number * block : number * block + 3]
            for line, first, size, out_ref, row in plan:
                size = size * block
                out_ref[row : row + 1, spot * size : (spot + 1) * size] = lines[
                    line : line + 1, first * block : first * block + size
                ]
            size = 2 * block
            begin = spot * size + (width if half else 0)
            offsets_ref[:, begin : begin + size] = lines[0:1, size : 2 * size]
    fill_ref[...] = offsets_ref[:, 2 * width :].astype(BF)


def spread(img, near, far, block, *earlier):
    width = 2 * near.shape[0]
    place = near.shape[1] // 128 - 1
    last = pl.BlockSpec((near.shape[0], 128), lambda step: (0, place))
    shapes = [((8, width), F32), ((1, 3 * width), F32), ((1, width), BF), ((1, 4 * width), F32)]
    return pl.pallas_call(
        ordered(partial(spread_kernel, block), 3, earlier),
        grid=(1,),
        in_specs=[pl.BlockSpec(memory_space=pltpu.SMEM), last, last] + [ANY] * len(earlier),
        out_specs=[whole(shape) for shape, _ in shapes],
        out_shape=[jax.ShapeDtypeStruct(shape, kind) for shape, kind in shapes],
        cost_estimate=cost(2),
        name="spread",
    )(img.reshape(1), near, far, *earlier)


def stack_kernel(*refs):
    refs[-1][...] = jnp.concatenate([ref[...].astype(F32) for ref in refs[:-1]], 0).astype(BF)


def stack(blocks, *earlier):
    vmem = pl.BlockSpec(memory_space=pltpu.VMEM)
    rows = sum(block.shape[0] for block in blocks)
    return pl.pallas_call(
        ordered(stack_kernel, len(blocks), earlier),
        in_specs=[vmem] * len(blocks) + [ANY] * len(earlier),
        out_specs=vmem,
        out_shape=jax.ShapeDtypeStruct((rows,) + blocks[0].shape[1:], BF),
        cost_estimate=cost(1.6),
        name="stack",
    )(*blocks, *earlier)


class Gather:
    def __init__(self, block):
        self.depth = lax.axis_size("rows") // 4
        self.bits = jnp.stack(rows_place()).astype(jnp.int32)
        self.rows, self.columns = block.shape
        self.cut = self.columns // 256 * 128
        self.held = [block]

    def call(self, kernel, name, values, shapes, earlier):
        vmem = pl.BlockSpec(memory_space=pltpu.VMEM)
        return pl.pallas_call(
            kernel,
            in_specs=[pl.BlockSpec(memory_space=pltpu.SMEM)] + [vmem] * len(values) + [ANY] * len(earlier),
            out_specs=[vmem] * len(shapes),
            out_shape=[jax.ShapeDtypeStruct(shape, BF) for shape in shapes],
            compiler_params=pltpu.CompilerParams(vmem_limit_bytes=VMEM_LIMIT),
            cost_estimate=cost(2.3),
            name=name,
        )(self.bits, *values, *earlier)

    def shapes(self, *lead):
        return [lead + (self.rows, self.cut), lead + (self.rows, self.columns - self.cut)]

    def shift(self):
        held = [(0, self.held[0])]
        bit = self.depth // 2
        while bit:
            held += [(offset ^ bit, swap_depth(block, bit)) for offset, block in held]
            bit //= 2
        self.offsets = [offset for offset, _ in held]
        self.far = [block for _, block in held[1:]]

    def join_one(self, *earlier):
        kernel = partial(join_one_kernel, self.offsets)
        self.held = self.call(kernel, "join_one", self.held + self.far, self.shapes(self.depth), earlier)
        return self.held

    def swap_near(self):
        self.far = [swap_rows(part, number) for number, part in enumerate(self.held)]

    def swap_far(self):
        self.far = [swap_rows(part, 1 - number) for number, part in enumerate(self.held)]

    def pairs(self):
        return [array for pair in zip(self.held, self.far) for array in pair]

    def join_two(self, *earlier):
        kernel = partial(join_two_kernel, 1)
        self.held = self.call(kernel, "join_two", self.pairs(), self.shapes(self.depth, 2), earlier)
        return self.held

    def join_three(self, begin, rows, *earlier):
        shapes = [(self.depth, 2, 2, rows, self.columns)]
        kernel = partial(join_three_kernel, begin)
        return self.call(kernel, "join_three", self.pairs(), shapes, earlier)[0].reshape(-1, self.columns)


def fold_one_kernel(count, ride, bits_ref, *refs):
    ins = refs[: 2 * count]
    a_give, a_keep, b_give, b_keep = refs[-4 - bool(ride) :][:4]
    x, y = bits_ref[0], bits_ref[1]
    cut = a_keep.shape[-1]
    begin = 0
    for near_ref, far_ref in zip(ins[:count], ins[count:]):
        columns = near_ref.shape[-1]
        pieces = [(max(begin, 0), min(begin + columns, cut), True), (max(begin, cut), begin + columns, False)]
        for low, high, first in pieces:
            if low >= high:
                continue
            here = slice(low - begin, high - begin)
            there = slice(low, high) if first else slice(low - cut, high - cut)
            for level in range(near_ref.shape[0]):
                for side in range(2):
                    if first:
                        kept, given = (level, side, x), (level, side, 1 - x)
                    else:
                        kept, given = (level, y, side), (level, 1 - y, side)
                    keep, give = (a_keep, a_give) if first else (b_keep, b_give)
                    value = near_ref[kept + (slice(None), here)].astype(F32) + far_ref[kept + (slice(None), here)].astype(F32)
                    keep[level, side, :, there] = value
                    value = near_ref[given + (slice(None), here)].astype(F32) + far_ref[given + (slice(None), here)].astype(F32)
                    give[level, side, :, there] = value.astype(BF)
        begin += columns
    if ride:
        near, far = refs[2 * count : 2 * count + 2]
        table = (near[...].astype(F32) + far[...].astype(F32)).astype(BF)
        refs[-1][...] = table
        a_give[:, :, :, cut:] = jnp.zeros(a_give.shape[:3] + (ride,), BF)
        a_give[0, 0, :, cut:] = table


def fold_two_kernel(ride, bits_ref, a_near, a_far, b_near, b_far, *refs):
    a_give, a_keep, b_give, b_keep = refs[-4 - bool(ride) :][:4]
    x, y = bits_ref[0], bits_ref[1]
    cut = a_keep.shape[-1]
    for level in range(a_near.shape[0]):
        a_keep[level] = a_near[level, y] + a_far[level, y, :, :cut].astype(F32)
        a_give[level, :, :cut] = (a_near[level, 1 - y] + a_far[level, 1 - y, :, :cut].astype(F32)).astype(BF)
        b_keep[level] = b_near[level, x] + b_far[level, x].astype(F32)
        b_give[level] = (b_near[level, 1 - x] + b_far[level, 1 - x].astype(F32)).astype(BF)
    if ride:
        table = (refs[0][...].astype(F32) + a_far[0, 0, :, cut:].astype(F32)).astype(BF)
        refs[-1][...] = table
        a_give[:, :, cut:] = jnp.zeros(a_give.shape[:2] + (ride,), BF)
        a_give[0, :, cut:] = table


def fold_three_kernel(depth, ride, bits_ref, a_near, a_far, b_near, b_far, *refs):
    place = bits_ref[2]
    keep, gives = refs[-depth], refs[len(refs) - depth + 1 :]
    cut = a_near.shape[-1]
    columns = cut + b_near.shape[-1]
    for step, out in enumerate((keep,) + tuple(gives)):
        spot = place ^ step
        out[:, :cut] = (a_near[spot] + a_far[spot, :, :cut].astype(F32)).astype(out.dtype)
        out[:, cut:columns] = (b_near[spot] + b_far[spot].astype(F32)).astype(out.dtype)
        if ride:
            table = (refs[0][...].astype(F32) + a_far[0, :, cut:].astype(F32)).astype(BF)
            out[:, columns:] = table.astype(out.dtype)


def fold_call(kernel, name, bits, values, outs, earlier, estimate):
    vmem = pl.BlockSpec(memory_space=pltpu.VMEM)
    return pl.pallas_call(
        kernel,
        in_specs=[pl.BlockSpec(memory_space=pltpu.SMEM)] + [vmem] * len(values)
        + [pl.BlockSpec(memory_space=pl.ANY)] * len(earlier),
        out_specs=[vmem] * len(outs),
        out_shape=[jax.ShapeDtypeStruct(shape, kind) for shape, kind in outs],
        compiler_params=pltpu.CompilerParams(vmem_limit_bytes=VMEM_LIMIT),
        cost_estimate=cost(estimate),
        name=name,
    )(bits, *values, *earlier)


class Scatter:
    def __init__(self, give, keep, costs, table=None):
        self.costs = costs
        self.depth = lax.axis_size("rows") // 4
        self.columns = sum(part.shape[-1] for part in keep)
        self.cut = self.columns // 256 * 128
        self.bits = jnp.stack(rows_place()).astype(jnp.int32)
        self.rows = keep[0].shape[0] // lax.axis_size("rows")
        self.give, self.keep = list(give), list(keep)
        self.table = table
        self.ride = table.shape[1] if table is not None else 0

    def swap_near(self):
        self.far = [swap_img(part) for part in self.give]

    def outs(self, *lead):
        first, second = lead + (self.rows, self.cut), lead + (self.rows, self.columns - self.cut)
        shapes = [(lead + (self.rows, self.cut + self.ride), BF), (first, F32), (second, BF), (second, F32)]
        if self.ride:
            shapes.append(((self.rows, self.ride), BF))
        return shapes

    def fold_one(self, *earlier):
        shape = (self.depth, 2, 2, self.rows, -1)
        values = [part.reshape(shape) for part in self.keep + self.far]
        if self.ride:
            values += [self.table, swap_img(self.table)]
        kernel = partial(fold_one_kernel, len(self.keep), self.ride)
        self.out = fold_call(
            kernel, "fold_one", self.bits, values, self.outs(self.depth, 2), earlier, self.costs[0]
        )
        return self.out

    def swap_middle(self):
        self.far = swap_rows(self.out[0], 0), swap_rows(self.out[2], 1)
        return self.far

    def fold_two(self, *earlier):
        values = [self.out[1], self.far[0], self.out[3], self.far[1]] + list(self.out[4:])
        kernel = partial(fold_two_kernel, self.ride)
        self.out = fold_call(
            kernel, "fold_two", self.bits, values, self.outs(self.depth), earlier, self.costs[1]
        )
        return self.out

    def swap_far(self):
        self.far = swap_rows(self.out[0], 1), swap_rows(self.out[2], 0)
        return self.far

    def fold_three(self, *earlier):
        block = (self.rows, self.columns + self.ride)
        values = [self.out[1], self.far[0], self.out[3], self.far[1]] + list(self.out[4:])
        outs = [(block, F32)] + [(block, BF)] * (self.depth - 1)
        kernel = partial(fold_three_kernel, self.depth, self.ride)
        self.out = fold_call(kernel, "fold_three", self.bits, values, outs, earlier, self.costs[2])
        return self.out

    def swap_last(self):
        return [self.out[0]] + [swap_depth(self.out[step], step) for step in range(1, self.depth)]

    def last(self):
        parts = self.swap_last()
        return sum((part.astype(F32) for part in parts[1:]), parts[0])


def to_odd(block):
    count = lax.axis_size("rows")
    return lax.ppermute(block, "rows", [(place, place + 1) for place in range(0, count, 2)])


def to_even(block):
    count = lax.axis_size("rows")
    return lax.ppermute(block, "rows", [(place + 1, place) for place in range(0, count, 2)])


def local(
    tokens,
    extent,
    pre_gain,
    pre_bias,
    triple_weight,
    triple_bias,
    height_table,
    width_table,
    output_weight,
    output_bias,
    post_gain,
    post_bias,
    expand_weight,
    expand_bias,
    reduce_weight,
    reduce_bias,
    cotangent,
):
    rows_dev, _, width = tokens.shape
    moved = rows_dev - WIN
    block = pre_gain.shape[0]
    parity = lax.axis_index("rows") % 2
    image = lax.axis_index("img") * (lax.axis_size("rows") // 2) + lax.axis_index("rows") // 2
    sides = lax.dynamic_slice(extent, (image, 0), (1, 2))

    img = lax.axis_index("img")
    last = []

    def then(result):
        arrays = result if isinstance(result, (list, tuple)) else [result]
        last[:] = [min(arrays, key=lambda array: array.size)]
        return result

    band_row, column_of = jnp.asarray(BAND_ROW), jnp.asarray(COLUMN)
    real_row = jnp.where(parity == 0, band_row, band_row + WIN)
    inside = (real_row < sides[0, 0]) & (column_of < sides[0, 1]) & (jnp.asarray(VALID) == 1)
    inside = inside & ((parity == 1) | (band_row < WIN))
    mask = inside.astype(F32)[:, None]
    table = reversed_table(height_table, width_table)
    vectors = (
        pre_gain, pre_bias, triple_bias, output_bias, post_gain, post_bias, expand_bias, reduce_bias,
    )

    far_rows = to_odd(jnp.concatenate([tokens[WIN:, :REAL], cotangent[WIN:, :REAL]]))
    later_all = lax.all_gather(
        jnp.concatenate([expand_weight, output_weight], 1), ("img", "rows"), axis=0, tiled=True
    )
    one = Gather(then(carry(triple_weight, vectors)))
    one.shift()
    two = Gather(then(stack([reduce_weight], *last)))
    then(one.join_one(*last))
    one.swap_near()
    two.shift()
    x = then(pack(parity, tokens, far_rows, mask, 0, *last))
    then(one.join_two(*last, *two.far[:-1]))
    one.swap_far()
    incoming = then(pack(parity, cotangent, far_rows, mask, moved, *last))
    triple_near = then(one.join_three(0, block, *last, two.far[-1]))
    triple_pair = triple_near, swap_img(triple_near)
    then(two.join_one(*last))
    two.swap_near()
    rows, offsets, fill, hidden_bias = then(spread(img, *triple_pair, block, *last))
    entry, joint = then(project(img, x, mask, rows, *triple_pair, offsets, *last))
    then(two.join_two(*last))
    two.swap_far()
    mixed, lse, features = then(attend(joint, fill, table, 0, HEADS // 2, (), *last))
    reduce_near = then(two.join_three(0, reduce_weight.shape[0], *last))
    reduce_pair = reduce_near, swap_img(reduce_near)
    middle, entry_two = then(mix(mixed, later_all, rows, x, mask, *last))

    result, grad_entry_two, reduce_grad, expand_far, expand_near, hidden_sums = then(
        mlp(img, entry_two, incoming, later_all, hidden_bias, *reduce_pair, *last)
    )
    reduce_part = lax.psum_scatter(reduce_grad, ("img", "rows"), scatter_dimension=0, tiled=True)
    grad_middle, grad_mixed, output_far, output_near, out_win, mix_sums = then(
        mix_back(img, grad_entry_two, result, middle, incoming, mask, rows, later_all, mixed, *last)
    )
    first_sum = Scatter([expand_far, output_far], [expand_near, output_near], (2.3, 2.3, 1.5))
    first_sum.swap_near()
    then(first_sum.fold_one(*last))
    first_sum.swap_middle()
    out_rows = to_even(then(send_rows(out_win, moved, *last)))
    grad_joint, tables, joint_sums = then(
        attend_back(joint, grad_mixed, lse, features, fill, table, 0, HEADS // 2, *last)
    )
    joint_far, joint_near = then(entry_grads(img, entry, grad_joint, *last))
    then(first_sum.fold_two(*last))
    first_sum.swap_far()
    grad_win, norm_sums = then(
        project_back(img, x, mask, rows, grad_middle, grad_joint, *triple_pair, *last)
    )
    vectors_far, vectors_near, table_sums = then(
        sums(img, norm_sums, joint_sums, mix_sums, hidden_sums, tables, block, *last)
    )
    last_sum = Scatter([joint_far, vectors_far], [joint_near, vectors_near], (0.3, 2.3, 1.5), table_sums)
    last_sum.swap_near()
    then(last_sum.fold_one(*last, out_rows))
    last_sum.swap_middle()
    then(first_sum.fold_three(*last))
    first_parts = first_sum.swap_last()
    block_output = then(unpack(parity, out_win, out_rows, tokens.shape, *last))
    grad_rows = to_even(then(send_rows(grad_win, moved, *last)))
    then(last_sum.fold_two(*last, *first_parts[1:2]))
    last_sum.swap_far()
    expand_shard, output_shard = then(settle(first_parts, expand_far.shape[1], *last))
    then(last_sum.fold_three(*last))
    last_parts = last_sum.swap_last()
    input_grad = then(unpack(parity, grad_win, grad_rows, tokens.shape, *last))
    (
        triple_shard, height_grad, width_grad, pre_gain_grad, pre_bias_grad, output_bias_grad,
        post_gain_grad, post_bias_grad, reduce_bias_grad, triple_bias_grad, expand_bias_grad,
    ) = then(place(last_sum.bits, last_parts, height_table.shape[0], *last))
    reduce_shard = wide(reduce_part, *last)
    return (
        block_output,
        input_grad,
        pre_gain_grad.reshape(-1),
        pre_bias_grad.reshape(-1),
        triple_shard,
        triple_bias_grad.reshape(-1),
        height_grad,
        width_grad,
        output_shard,
        output_bias_grad.reshape(-1),
        post_gain_grad.reshape(-1),
        post_bias_grad.reshape(-1),
        expand_shard,
        expand_bias_grad.reshape(-1),
        reduce_shard,
        reduce_bias_grad.reshape(-1),
    )


def solution(mesh):
    split = P(("img", "rows"))
    flat = P(("img", "rows"), None)
    grids = P(("img", "rows"), None, None)
    in_specs = (
        grids, P(), split, split, flat, split, P(), P(), flat, split, split, split, flat, split,
        flat, split, grids,
    )
    out_specs = (
        grids, grids, split, split, flat, split, P(), P(), flat, split, split, split, flat, split,
        flat, split,
    )
    return jax.shard_map(local, mesh=mesh, in_specs=in_specs, out_specs=out_specs, check_vma=False)
```
